512 devices in a mesh: dom: 128 (over x, z, core), tile: 4 (over y).
Axes of the slice: x: 4, y: 4, z: 16, core: 2. Of those that a mesh axis runs over, the one named last changes fastest.
Arguments:
- pumping: float32 [8192, 4096], P(('dom', 'tile')), may hold values from -36 to 36
- coupling: float32 [8192, 4096], P(('dom', 'tile')), may hold values from -0.75 to 0.75
- storage: float32 [8192, 64], P(('dom', 'tile')), may hold values from 0.2 to 2
- tile_order: int32 [512, 1024], P(('dom', 'tile')), may hold values from 0 to 1023, each once within a row
- kriging: bfloat16 [8192, 1024], P(('dom', 'tile')), may hold values from -0.75 to 0.75
Outputs:
- sensitivity: float32 [8192, 64], P(('dom', 'tile'))
- residual_gram: float32 [64, 64], replicated
The draws below stay inside these ranges and needn't reach their ends.
All inputs are finite; a program needn't handle non-finite values.
Results may differ from the reference program's by a relative error of at most 0.00105.
Values may be sent and summed in bfloat16 or wider, within the bound.
No kernel may reach another device: no remote copies, remote signals or barrier semaphores. Data moves between devices by JAX's collectives and lax.ppermute only.
A program may use at most 64 MiB of HBM per device.

```python
import math
import jax
import jax.numpy as jnp
from jax import lax

RHS = 64
CB = 64
FX = 8
FY = 2
PILOT = 16
ITERS = 2
BLK = 16
CELLS_DEV = 1024
GC = 8
GX = 1024
GY = 8
BLOCKS = 8192
CELLS = 524288
N_DOM = 128
N_TILE = 4


def draw_pumping(key, part):
    keys = jax.random.split(key, 3)
    rates = jnp.exp(jax.random.uniform(keys[0], (1, RHS, 1), jnp.float32, math.log(0.1), 0.0))
    cell_scale = jnp.exp(jax.random.uniform(keys[1], (BLOCKS, 1, CB), jnp.float32, 0.0, math.log(3.0)))
    dom_index = (jnp.arange(BLOCKS) // (BLK * N_TILE)).astype(jnp.float32)
    ramp = (1.0 + 2.0 * dom_index / max(N_DOM - 1, 1)).reshape(BLOCKS, 1, 1)
    noise = jnp.clip(jax.random.normal(keys[2], (BLOCKS, RHS, CB), jnp.float32), -4.0, 4.0)
    return (rates * cell_scale * ramp * noise).reshape(BLOCKS, RHS * CB)


def block_scale(key, dims, cuts, smallest, high):
    factor_of, own = 1.0, jax.random.fold_in(key, 6)
    for dim, blocks in cuts:
        heights = jnp.exp(jax.random.uniform(jax.random.fold_in(own, dim), (blocks,), jnp.float32, smallest / len(cuts), high / len(cuts)))
        factor_of = factor_of * jnp.repeat(heights, dims[dim] // blocks).reshape([-1 if axis == dim else 1 for axis in range(len(dims))])
    return factor_of


def centred(stream_key, dims, width, reach, cuts=(), kind=jnp.bfloat16):
    values = width * jax.random.normal(stream_key, dims, jnp.float32)
    if cuts:
        values = values * block_scale(stream_key, dims, cuts, -0.22, 0.18)
    return jnp.clip(values, -reach, reach).astype(kind)


def setup_inputs(seed: int = 0) -> dict:
    arg_keys = jax.random.split(jax.random.key(seed), 6)
    return {
        "pumping": draw_pumping(jax.random.fold_in(arg_keys[5], 71), 0),
        "coupling": centred(arg_keys[1], (BLOCKS, CB * CB), CB ** -0.5, 0.75, ((0, 512),), jnp.float32),
        "storage": jnp.clip(jnp.exp(math.log(2.0) - 2.3025851 * jax.random.uniform(arg_keys[2], (BLOCKS, CB), jnp.float32) ** block_scale(arg_keys[2], (BLOCKS, CB), ((0, 512),), -0.2, 0.2)), 0.2, 2.0),
        "tile_order": jax.vmap(lambda own: jax.random.permutation(own, CELLS_DEV))(jax.random.split(arg_keys[3], (N_DOM * N_TILE))).reshape((N_DOM * N_TILE, CELLS_DEV)).astype(jnp.int32),
        "kriging": centred(arg_keys[4], (N_DOM * N_TILE * PILOT, CELLS_DEV), (CELLS_DEV // 16) ** -0.5, 0.75, ((0, 512),)),
    }


PRECISE = lax.Precision.HIGHEST


def symmetric(matrix):
    return 0.5 * (matrix + matrix.T)


def gram_matrix(left, right):
    return jnp.einsum('xyrc,xysc->rs', left, right, precision=PRECISE)


def mix_rows(weights, values):
    return jnp.einsum('rs,xyrc->xysc', weights, values, precision=PRECISE)


def solve_definite(matrix, target):
    order = matrix.shape[0]
    joined = jnp.concatenate([matrix, target], axis=1)
    row_index = jnp.arange(order, dtype=jnp.int32)[:, None]

    def eliminate(pivot_at, current):
        pivot_at = jnp.asarray(pivot_at).astype(jnp.int32)
        pivot_row = lax.dynamic_slice_in_dim(current, pivot_at, 1, 0)
        pivot_value = lax.dynamic_slice_in_dim(pivot_row, pivot_at, 1, 1)
        scaled = pivot_row / pivot_value
        column = lax.dynamic_slice_in_dim(current, pivot_at, 1, 1)
        factor = jnp.where(row_index == pivot_at, jnp.zeros_like(column), column)
        updated = current - factor * scaled
        return lax.dynamic_update_slice_in_dim(updated, scaled, pivot_at, 0)

    joined = lax.fori_loop(0, order, eliminate, joined)
    return joined[:, order:]


def to_grid(array):
    rest = array.shape[1:]
    shaped = array.reshape((N_DOM, N_TILE, FX, FY) + rest)
    order = (0, 2, 1, 3) + tuple(range(4, 4 + len(rest)))
    return jnp.transpose(shaped, order).reshape((GX, GY) + rest)


def apply_operator(values, matrices, capacity):
    spread = jnp.einsum('xyrc,xyce->xyre', values, matrices, precision=PRECISE)
    padded = jnp.pad(spread, ((1, 1), (1, 1), (0, 0), (0, 0)))
    beside = padded[:-2, 1:-1] + padded[2:, 1:-1] + padded[1:-1, :-2] + padded[1:-1, 2:]
    pulled = 4.0 * spread - beside
    return capacity[:, :, None, :] * values + jnp.einsum('xyre,xyce->xyrc', pulled, matrices, precision=PRECISE)


def reference(pumping, coupling, storage, tile_order, kriging):
    field_grid = to_grid(pumping.reshape(BLOCKS, RHS, CB))
    matrices = to_grid(coupling.reshape(BLOCKS, CB, CB))
    capacity = to_grid(storage)
    solution = jnp.zeros_like(field_grid)
    residual = field_grid
    direction = field_grid
    residual_gram = symmetric(gram_matrix(residual, residual))
    for iteration in range(ITERS):
        applied = apply_operator(direction, matrices, capacity)
        step_size = solve_definite(symmetric(gram_matrix(direction, applied)), residual_gram)
        solution = solution + mix_rows(step_size, direction)
        residual = residual - mix_rows(step_size, applied)
        next_gram = symmetric(gram_matrix(residual, residual))
        if iteration + 1 < ITERS:
            direction = residual + mix_rows(solve_definite(residual_gram, next_gram), direction)
        residual_gram = next_gram
    head_table = solution.reshape(N_DOM, FX, N_TILE, FY, RHS, CB)
    head_table = jnp.transpose(head_table, (0, 2, 4, 1, 3, 5)).reshape(N_DOM, N_TILE, RHS, CELLS_DEV)
    orders = tile_order.reshape(N_DOM, N_TILE, CELLS_DEV)
    ordered = jax.vmap(jax.vmap(lambda table, order_row: jnp.take(table, order_row, axis=1)))(head_table, orders)
    ordered = ordered.reshape(N_DOM, N_TILE, RHS, N_DOM, GC)
    received = jnp.transpose(ordered, (3, 1, 2, 0, 4)).reshape(N_DOM, N_TILE, RHS, CELLS_DEV)
    weights = kriging.astype(jnp.float32).reshape(N_DOM, N_TILE, PILOT, CELLS_DEV)
    sensitivity = jnp.einsum('gtpm,gtrm->gtpr', weights, received, precision=PRECISE)
    sensitivity = sensitivity.reshape(N_DOM * N_TILE * PILOT, RHS)
    return sensitivity, residual_gram / CELLS
```

```python
import jax
import jax.numpy as jnp
from jax import lax
from jax.experimental import pallas as pl
from jax.experimental.pallas import tpu as pltpu
from jax.sharding import PartitionSpec as P

RHS = 64
CB = 64
FX = 8
LANE = 128
ROWS = FX * RHS
F32 = jnp.float32
BF16 = jnp.bfloat16
HIGHEST = lax.Precision.HIGHEST
PARAMS = pltpu.CompilerParams(vmem_limit_bytes=40 * 1024 * 1024)
NN = (((1,), (0,)), ((), ()))
NT = (((1,), (1,)), ((), ()))


def split(value):
    high = value.astype(BF16)
    return high, (value - high.astype(F32)).astype(BF16)


def dot(left, right, dims):
    return lax.dot_general(left, right, dims, preferred_element_type=F32)


def dot3(left, right, dims):
    (lh, ll), (rh, rl) = left, right
    return dot(lh, rh, dims) + (dot(ll, rh, dims) + dot(lh, rl, dims))


def exact(left, right, dims=NN):
    return lax.dot_general(left, right, dims, precision=HIGHEST, preferred_element_type=F32)


def low_lanes(rows):
    return lax.broadcasted_iota(jnp.int32, (rows, LANE), 1) < CB


def swap(value):
    return pltpu.roll(value, CB, 1)


def part(x):
    return pl.ds(x * RHS, RHS)


def write_edges(spread, dl, dr, tl, tr):
    low = low_lanes(RHS)
    dl[...] = spread[0].astype(BF16)
    dr[...] = spread[FX - 1].astype(BF16)
    for i in range(FX // 2):
        even, odd = spread[2 * i], spread[2 * i + 1]
        tl[part(i), :] = jnp.where(low, even, swap(odd)).astype(BF16)
        tr[part(i), :] = jnp.where(low, swap(even), odd).astype(BF16)


def first_kernel(pump, coup, p_out, sh_out, sl_out, u_out, dl, dr, tl, tr, rows_p, rows_s, mats):
    for k in range(RHS // 2):
        chunk = slice(k * LANE, (k + 1) * LANE)
        rows_p[pl.ds(k, 16, stride=32), :] = pump[:, chunk]
        rows_s[pl.ds(k, 16, stride=32), :] = coup[:, chunk]
    low = low_lanes(32)
    zero = jnp.zeros((32, LANE), F32)
    for x in range(FX):
        a0, a1 = rows_p[pl.ds(x * 64, 32), :], rows_p[pl.ds(x * 64 + 32, 32), :]
        p_out[pl.ds(x * 64, 32, stride=2), :] = jnp.where(low, a0, swap(a1))
        p_out[pl.ds(x * 64 + 1, 32, stride=2), :] = jnp.where(low, swap(a0), a1)
        s0, s1 = rows_s[pl.ds(x * 64, 32), :], rows_s[pl.ds(x * 64 + 32, 32), :]
        mats[pl.ds(x * 128, 32, stride=2), :] = jnp.where(low, s0, zero)
        mats[pl.ds(x * 128 + 1, 32, stride=2), :] = jnp.where(low, swap(s0), zero)
        mats[pl.ds(x * 128 + 64, 32, stride=2), :] = jnp.where(low, zero, swap(s1))
        mats[pl.ds(x * 128 + 65, 32, stride=2), :] = jnp.where(low, zero, s1)
    spread = []
    for x in range(FX):
        block = pl.ds(x * LANE, LANE)
        high, rest = split(mats[block, :])
        sh_out[block, :] = high
        sl_out[block, :] = rest
        u = dot3(split(p_out[part(x), :]), (high, rest), NN)
        u_out[part(x), :] = u
        spread.append(u)
    write_edges(spread, dl, dr, tl, tr)


def operator(v, u, sh, sl, stor, before, after, left, right):
    low = low_lanes(RHS)
    spread = [u[part(x), :] for x in range(FX)]
    ends = [before[...].astype(F32)] + spread + [after[...].astype(F32)]
    applied = []
    for x in range(FX):
        from_left = left[part(x // 2), :].astype(F32)
        from_right = right[part(x // 2), :].astype(F32)
        if x % 2 == 0:
            outside = jnp.where(low, from_left, swap(from_right))
        else:
            outside = jnp.where(low, swap(from_left), from_right)
        pulled = 4.0 * spread[x] - (ends[x] + ends[x + 2] + swap(spread[x]) + outside)
        block = pl.ds(x * LANE, LANE)
        capacity = jnp.concatenate([stor[2 * x : 2 * x + 1, :], stor[2 * x + 1 : 2 * x + 2, :]], axis=1)
        applied.append(
            capacity * v[part(x), :] + dot3(split(pulled), (sh[block, :], sl[block, :]), NT)
        )
    return applied


def second_kernel(v, u, sh, sl, stor, before, after, left, right, ap_out, u_out, dl, dr, tl, tr):
    applied = operator(v, u, sh, sl, stor, before, after, left, right)
    spread = []
    for x in range(FX):
        ap_out[part(x), :] = applied[x]
        block = pl.ds(x * LANE, LANE)
        s = dot3(split(applied[x]), (sh[block, :], sl[block, :]), NN)
        u_out[part(x), :] = s
        spread.append(s)
    write_edges(spread, dl, dr, tl, tr)


def order_kernel(order, v, ap, cells, grams, table):
    total = jnp.zeros((2 * RHS, 2 * RHS), F32)
    for x in range(FX):
        high, rest = split(jnp.concatenate([v[part(x), :], ap[part(x), :]], axis=0))
        table[: 2 * RHS, x * LANE : (x + 1) * LANE] = high
        table[2 * RHS :, x * LANE : (x + 1) * LANE] = rest
        total += dot3((high, rest), (high, rest), NT)
    grams[...] = total
    lane = lax.broadcasted_iota(jnp.int32, (LANE, LANE), 1)
    for g in range(FX):
        row = jnp.broadcast_to(order[:, g * LANE : (g + 1) * LANE], (LANE, LANE))
        wanted = jnp.transpose(row)
        picks = [
            jnp.where(wanted == lane + l * LANE, 1.0, 0.0).astype(BF16) for l in range(FX)
        ]
        cells[pl.ds(g * LANE, LANE), :] = dot(
            jnp.concatenate(picks, axis=1), table[...], NT
        ).astype(BF16)


def third_kernel(v, u, sh, sl, stor, before, after, left, right, grams, packed):
    applied = operator(v, u, sh, sl, stor, before, after, left, right)
    total = jnp.zeros((2 * RHS, RHS), F32)
    for x in range(FX):
        high, rest = split(jnp.concatenate([v[part(x), :], applied[x]], axis=0))
        total += dot3((high, rest), (high[RHS:], rest[RHS:]), NT)
    packed[0:128, :] = grams[...]
    packed[128:192, :] = jnp.concatenate([total[:RHS], total[RHS:]], axis=1)
    packed[192:256, :] = jnp.zeros((64, LANE), F32)


def eliminate(joined):
    order = joined.shape[0]
    row_index = lax.broadcasted_iota(jnp.int32, (order, 1), 0)
    column_index = lax.broadcasted_iota(jnp.int32, (order, order), 1)
    row_full = lax.broadcasted_iota(jnp.int32, (order, order), 0)
    for k in range(order):
        row = joined[k : k + 1, :]
        factor = joined[:, k : k + 1] / row[:, k : k + 1]
        factor = jnp.where(row_index == k, 0.0, factor)
        joined = joined - factor * row
    diagonal = jnp.sum(
        jnp.where(row_full == column_index, joined[:, :order], 0.0), axis=1, keepdims=True
    )
    return joined[:, order:] / diagonal


def symmetric(matrix):
    return 0.5 * (matrix + jnp.transpose(matrix))


def final_kernel(cell_total, packed, kriging, cells, sens, gram):
    m0 = symmetric(packed[0:64, 0:64])
    m1 = 0.5 * (packed[0:64, 64:128] + packed[64:128, 0:64])
    m2 = symmetric(packed[64:128, 64:128])
    m3 = symmetric(packed[128:192, 0:64])
    m4 = symmetric(packed[128:192, 64:128])
    weighted = dot(kriging[...], cells[...], NN)
    weighted = weighted[:, :LANE] + weighted[:, LANE:]
    first = eliminate(jnp.concatenate([m1, m0, m2], axis=1))
    alpha, shift = first[:, :RHS], first[:, RHS:]
    curved = symmetric(m3 - exact(m2, shift))
    target = m1 - exact(m2, alpha)
    gamma = eliminate(jnp.concatenate([curved, target], axis=1))
    mixed = alpha - exact(shift, gamma)
    rest = exact(m4, gamma) + exact(m3, mixed) - m2
    gram[...] = symmetric(exact(jnp.transpose(gamma), rest)) * (1.0 / cell_total)
    sens[...] = exact(weighted, jnp.concatenate([mixed, gamma], axis=0))


def call(kernel, shapes, *operands, scratch=(), flops=1000000):
    return pl.pallas_call(
        kernel,
        out_shape=[jax.ShapeDtypeStruct(shape, kind) for shape, kind in shapes],
        in_specs=[pl.BlockSpec(memory_space=pltpu.VMEM)] * len(operands),
        out_specs=[pl.BlockSpec(memory_space=pltpu.VMEM)] * len(shapes),
        scratch_shapes=list(scratch),
        compiler_params=PARAMS,
        cost_estimate=pl.CostEstimate(flops=flops, bytes_accessed=1 << 20, transcendentals=0),
    )(*operands)


EDGES = (((RHS, LANE), BF16), ((RHS, LANE), BF16), ((ROWS // 2, LANE), BF16), ((ROWS // 2, LANE), BF16))
FIELD = ((ROWS, LANE), F32)


def exchange(dl, dr, tl, tr):
    def along(axis, first, last):
        devices = lax.axis_size(axis)
        up = [(i, i + 1) for i in range(devices - 1)]
        down = [(i + 1, i) for i in range(devices - 1)]
        return lax.ppermute(last, axis, up), lax.ppermute(first, axis, down)

    return along("dom", dl, dr) + along("tile", tl, tr)


def member_groups(sizes, together):
    strides, total = [], 1
    for size in reversed(sizes):
        strides.insert(0, total)
        total *= size

    def numbers(axes):
        values = [0]
        for axis in axes:
            values = [v + i * strides[axis] for v in values for i in range(sizes[axis])]
        return values

    apart = [axis for axis in range(len(sizes)) if axis not in together]
    return [[base + v for v in numbers(together)] for base in numbers(apart)]


def reduce_all(packed):
    axes = ("dom", "tile")
    sizes = (4, 16, 2, 4)
    near = member_groups(sizes, (0, 2, 3))
    far = member_groups(sizes, (1,))

    def trade(array, groups):
        return lax.all_to_all(array, axes, 0, 0, axis_index_groups=groups, tiled=True)

    n, m = len(near[0]), len(far[0])
    mine = jnp.sum(trade(packed.reshape(n, -1, LANE), near), axis=0)
    mine = jnp.sum(trade(jnp.broadcast_to(mine[None], (m,) + mine.shape), far), axis=0)
    return trade(jnp.broadcast_to(mine[None], (n,) + mine.shape), near).reshape(packed.shape)


def shards(pumping, coupling, storage, tile_order, kriging):
    groups = lax.axis_size("dom")
    cell_total = storage.shape[0] * CB * groups * lax.axis_size("tile")
    scratch = lambda rows: pltpu.VMEM((rows, LANE), F32)
    p, sh, sl, u, *edges = call(
        first_kernel,
        (FIELD, ((FX * LANE, LANE), BF16), ((FX * LANE, LANE), BF16), FIELD) + EDGES,
        pumping,
        coupling,
        scratch=(scratch(ROWS), scratch(ROWS), scratch(FX * LANE)),
    )
    ap, u, *edges = call(
        second_kernel, (FIELD, FIELD) + EDGES, p, u, sh, sl, storage, *exchange(*edges)
    )
    halo = exchange(*edges)
    cells, grams = call(
        order_kernel,
        (((FX * LANE, 4 * RHS), BF16), ((2 * RHS, 2 * RHS), F32)),
        tile_order,
        p,
        ap,
        scratch=(pltpu.VMEM((4 * RHS, FX * LANE), BF16),),
    )
    cells = lax.all_to_all(cells.reshape(groups, -1, 4 * RHS), "dom", 0, 0, tiled=True)
    (packed,) = call(
        third_kernel, (((256, LANE), F32),), ap, u, sh, sl, storage, *halo, grams
    )
    packed = reduce_all(packed)
    sens, gram = call(
        lambda *refs: final_kernel(cell_total, *refs),
        (((kriging.shape[0], RHS), F32), ((RHS, RHS), F32)),
        packed,
        kriging,
        cells.reshape(-1, 4 * RHS),
    )
    return sens, gram


def solution(mesh):
    spec = P(("dom", "tile"), None)
    return jax.shard_map(
        shards, mesh=mesh, in_specs=(spec,) * 5, out_specs=(spec, P()), check_vma=False
    )
```

```python
import jax
import jax.numpy as jnp
from jax import lax
from jax.experimental import pallas as pl
from jax.experimental.pallas import tpu as pltpu
from jax.sharding import PartitionSpec as P

RHS = 64
CB = 64
FX = 8
LANE = 128
ROWS = FX * RHS
F32 = jnp.float32
BF16 = jnp.bfloat16
HIGHEST = lax.Precision.HIGHEST
PARAMS = pltpu.CompilerParams(vmem_limit_bytes=40 * 1024 * 1024)
NN = (((1,), (0,)), ((), ()))
NT = (((1,), (1,)), ((), ()))


def split(value):
    high = value.astype(BF16)
    return high, (value - high.astype(F32)).astype(BF16)


def dot(left, right, dims):
    return lax.dot_general(left, right, dims, preferred_element_type=F32)


def dot3(left, right, dims):
    (lh, ll), (rh, rl) = left, right
    return dot(lh, rh, dims) + (dot(ll, rh, dims) + dot(lh, rl, dims))


def exact(left, right, dims=NN):
    return lax.dot_general(left, right, dims, precision=HIGHEST, preferred_element_type=F32)


def low_lanes(rows):
    return lax.broadcasted_iota(jnp.int32, (rows, LANE), 1) < CB


def swap(value):
    return pltpu.roll(value, CB, 1)


def part(x):
    return pl.ds(x * RHS, RHS)


def write_edges(spread, dl, dr, tl, tr):
    low = low_lanes(RHS)
    dl[...] = spread[0].astype(BF16)
    dr[...] = spread[FX - 1].astype(BF16)
    for i in range(FX // 2):
        even, odd = spread[2 * i], spread[2 * i + 1]
        tl[part(i), :] = jnp.where(low, even, swap(odd)).astype(BF16)
        tr[part(i), :] = jnp.where(low, swap(even), odd).astype(BF16)


def first_kernel(pump, coup, p_out, sh_out, sl_out, u_out, dl, dr, tl, tr, rows_p, rows_s, mats):
    for k in range(RHS // 2):
        chunk = slice(k * LANE, (k + 1) * LANE)
        rows_p[pl.ds(k, 16, stride=32), :] = pump[:, chunk]
        rows_s[pl.ds(k, 16, stride=32), :] = coup[:, chunk]
    low = low_lanes(32)
    zero = jnp.zeros((32, LANE), F32)
    for x in range(FX):
        a0, a1 = rows_p[pl.ds(x * 64, 32), :], rows_p[pl.ds(x * 64 + 32, 32), :]
        p_out[pl.ds(x * 64, 32, stride=2), :] = jnp.where(low, a0, swap(a1))
        p_out[pl.ds(x * 64 + 1, 32, stride=2), :] = jnp.where(low, swap(a0), a1)
        s0, s1 = rows_s[pl.ds(x * 64, 32), :], rows_s[pl.ds(x * 64 + 32, 32), :]
        mats[pl.ds(x * 128, 32, stride=2), :] = jnp.where(low, s0, zero)
        mats[pl.ds(x * 128 + 1, 32, stride=2), :] = jnp.where(low, swap(s0), zero)
        mats[pl.ds(x * 128 + 64, 32, stride=2), :] = jnp.where(low, zero, swap(s1))
        mats[pl.ds(x * 128 + 65, 32, stride=2), :] = jnp.where(low, zero, s1)
    spread = []
    for x in range(FX):
        block = pl.ds(x * LANE, LANE)
        high, rest = split(mats[block, :])
        sh_out[block, :] = high
        sl_out[block, :] = rest
        u = dot3(split(p_out[part(x), :]), (high, rest), NN)
        u_out[part(x), :] = u
        spread.append(u)
    write_edges(spread, dl, dr, tl, tr)


def operator(v, u, sh, sl, stor, before, after, left, right):
    low = low_lanes(RHS)
    spread = [u[part(x), :] for x in range(FX)]
    ends = [before[...].astype(F32)] + spread + [after[...].astype(F32)]
    applied = []
    for x in range(FX):
        from_left = left[part(x // 2), :].astype(F32)
        from_right = right[part(x // 2), :].astype(F32)
        if x % 2 == 0:
            outside = jnp.where(low, from_left, swap(from_right))
        else:
            outside = jnp.where(low, swap(from_left), from_right)
        pulled = 4.0 * spread[x] - (ends[x] + ends[x + 2] + swap(spread[x]) + outside)
        block = pl.ds(x * LANE, LANE)
        capacity = jnp.concatenate([stor[2 * x : 2 * x + 1, :], stor[2 * x + 1 : 2 * x + 2, :]], axis=1)
        applied.append(
            capacity * v[part(x), :] + dot3(split(pulled), (sh[block, :], sl[block, :]), NT)
        )
    return applied


def second_kernel(v, u, sh, sl, stor, before, after, left, right, ap_out, u_out, dl, dr, tl, tr):
    applied = operator(v, u, sh, sl, stor, before, after, left, right)
    spread = []
    for x in range(FX):
        ap_out[part(x), :] = applied[x]
        block = pl.ds(x * LANE, LANE)
        s = dot3(split(applied[x]), (sh[block, :], sl[block, :]), NN)
        u_out[part(x), :] = s
        spread.append(s)
    write_edges(spread, dl, dr, tl, tr)


def order_kernel(order, v, ap, cells, grams, table):
    total = jnp.zeros((2 * RHS, 2 * RHS), F32)
    for x in range(FX):
        high, rest = split(jnp.concatenate([v[part(x), :], ap[part(x), :]], axis=0))
        table[: 2 * RHS, x * LANE : (x + 1) * LANE] = high
        table[2 * RHS :, x * LANE : (x + 1) * LANE] = rest
        total += dot3((high, rest), (high, rest), NT)
    grams[...] = total
    lane = lax.broadcasted_iota(jnp.int32, (LANE, LANE), 1)
    for g in range(FX):
        row = jnp.broadcast_to(order[:, g * LANE : (g + 1) * LANE], (LANE, LANE))
        wanted = jnp.transpose(row)
        picks = [
            jnp.where(wanted == lane + l * LANE, 1.0, 0.0).astype(BF16) for l in range(FX)
        ]
        cells[pl.ds(g * LANE, LANE), :] = dot(
            jnp.concatenate(picks, axis=1), table[...], NT
        ).astype(BF16)


def third_kernel(v, u, sh, sl, stor, before, after, left, right, grams, kriging, cells, packed, weighted):
    product = dot(kriging[...], cells[...], NN)
    weighted[...] = product[:, :LANE] + product[:, LANE:]
    applied = operator(v, u, sh, sl, stor, before, after, left, right)
    total = jnp.zeros((2 * RHS, RHS), F32)
    for x in range(FX):
        high, rest = split(jnp.concatenate([v[part(x), :], applied[x]], axis=0))
        total += dot3((high, rest), (high[RHS:], rest[RHS:]), NT)
    packed[0:128, :] = grams[...]
    packed[128:192, :] = jnp.concatenate([total[:RHS], total[RHS:]], axis=1)
    packed[192:256, :] = jnp.zeros((64, LANE), F32)


def eliminate(joined):
    order = joined.shape[0]
    row_index = lax.broadcasted_iota(jnp.int32, (order, 1), 0)
    column_index = lax.broadcasted_iota(jnp.int32, (order, order), 1)
    row_full = lax.broadcasted_iota(jnp.int32, (order, order), 0)
    for k in range(order):
        row = joined[k : k + 1, :]
        factor = joined[:, k : k + 1] / row[:, k : k + 1]
        factor = jnp.where(row_index == k, 0.0, factor)
        joined = joined - factor * row
    diagonal = jnp.sum(
        jnp.where(row_full == column_index, joined[:, :order], 0.0), axis=1, keepdims=True
    )
    return joined[:, order:] / diagonal


def symmetric(matrix):
    return 0.5 * (matrix + jnp.transpose(matrix))


def final_kernel(cell_total, packed, weighted, sens, gram):
    m0 = symmetric(packed[0:64, 0:64])
    m1 = 0.5 * (packed[0:64, 64:128] + packed[64:128, 0:64])
    m2 = symmetric(packed[64:128, 64:128])
    m3 = symmetric(packed[128:192, 0:64])
    m4 = symmetric(packed[128:192, 64:128])
    first = eliminate(jnp.concatenate([m1, m0, m2], axis=1))
    alpha, shift = first[:, :RHS], first[:, RHS:]
    curved = symmetric(m3 - exact(m2, shift))
    target = m1 - exact(m2, alpha)
    gamma = eliminate(jnp.concatenate([curved, target], axis=1))
    mixed = alpha - exact(shift, gamma)
    rest = exact(m4, gamma) + exact(m3, mixed) - m2
    gram[...] = symmetric(exact(jnp.transpose(gamma), rest)) * (1.0 / cell_total)
    sens[...] = exact(weighted[...], jnp.concatenate([mixed, gamma], axis=0))


def call(kernel, shapes, *operands, scratch=(), flops=1000000):
    return pl.pallas_call(
        kernel,
        out_shape=[jax.ShapeDtypeStruct(shape, kind) for shape, kind in shapes],
        in_specs=[pl.BlockSpec(memory_space=pltpu.VMEM)] * len(operands),
        out_specs=[pl.BlockSpec(memory_space=pltpu.VMEM)] * len(shapes),
        scratch_shapes=list(scratch),
        compiler_params=PARAMS,
        cost_estimate=pl.CostEstimate(flops=flops, bytes_accessed=1 << 20, transcendentals=0),
    )(*operands)


EDGES = (((RHS, LANE), BF16), ((RHS, LANE), BF16), ((ROWS // 2, LANE), BF16), ((ROWS // 2, LANE), BF16))
FIELD = ((ROWS, LANE), F32)


def exchange(dl, dr, tl, tr):
    def along(axis, first, last):
        devices = lax.axis_size(axis)
        up = [(i, i + 1) for i in range(devices - 1)]
        down = [(i + 1, i) for i in range(devices - 1)]
        return lax.ppermute(last, axis, up), lax.ppermute(first, axis, down)

    return along("dom", dl, dr) + along("tile", tl, tr)


def member_groups(sizes, together):
    strides, total = [], 1
    for size in reversed(sizes):
        strides.insert(0, total)
        total *= size

    def numbers(axes):
        values = [0]
        for axis in axes:
            values = [v + i * strides[axis] for v in values for i in range(sizes[axis])]
        return values

    apart = [axis for axis in range(len(sizes)) if axis not in together]
    return [[base + v for v in numbers(together)] for base in numbers(apart)]


def reduce_all(packed):
    axes = ("dom", "tile")
    sizes = (4, 16, 2, 4)
    near = member_groups(sizes, (0, 2, 3))
    far = member_groups(sizes, (1,))

    def trade(array, groups):
        return lax.all_to_all(array, axes, 0, 0, axis_index_groups=groups, tiled=True)

    n, m = len(near[0]), len(far[0])
    mine = jnp.sum(trade(packed.reshape(n, -1, LANE), near), axis=0)
    mine = jnp.sum(trade(jnp.broadcast_to(mine[None], (m,) + mine.shape), far), axis=0)
    return trade(jnp.broadcast_to(mine[None], (n,) + mine.shape), near).reshape(packed.shape)


def shards(pumping, coupling, storage, tile_order, kriging):
    groups = lax.axis_size("dom")
    cell_total = storage.shape[0] * CB * groups * lax.axis_size("tile")
    scratch = lambda rows: pltpu.VMEM((rows, LANE), F32)
    p, sh, sl, u, *edges = call(
        first_kernel,
        (FIELD, ((FX * LANE, LANE), BF16), ((FX * LANE, LANE), BF16), FIELD) + EDGES,
        pumping,
        coupling,
        scratch=(scratch(ROWS), scratch(ROWS), scratch(FX * LANE)),
    )
    ap, u, *edges = call(
        second_kernel, (FIELD, FIELD) + EDGES, p, u, sh, sl, storage, *exchange(*edges)
    )
    halo = exchange(*edges)
    cells, grams = call(
        order_kernel,
        (((FX * LANE, 4 * RHS), BF16), ((2 * RHS, 2 * RHS), F32)),
        tile_order,
        p,
        ap,
        scratch=(pltpu.VMEM((4 * RHS, FX * LANE), BF16),),
    )
    cells = lax.all_to_all(cells.reshape(groups, -1, 4 * RHS), "dom", 0, 0, tiled=True)
    packed, weighted = call(
        third_kernel,
        (((256, LANE), F32), ((kriging.shape[0], LANE), F32)),
        *(ap, u, sh, sl, storage, *halo, grams, kriging, cells.reshape(-1, 4 * RHS)),
    )
    packed = reduce_all(packed)
    sens, gram = call(
        lambda *refs: final_kernel(cell_total, *refs),
        (((kriging.shape[0], RHS), F32), ((RHS, RHS), F32)),
        packed,
        weighted,
    )
    return sens, gram


def solution(mesh):
    spec = P(("dom", "tile"), None)
    return jax.shard_map(
        shards, mesh=mesh, in_specs=(spec,) * 5, out_specs=(spec, P()), check_vma=False
    )
```

```python
import jax
import jax.numpy as jnp
from jax import lax
from jax.experimental import pallas as pl
from jax.experimental.pallas import tpu as pltpu
from jax.sharding import PartitionSpec as P

RHS = 64
CB = 64
FX = 8
LANE = 128
ROWS = FX * RHS
F32 = jnp.float32
BF16 = jnp.bfloat16
HIGHEST = lax.Precision.HIGHEST
PARAMS = pltpu.CompilerParams(vmem_limit_bytes=40 * 1024 * 1024)
LONG = 10**11
NN = (((1,), (0,)), ((), ()))
NT = (((1,), (1,)), ((), ()))


def split(value):
    high = value.astype(BF16)
    return high, (value - high.astype(F32)).astype(BF16)


def dot(left, right, dims):
    return lax.dot_general(left, right, dims, preferred_element_type=F32)


def dot3(left, right, dims):
    (lh, ll), (rh, rl) = left, right
    return dot(lh, rh, dims) + (dot(ll, rh, dims) + dot(lh, rl, dims))


def exact(left, right, dims=NN):
    return lax.dot_general(left, right, dims, precision=HIGHEST, preferred_element_type=F32)


def low_lanes(rows):
    return lax.broadcasted_iota(jnp.int32, (rows, LANE), 1) < CB


def swap(value):
    return pltpu.roll(value, CB, 1)


def part(x):
    return pl.ds(x * RHS, RHS)


def write_edges(spread, dl, dr, tl, tr):
    low = low_lanes(RHS)
    dl[...] = spread[0].astype(BF16)
    dr[...] = spread[FX - 1].astype(BF16)
    for i in range(FX // 2):
        even, odd = spread[2 * i], spread[2 * i + 1]
        tl[part(i), :] = jnp.where(low, even, swap(odd)).astype(BF16)
        tr[part(i), :] = jnp.where(low, swap(even), odd).astype(BF16)


def first_kernel(pump, coup, p_out, sh_out, sl_out, u_out, dl, dr, tl, tr, rows_p, rows_s, mats):
    for k in range(RHS // 2):
        chunk = slice(k * LANE, (k + 1) * LANE)
        rows_p[pl.ds(k, 16, stride=32), :] = pump[:, chunk]
        rows_s[pl.ds(k, 16, stride=32), :] = coup[:, chunk]
    low = low_lanes(32)
    zero = jnp.zeros((32, LANE), F32)
    for x in range(FX):
        a0, a1 = rows_p[pl.ds(x * 64, 32), :], rows_p[pl.ds(x * 64 + 32, 32), :]
        p_out[pl.ds(x * 64, 32, stride=2), :] = jnp.where(low, a0, swap(a1))
        p_out[pl.ds(x * 64 + 1, 32, stride=2), :] = jnp.where(low, swap(a0), a1)
        s0, s1 = rows_s[pl.ds(x * 64, 32), :], rows_s[pl.ds(x * 64 + 32, 32), :]
        mats[pl.ds(x * 128, 32, stride=2), :] = jnp.where(low, s0, zero)
        mats[pl.ds(x * 128 + 1, 32, stride=2), :] = jnp.where(low, swap(s0), zero)
        mats[pl.ds(x * 128 + 64, 32, stride=2), :] = jnp.where(low, zero, swap(s1))
        mats[pl.ds(x * 128 + 65, 32, stride=2), :] = jnp.where(low, zero, s1)
    spread = []
    for x in range(FX):
        block = pl.ds(x * LANE, LANE)
        high, rest = split(mats[block, :])
        sh_out[block, :] = high
        sl_out[block, :] = rest
        u = dot3(split(p_out[part(x), :]), (high, rest), NN)
        u_out[part(x), :] = u
        spread.append(u)
    write_edges(spread, dl, dr, tl, tr)


def operator(v, u, sh, sl, stor, before, after, left, right):
    low = low_lanes(RHS)
    spread = [u[part(x), :] for x in range(FX)]
    ends = [before[...].astype(F32)] + spread + [after[...].astype(F32)]
    applied = []
    for x in range(FX):
        from_left = left[part(x // 2), :].astype(F32)
        from_right = right[part(x // 2), :].astype(F32)
        if x % 2 == 0:
            outside = jnp.where(low, from_left, swap(from_right))
        else:
            outside = jnp.where(low, swap(from_left), from_right)
        pulled = 4.0 * spread[x] - (ends[x] + ends[x + 2] + swap(spread[x]) + outside)
        block = pl.ds(x * LANE, LANE)
        capacity = jnp.concatenate([stor[2 * x : 2 * x + 1, :], stor[2 * x + 1 : 2 * x + 2, :]], axis=1)
        applied.append(
            capacity * v[part(x), :] + dot3(split(pulled), (sh[block, :], sl[block, :]), NT)
        )
    return applied


def second_kernel(v, u, sh, sl, stor, before, after, left, right, ap_out, u_out, dl, dr, tl, tr):
    applied = operator(v, u, sh, sl, stor, before, after, left, right)
    spread = []
    for x in range(FX):
        ap_out[part(x), :] = applied[x]
        block = pl.ds(x * LANE, LANE)
        s = dot3(split(applied[x]), (sh[block, :], sl[block, :]), NN)
        u_out[part(x), :] = s
        spread.append(s)
    write_edges(spread, dl, dr, tl, tr)


def deal(order, v, cells, table):
    for x in range(FX):
        high, rest = split(v[part(x), :])
        table[:RHS, x * LANE : (x + 1) * LANE] = high
        table[RHS:, x * LANE : (x + 1) * LANE] = rest
    lane = lax.broadcasted_iota(jnp.int32, (LANE, LANE), 1)
    for g in range(FX):
        row = jnp.broadcast_to(order[:, g * LANE : (g + 1) * LANE], (LANE, LANE))
        wanted = jnp.transpose(row)
        picks = [
            jnp.where(wanted == lane + l * LANE, 1.0, 0.0).astype(BF16) for l in range(FX)
        ]
        cells[pl.ds(g * LANE, LANE), :] = dot(
            jnp.concatenate(picks, axis=1), table[...], NT
        ).astype(BF16)


def weigh(kriging, cells):
    product = dot(kriging[...], cells[...], NN)
    return product[:, :RHS] + product[:, RHS:]


def deal_images(order, v, ap, kriging, arrived, cells, grams, weighted, table):
    deal(order, ap, cells, table)
    total = jnp.zeros((2 * RHS, 2 * RHS), F32)
    for x in range(FX):
        both = split(jnp.concatenate([v[part(x), :], ap[part(x), :]], axis=0))
        total += dot3(both, both, NT)
    grams[...] = total
    weighted[...] = weigh(kriging, arrived)


def third_kernel(v, u, sh, sl, stor, before, after, left, right, grams, packed):
    applied = operator(v, u, sh, sl, stor, before, after, left, right)
    total = jnp.zeros((2 * RHS, RHS), F32)
    for x in range(FX):
        high, rest = split(jnp.concatenate([v[part(x), :], applied[x]], axis=0))
        total += dot3((high, rest), (high[RHS:], rest[RHS:]), NT)
    m0 = symmetric(grams[:RHS, :RHS])
    m1 = 0.5 * (grams[:RHS, RHS:] + grams[RHS:, :RHS])
    m2 = symmetric(grams[RHS:, RHS:])
    m3 = symmetric(total[:RHS])
    m4 = symmetric(total[RHS:])
    row, column = square_index()
    upper = row <= column
    packed[:RHS, :] = jnp.concatenate([jnp.where(upper, m0, m2), jnp.where(upper, m1, m3)], axis=1)
    ends = jnp.where(row == 0, diagonal(m2), jnp.where(row == 1, diagonal(m3), 0.0))
    packed[RHS:, :] = jnp.concatenate([m4, ends], axis=1)


def weigh_images(kriging, arrived, packed, weighted, packed_out):
    weighted[...] = weigh(kriging, arrived)
    packed_out[...] = packed[...]


def square_index():
    return [lax.broadcasted_iota(jnp.int32, (RHS, RHS), d) for d in (0, 1)]


def diagonal(matrix):
    row, column = square_index()
    return jnp.sum(jnp.where(row == column, matrix, 0.0), axis=0, keepdims=True)


def unpack_pair(matrix, ends):
    row, column = square_index()
    turned = jnp.transpose(matrix)
    first = jnp.where(row <= column, matrix, turned)
    second = jnp.where(row > column, matrix, jnp.where(row < column, turned, ends))
    return first, second


def eliminate(joined, panel=8):
    order, width = joined.shape
    parts = [joined[g : g + panel, :] for g in range(0, order, panel)]
    index = lax.broadcasted_iota(jnp.int32, (panel, width), 0)

    def wide(value):
        pieces = [value] * (width // LANE)
        if width % LANE:
            pieces.append(value[:, : width % LANE])
        return jnp.concatenate(pieces, axis=1) if len(pieces) > 1 else value

    def apply(rows, at, c0, c1, inverse, where):
        r0, r1 = rows[at : at + 1, :], rows[at + 1 : at + 2, :]
        s0 = inverse[0] * r0 + inverse[1] * r1
        s1 = inverse[2] * r0 + inverse[3] * r1
        rest = rows - (c0 * s0 + c1 * s1)
        return jnp.where(where == at, s0, jnp.where(where == at + 1, s1, rest))

    for g in range(len(parts)):
        rows = parts[g]
        first = g * panel
        columns = [
            jnp.broadcast_to(rows[:, first + q : first + q + 1], (panel, LANE)) for q in range(panel)
        ]
        for at in range(0, panel, 2):
            c0, c1 = columns[at], columns[at + 1]
            a, c = c0[at : at + 1, :], c0[at + 1 : at + 2, :]
            b, d = c1[at : at + 1, :], c1[at + 1 : at + 2, :]
            scale = 1.0 / (a * d - b * c)
            inverse = (d * scale, -b * scale, -c * scale, a * scale)
            for q in range(at + 2, panel):
                columns[q] = apply(columns[q], at, c0, c1, inverse, index[:, :LANE])
            rows = apply(rows, at, wide(c0), wide(c1), [wide(v) for v in inverse], index)
        parts[g] = rows
        for h in range(len(parts)):
            if h != g:
                taken = None
                for q in range(panel):
                    column = jnp.broadcast_to(parts[h][:, first + q : first + q + 1], (panel, width))
                    term = column * rows[q : q + 1, :]
                    taken = term if taken is None else taken + term
                parts[h] = parts[h] - taken
    return jnp.concatenate(parts, axis=0)[:, order:]


def symmetric(matrix):
    return 0.5 * (matrix + jnp.transpose(matrix))


def final_kernel(cell_total, packed, weighted_p, weighted_ap, sens, gram):
    m0, m2 = unpack_pair(packed[:RHS, :RHS], packed[RHS : RHS + 1, RHS:])
    m1, m3 = unpack_pair(packed[:RHS, RHS:], packed[RHS + 1 : RHS + 2, RHS:])
    m4 = packed[RHS:, :RHS]
    first = eliminate(jnp.concatenate([m1, m0, m2], axis=1))
    alpha, shift = first[:, :RHS], first[:, RHS:]
    curved = symmetric(m3 - exact(m2, shift))
    target = m1 - exact(m2, alpha)
    gamma = eliminate(jnp.concatenate([curved, target], axis=1))
    mixed = alpha - exact(shift, gamma)
    rest = exact(m4, gamma) + exact(m3, mixed) - m2
    gram[...] = symmetric(exact(jnp.transpose(gamma), rest)) * (1.0 / cell_total)
    sens[...] = exact(weighted_p[...], mixed) + exact(weighted_ap[...], gamma)


def call(kernel, shapes, *operands, scratch=(), flops=1000000):
    return pl.pallas_call(
        kernel,
        out_shape=[jax.ShapeDtypeStruct(shape, kind) for shape, kind in shapes],
        in_specs=[pl.BlockSpec(memory_space=pltpu.VMEM)] * len(operands),
        out_specs=[pl.BlockSpec(memory_space=pltpu.VMEM)] * len(shapes),
        scratch_shapes=list(scratch),
        compiler_params=PARAMS,
        cost_estimate=pl.CostEstimate(flops=flops, bytes_accessed=1 << 20, transcendentals=0),
    )(*operands)


EDGES = (((RHS, LANE), BF16), ((RHS, LANE), BF16), ((ROWS // 2, LANE), BF16), ((ROWS // 2, LANE), BF16))
FIELD = ((ROWS, LANE), F32)


def exchange(dl, dr, tl, tr):
    def along(axis, first, last):
        devices = lax.axis_size(axis)
        up = [(i, i + 1) for i in range(devices - 1)]
        down = [(i + 1, i) for i in range(devices - 1)]
        return lax.ppermute(last, axis, up), lax.ppermute(first, axis, down)

    return along("dom", dl, dr) + along("tile", tl, tr)


def member_groups(sizes, together):
    strides, total = [], 1
    for size in reversed(sizes):
        strides.insert(0, total)
        total *= size

    def numbers(axes):
        values = [0]
        for axis in axes:
            values = [v + i * strides[axis] for v in values for i in range(sizes[axis])]
        return values

    apart = [axis for axis in range(len(sizes)) if axis not in together]
    return [[base + v for v in numbers(together)] for base in numbers(apart)]


def reduce_all(packed):
    axes = ("dom", "tile")
    sizes = (4, 16, 2, 4)
    near = member_groups(sizes, (0, 2, 3))
    far = member_groups(sizes, (1,))

    def trade(array, groups):
        return lax.all_to_all(array, axes, 0, 0, axis_index_groups=groups, tiled=True)

    n, m = len(near[0]), len(far[0])
    mine = jnp.sum(trade(packed.reshape(n, -1, LANE), near), axis=0)
    mine = jnp.sum(trade(jnp.broadcast_to(mine[None], (m,) + mine.shape), far), axis=0)
    return trade(jnp.broadcast_to(mine[None], (n,) + mine.shape), near).reshape(packed.shape)


def shards(pumping, coupling, storage, tile_order, kriging):
    groups = lax.axis_size("dom")
    cell_total = storage.shape[0] * CB * groups * lax.axis_size("tile")
    scratch = lambda rows: pltpu.VMEM((rows, LANE), F32)
    p, sh, sl, u, *edges = call(
        first_kernel,
        (FIELD, ((FX * LANE, LANE), BF16), ((FX * LANE, LANE), BF16), FIELD) + EDGES,
        pumping,
        coupling,
        scratch=(scratch(ROWS), scratch(ROWS), scratch(FX * LANE)),
    )
    halo = exchange(*edges)
    table = pltpu.VMEM((2 * RHS, FX * LANE), BF16)
    cells = ((FX * LANE, 2 * RHS), BF16)
    product = ((kriging.shape[0], RHS), F32)

    def deliver(rows):
        rows = rows.reshape(groups, -1, 2 * RHS)
        return lax.all_to_all(rows, "dom", 0, 0, tiled=True).reshape(-1, 2 * RHS)

    (dealt,) = call(deal, (cells,), tile_order, p, scratch=(table,))
    arrived = deliver(dealt)
    ap, u, *edges = call(
        second_kernel, (FIELD, FIELD) + EDGES, p, u, sh, sl, storage, *halo, flops=LONG
    )
    halo = exchange(*edges)
    dealt, grams, weighted_p = call(
        deal_images,
        (cells, ((2 * RHS, 2 * RHS), F32), product),
        *(tile_order, p, ap, kriging, arrived),
        scratch=(table,),
    )
    arrived = deliver(dealt)
    moments = ((2 * RHS, LANE), F32)
    (packed,) = call(
        third_kernel, (moments,), *(ap, u, sh, sl, storage, *halo, grams), flops=LONG
    )
    weighted_ap, packed = call(weigh_images, (product, moments), kriging, arrived, packed)
    packed = reduce_all(packed)
    sens, gram = call(
        lambda *refs: final_kernel(cell_total, *refs),
        (((kriging.shape[0], RHS), F32), ((RHS, RHS), F32)),
        packed,
        weighted_p,
        weighted_ap,
    )
    return sens, gram


def solution(mesh):
    spec = P(("dom", "tile"), None)
    return jax.shard_map(
        shards, mesh=mesh, in_specs=(spec,) * 5, out_specs=(spec, P()), check_vma=False
    )
```

```python
import jax
import jax.numpy as jnp
from jax import lax
from jax.experimental import pallas as pl
from jax.experimental.pallas import tpu as pltpu
from jax.sharding import PartitionSpec as P

RHS = 64
CB = 64
FX = 8
LANE = 128
ROWS = FX * RHS
F32 = jnp.float32
BF16 = jnp.bfloat16
HIGHEST = lax.Precision.HIGHEST
PARAMS = pltpu.CompilerParams(vmem_limit_bytes=40 * 1024 * 1024)
PIECES = 4
WIDTH = RHS * CB // PIECES
LONG = 10**11
NN = (((1,), (0,)), ((), ()))
NT = (((1,), (1,)), ((), ()))


def split(value):
    high = value.astype(BF16)
    return high, (value - high.astype(F32)).astype(BF16)


def dot(left, right, dims):
    return lax.dot_general(left, right, dims, preferred_element_type=F32)


def dot3(left, right, dims):
    (lh, ll), (rh, rl) = left, right
    return dot(lh, rh, dims) + (dot(ll, rh, dims) + dot(lh, rl, dims))


def exact(left, right, dims=NN):
    return lax.dot_general(left, right, dims, precision=HIGHEST, preferred_element_type=F32)


def low_lanes(rows):
    return lax.broadcasted_iota(jnp.int32, (rows, LANE), 1) < CB


def swap(value):
    return pltpu.roll(value, CB, 1)


def part(x):
    return pl.ds(x * RHS, RHS)


def write_edges(spread, dl, dr, tl, tr):
    low = low_lanes(RHS)
    dl[...] = spread[0].astype(BF16)
    dr[...] = spread[FX - 1].astype(BF16)
    for i in range(FX // 2):
        even, odd = spread[2 * i], spread[2 * i + 1]
        tl[part(i), :] = jnp.where(low, even, swap(odd)).astype(BF16)
        tr[part(i), :] = jnp.where(low, swap(even), odd).astype(BF16)


def first_kernel(pump_hbm, coup_hbm, p_out, sh_out, sl_out, u_out, dl, dr, tl, tr, pump, coup, rows_p, rows_s, mats, arrived):
    copies = []
    for i in range(PIECES):
        columns = pl.ds(i * WIDTH, WIDTH)
        for j, (source, target) in enumerate(((coup_hbm, coup), (pump_hbm, pump))):
            copies.append(
                pltpu.make_async_copy(source.at[:, columns], target.at[:, columns], arrived.at[j, i])
            )
    for copy in copies:
        copy.start()
    for copy in copies:
        copy.wait()
    for k in range(RHS // 2):
        chunk = slice(k * LANE, (k + 1) * LANE)
        rows_p[pl.ds(k, 16, stride=32), :] = pump[:, chunk]
        rows_s[pl.ds(k, 16, stride=32), :] = coup[:, chunk]
    low = low_lanes(32)
    zero = jnp.zeros((32, LANE), F32)
    for x in range(FX):
        a0, a1 = rows_p[pl.ds(x * 64, 32), :], rows_p[pl.ds(x * 64 + 32, 32), :]
        p_out[pl.ds(x * 64, 32, stride=2), :] = jnp.where(low, a0, swap(a1))
        p_out[pl.ds(x * 64 + 1, 32, stride=2), :] = jnp.where(low, swap(a0), a1)
        s0, s1 = rows_s[pl.ds(x * 64, 32), :], rows_s[pl.ds(x * 64 + 32, 32), :]
        mats[pl.ds(x * 128, 32, stride=2), :] = jnp.where(low, s0, zero)
        mats[pl.ds(x * 128 + 1, 32, stride=2), :] = jnp.where(low, swap(s0), zero)
        mats[pl.ds(x * 128 + 64, 32, stride=2), :] = jnp.where(low, zero, swap(s1))
        mats[pl.ds(x * 128 + 65, 32, stride=2), :] = jnp.where(low, zero, s1)
    spread = []
    for x in range(FX):
        block = pl.ds(x * LANE, LANE)
        high, rest = split(mats[block, :])
        sh_out[block, :] = high
        sl_out[block, :] = rest
        u = dot3(split(p_out[part(x), :]), (high, rest), NN)
        u_out[part(x), :] = u
        spread.append(u)
    write_edges(spread, dl, dr, tl, tr)


def operator(v, u, sh, sl, stor, before, after, left, right):
    low = low_lanes(RHS)
    spread = [u[part(x), :] for x in range(FX)]
    ends = [before[...].astype(F32)] + spread + [after[...].astype(F32)]
    applied = []
    for x in range(FX):
        from_left = left[part(x // 2), :].astype(F32)
        from_right = right[part(x // 2), :].astype(F32)
        if x % 2 == 0:
            outside = jnp.where(low, from_left, swap(from_right))
        else:
            outside = jnp.where(low, swap(from_left), from_right)
        pulled = 4.0 * spread[x] - (ends[x] + ends[x + 2] + swap(spread[x]) + outside)
        block = pl.ds(x * LANE, LANE)
        capacity = jnp.concatenate([stor[2 * x : 2 * x + 1, :], stor[2 * x + 1 : 2 * x + 2, :]], axis=1)
        applied.append(
            capacity * v[part(x), :] + dot3(split(pulled), (sh[block, :], sl[block, :]), NT)
        )
    return applied


def second_kernel(v, u, sh, sl, stor, before, after, left, right, ap_out, u_out, dl, dr, tl, tr):
    applied = operator(v, u, sh, sl, stor, before, after, left, right)
    spread = []
    for x in range(FX):
        ap_out[part(x), :] = applied[x]
        block = pl.ds(x * LANE, LANE)
        s = dot3(split(applied[x]), (sh[block, :], sl[block, :]), NN)
        u_out[part(x), :] = s
        spread.append(s)
    write_edges(spread, dl, dr, tl, tr)


def deal_kernel(order, v, ap, cells, grams, table):
    total = jnp.zeros((2 * RHS, 2 * RHS), F32)
    for x in range(FX):
        high, rest = split(jnp.concatenate([v[part(x), :], ap[part(x), :]], axis=0))
        table[: 2 * RHS, x * LANE : (x + 1) * LANE] = high
        table[2 * RHS :, x * LANE : (x + 1) * LANE] = rest
        total += dot3((high, rest), (high, rest), NT)
    grams[...] = total
    lane = lax.broadcasted_iota(jnp.int32, (LANE, LANE), 1)
    for g in range(FX):
        row = jnp.broadcast_to(order[:, g * LANE : (g + 1) * LANE], (LANE, LANE))
        wanted = jnp.transpose(row)
        picks = [
            jnp.where(wanted == lane + l * LANE, 1.0, 0.0).astype(BF16) for l in range(FX)
        ]
        cells[pl.ds(g * LANE, LANE), :] = dot(
            jnp.concatenate(picks, axis=1), table[...], NT
        ).astype(BF16)


def third_kernel(v, u, sh, sl, stor, before, after, left, right, grams, packed):
    applied = operator(v, u, sh, sl, stor, before, after, left, right)
    total = jnp.zeros((2 * RHS, RHS), F32)
    for x in range(FX):
        high, rest = split(jnp.concatenate([v[part(x), :], applied[x]], axis=0))
        total += dot3((high, rest), (high[RHS:], rest[RHS:]), NT)
    m0 = symmetric(grams[:RHS, :RHS])
    m1 = 0.5 * (grams[:RHS, RHS:] + grams[RHS:, :RHS])
    m2 = symmetric(grams[RHS:, RHS:])
    m3 = symmetric(total[:RHS])
    m4 = symmetric(total[RHS:])
    row, column = square_index()
    upper = row <= column
    packed[:RHS, :] = jnp.concatenate([jnp.where(upper, m0, m2), jnp.where(upper, m1, m3)], axis=1)
    ends = jnp.where(row == 0, diagonal(m2), jnp.where(row == 1, diagonal(m3), 0.0))
    packed[RHS:, :] = jnp.concatenate([m4, ends], axis=1)


def square_index():
    return [lax.broadcasted_iota(jnp.int32, (RHS, RHS), d) for d in (0, 1)]


def diagonal(matrix):
    row, column = square_index()
    return jnp.sum(jnp.where(row == column, matrix, 0.0), axis=0, keepdims=True)


def unpack_pair(matrix, ends):
    row, column = square_index()
    turned = jnp.transpose(matrix)
    first = jnp.where(row <= column, matrix, turned)
    second = jnp.where(row > column, matrix, jnp.where(row < column, turned, ends))
    return first, second


def eliminate(joined, panel=8):
    order, width = joined.shape
    parts = [joined[g : g + panel, :] for g in range(0, order, panel)]
    index = lax.broadcasted_iota(jnp.int32, (panel, width), 0)

    def wide(value):
        pieces = [value] * (width // LANE)
        if width % LANE:
            pieces.append(value[:, : width % LANE])
        return jnp.concatenate(pieces, axis=1) if len(pieces) > 1 else value

    def apply(rows, at, c0, c1, inverse, where):
        r0, r1 = rows[at : at + 1, :], rows[at + 1 : at + 2, :]
        s0 = inverse[0] * r0 + inverse[1] * r1
        s1 = inverse[2] * r0 + inverse[3] * r1
        rest = rows - (c0 * s0 + c1 * s1)
        return jnp.where(where == at, s0, jnp.where(where == at + 1, s1, rest))

    for g in range(len(parts)):
        rows = parts[g]
        first = g * panel
        columns = [
            jnp.broadcast_to(rows[:, first + q : first + q + 1], (panel, LANE)) for q in range(panel)
        ]
        for at in range(0, panel, 2):
            c0, c1 = columns[at], columns[at + 1]
            a, c = c0[at : at + 1, :], c0[at + 1 : at + 2, :]
            b, d = c1[at : at + 1, :], c1[at + 1 : at + 2, :]
            scale = 1.0 / (a * d - b * c)
            inverse = (d * scale, -b * scale, -c * scale, a * scale)
            for q in range(at + 2, panel):
                columns[q] = apply(columns[q], at, c0, c1, inverse, index[:, :LANE])
            rows = apply(rows, at, wide(c0), wide(c1), [wide(v) for v in inverse], index)
        parts[g] = rows
        for h in range(len(parts)):
            if h != g:
                taken = None
                for q in range(panel):
                    column = jnp.broadcast_to(parts[h][:, first + q : first + q + 1], (panel, width))
                    term = column * rows[q : q + 1, :]
                    taken = term if taken is None else taken + term
                parts[h] = parts[h] - taken
    return jnp.concatenate(parts, axis=0)[:, order:]


def symmetric(matrix):
    return 0.5 * (matrix + jnp.transpose(matrix))


def solve_kernel(packed, cells, heads, weights, later):
    m0, m2 = unpack_pair(packed[:RHS, :RHS], packed[RHS : RHS + 1, RHS:])
    m1, m3 = unpack_pair(packed[:RHS, RHS:], packed[RHS + 1 : RHS + 2, RHS:])
    first = eliminate(jnp.concatenate([m1, m0, m2], axis=1))
    alpha, shift = first[:, :RHS], first[:, RHS:]
    curved = symmetric(m3 - exact(m2, shift))
    target = m1 - exact(m2, alpha)
    gamma = eliminate(jnp.concatenate([curved, target], axis=1))
    mixed = alpha - exact(shift, gamma)
    both = jnp.concatenate([mixed, gamma], axis=0)
    high, rest = split(jnp.concatenate([both, both], axis=1))
    value = dot3((cells[:, :LANE], cells[:, LANE:]), (high, rest), NN)
    high = value.astype(BF16).astype(F32)
    heads[...] = jnp.where(low_lanes(FX * LANE), high, value - high).astype(BF16)
    weights[...] = both
    later[...] = jnp.concatenate([m2, m3], axis=1)


def gram_kernel(cell_total, packed, weights, later, gram):
    mixed, gamma = weights[:RHS, :], weights[RHS:, :]
    rest = exact(packed[RHS:, :RHS], gamma) + exact(later[:, RHS:], mixed) - later[:, :RHS]
    gram[...] = symmetric(exact(jnp.transpose(gamma), rest)) * (1.0 / cell_total)


def product_kernel(kriging, arrived, sens):
    product = dot(kriging[...], arrived[...], NN)
    sens[...] = product[:, :RHS] + product[:, RHS:]


def call(kernel, shapes, *operands, scratch=(), flops=1000000, place=pltpu.VMEM):
    return pl.pallas_call(
        kernel,
        out_shape=[jax.ShapeDtypeStruct(shape, kind) for shape, kind in shapes],
        in_specs=[pl.BlockSpec(memory_space=place)] * len(operands),
        out_specs=[pl.BlockSpec(memory_space=pltpu.VMEM)] * len(shapes),
        scratch_shapes=list(scratch),
        compiler_params=PARAMS,
        cost_estimate=pl.CostEstimate(flops=flops, bytes_accessed=1 << 20, transcendentals=0),
    )(*operands)


EDGES = (((RHS, LANE), BF16), ((RHS, LANE), BF16), ((ROWS // 2, LANE), BF16), ((ROWS // 2, LANE), BF16))
FIELD = ((ROWS, LANE), F32)


def exchange(dl, dr, tl, tr):
    def along(axis, first, last):
        devices = lax.axis_size(axis)
        up = [(i, i + 1) for i in range(devices - 1)]
        down = [(i + 1, i) for i in range(devices - 1)]
        return lax.ppermute(last, axis, up), lax.ppermute(first, axis, down)

    return along("dom", dl, dr) + along("tile", tl, tr)


def member_groups(sizes, together):
    strides, total = [], 1
    for size in reversed(sizes):
        strides.insert(0, total)
        total *= size

    def numbers(axes):
        values = [0]
        for axis in axes:
            values = [v + i * strides[axis] for v in values for i in range(sizes[axis])]
        return values

    apart = [axis for axis in range(len(sizes)) if axis not in together]
    return [[base + v for v in numbers(together)] for base in numbers(apart)]


def reduce_all(packed):
    axes = ("dom", "tile")
    sizes = (4, 16, 2, 4)
    near = member_groups(sizes, (0, 2, 3))
    far = member_groups(sizes, (1,))

    def trade(array, groups):
        return lax.all_to_all(array, axes, 0, 0, axis_index_groups=groups, tiled=True)

    n, m = len(near[0]), len(far[0])
    mine = jnp.sum(trade(packed.reshape(n, -1, LANE), near), axis=0)
    mine = jnp.sum(trade(jnp.broadcast_to(mine[None], (m,) + mine.shape), far), axis=0)
    return trade(jnp.broadcast_to(mine[None], (n,) + mine.shape), near).reshape(packed.shape)


def shards(pumping, coupling, storage, tile_order, kriging):
    groups = lax.axis_size("dom")
    cell_total = storage.shape[0] * CB * groups * lax.axis_size("tile")
    scratch = lambda rows: pltpu.VMEM((rows, LANE), F32)
    p, sh, sl, u, *edges = call(
        first_kernel,
        (FIELD, ((FX * LANE, LANE), BF16), ((FX * LANE, LANE), BF16), FIELD) + EDGES,
        pumping,
        coupling,
        scratch=(
            pltpu.VMEM((16, RHS * CB), F32),
            pltpu.VMEM((16, CB * CB), F32),
            scratch(ROWS),
            scratch(ROWS),
            scratch(FX * LANE),
            pltpu.SemaphoreType.DMA((2, PIECES)),
        ),
        place=pltpu.HBM,
    )
    halo = exchange(*edges)
    ap, u, *edges = call(second_kernel, (FIELD, FIELD) + EDGES, p, u, sh, sl, storage, *halo)
    halo = exchange(*edges)
    cells, grams = call(
        deal_kernel,
        (((FX * LANE, 4 * RHS), BF16), ((2 * RHS, LANE), F32)),
        *(tile_order, p, ap),
        scratch=(pltpu.VMEM((4 * RHS, FX * LANE), BF16),),
    )
    (packed,) = call(
        third_kernel, (((2 * RHS, LANE), F32),), ap, u, sh, sl, storage, *halo, grams
    )
    packed = reduce_all(packed)
    heads, weights, later = call(
        solve_kernel,
        (((FX * LANE, LANE), BF16), ((2 * RHS, RHS), F32), ((RHS, LANE), F32)),
        *(packed, cells),
    )
    heads = lax.all_to_all(heads.reshape(groups, -1, LANE), "dom", 0, 0, tiled=True)
    (gram,) = call(
        lambda *refs: gram_kernel(cell_total, *refs),
        (((RHS, RHS), F32),),
        *(packed, weights, later),
        flops=LONG,
    )
    (sens,) = call(
        product_kernel,
        (((kriging.shape[0], RHS), F32),),
        *(kriging, heads.reshape(-1, LANE)),
    )
    return sens, gram


def solution(mesh):
    spec = P(("dom", "tile"), None)
    return jax.shard_map(
        shards, mesh=mesh, in_specs=(spec,) * 5, out_specs=(spec, P()), check_vma=False
    )
```

```python
import jax
import jax.numpy as jnp
from jax import lax
from jax.experimental import pallas as pl
from jax.experimental.pallas import tpu as pltpu
from jax.sharding import PartitionSpec as P

RHS = 64
CB = 64
FX = 8
LANE = 128
ROWS = FX * RHS
F32 = jnp.float32
BF16 = jnp.bfloat16
HIGHEST = lax.Precision.HIGHEST
PARAMS = pltpu.CompilerParams(vmem_limit_bytes=40 * 1024 * 1024)
PIECES = 4
WIDTH = RHS * CB // PIECES
LONG = 10**11
NN = (((1,), (0,)), ((), ()))
NT = (((1,), (1,)), ((), ()))


def split(value):
    high = value.astype(BF16)
    return high, (value - high.astype(F32)).astype(BF16)


def dot(left, right, dims):
    return lax.dot_general(left, right, dims, preferred_element_type=F32)


def dot3(left, right, dims):
    (lh, ll), (rh, rl) = left, right
    return dot(lh, rh, dims) + (dot(ll, rh, dims) + dot(lh, rl, dims))


def exact(left, right, dims=NN):
    return lax.dot_general(left, right, dims, precision=HIGHEST, preferred_element_type=F32)


def low_lanes(rows):
    return lax.broadcasted_iota(jnp.int32, (rows, LANE), 1) < CB


def swap(value):
    return pltpu.roll(value, CB, 1)


def part(x):
    return pl.ds(x * RHS, RHS)


def is_even(axis):
    return lax.rem(lax.axis_index(axis), 2) == 0


def by_parity(axis, first, second):
    even = is_even(axis)
    return jnp.where(even, first, second), jnp.where(even, second, first)


def write_edges(spread, d1, d2, t1, t2):
    low = low_lanes(RHS)
    one, two = by_parity("dom", spread[FX - 1], spread[0])
    d1[...] = one.astype(BF16)
    d2[...] = two.astype(BF16)
    for i in range(FX // 2):
        even, odd = spread[2 * i], spread[2 * i + 1]
        left = jnp.where(low, even, swap(odd))
        right = jnp.where(low, swap(even), odd)
        one, two = by_parity("tile", right, left)
        t1[part(i), :] = one.astype(BF16)
        t2[part(i), :] = two.astype(BF16)


def first_kernel(pump_hbm, coup_hbm, p_out, sh_out, sl_out, u_out, d1, d2, t1, t2, pump, coup, rows_p, rows_s, mats, arrived):
    copies = []
    for i in range(PIECES):
        columns = pl.ds(i * WIDTH, WIDTH)
        for j, (source, target) in enumerate(((coup_hbm, coup), (pump_hbm, pump))):
            copies.append(
                pltpu.make_async_copy(source.at[:, columns], target.at[:, columns], arrived.at[j, i])
            )
    for copy in copies:
        copy.start()
    for copy in copies:
        copy.wait()
    for k in range(RHS // 2):
        chunk = slice(k * LANE, (k + 1) * LANE)
        rows_p[pl.ds(k, 16, stride=32), :] = pump[:, chunk]
        rows_s[pl.ds(k, 16, stride=32), :] = coup[:, chunk]
    low = low_lanes(32)
    zero = jnp.zeros((32, LANE), F32)
    for x in range(FX):
        a0, a1 = rows_p[pl.ds(x * 64, 32), :], rows_p[pl.ds(x * 64 + 32, 32), :]
        p_out[pl.ds(x * 64, 32, stride=2), :] = jnp.where(low, a0, swap(a1))
        p_out[pl.ds(x * 64 + 1, 32, stride=2), :] = jnp.where(low, swap(a0), a1)
        s0, s1 = rows_s[pl.ds(x * 64, 32), :], rows_s[pl.ds(x * 64 + 32, 32), :]
        mats[pl.ds(x * 128, 32, stride=2), :] = jnp.where(low, s0, zero)
        mats[pl.ds(x * 128 + 1, 32, stride=2), :] = jnp.where(low, swap(s0), zero)
        mats[pl.ds(x * 128 + 64, 32, stride=2), :] = jnp.where(low, zero, swap(s1))
        mats[pl.ds(x * 128 + 65, 32, stride=2), :] = jnp.where(low, zero, s1)
    spread = []
    for x in range(FX):
        block = pl.ds(x * LANE, LANE)
        high, rest = split(mats[block, :])
        sh_out[block, :] = high
        sl_out[block, :] = rest
        u = dot3(split(p_out[part(x), :]), (high, rest), NN)
        u_out[part(x), :] = u
        spread.append(u)
    write_edges(spread, d1, d2, t1, t2)


def operator(v, u, sh, sl, stor, d1, d2, t1, t2):
    low = low_lanes(RHS)
    spread = [u[part(x), :] for x in range(FX)]
    after, before = by_parity("dom", d1[...].astype(F32), d2[...].astype(F32))
    ends = [before] + spread + [after]
    right, left = [], []
    for i in range(FX // 2):
        one, two = by_parity("tile", t1[part(i), :].astype(F32), t2[part(i), :].astype(F32))
        right.append(one)
        left.append(two)
    applied = []
    for x in range(FX):
        from_left, from_right = left[x // 2], right[x // 2]
        if x % 2 == 0:
            outside = jnp.where(low, from_left, swap(from_right))
        else:
            outside = jnp.where(low, swap(from_left), from_right)
        pulled = 4.0 * spread[x] - (ends[x] + ends[x + 2] + swap(spread[x]) + outside)
        block = pl.ds(x * LANE, LANE)
        capacity = jnp.concatenate([stor[2 * x : 2 * x + 1, :], stor[2 * x + 1 : 2 * x + 2, :]], axis=1)
        applied.append(
            capacity * v[part(x), :] + dot3(split(pulled), (sh[block, :], sl[block, :]), NT)
        )
    return applied


def second_kernel(v, u, sh, sl, stor, d1, d2, t1, t2, ap_out, u_out, *edges):
    applied = operator(v, u, sh, sl, stor, d1, d2, t1, t2)
    spread = []
    for x in range(FX):
        ap_out[part(x), :] = applied[x]
        block = pl.ds(x * LANE, LANE)
        s = dot3(split(applied[x]), (sh[block, :], sl[block, :]), NN)
        u_out[part(x), :] = s
        spread.append(s)
    write_edges(spread, *edges)


def deal_kernel(order, v, ap, cells, table):
    for x in range(FX):
        high, rest = split(jnp.concatenate([v[part(x), :], ap[part(x), :]], axis=0))
        table[: 2 * RHS, x * LANE : (x + 1) * LANE] = high
        table[2 * RHS :, x * LANE : (x + 1) * LANE] = rest
    lane = lax.broadcasted_iota(jnp.int32, (LANE, LANE), 1)
    for g in range(FX):
        row = jnp.broadcast_to(order[:, g * LANE : (g + 1) * LANE], (LANE, LANE))
        wanted = jnp.transpose(row)
        picks = [
            jnp.where(wanted == lane + l * LANE, 1.0, 0.0).astype(BF16) for l in range(FX)
        ]
        cells[pl.ds(g * LANE, LANE), :] = dot(
            jnp.concatenate(picks, axis=1), table[...], NT
        ).astype(BF16)


def third_kernel(v, u, sh, sl, stor, d1, d2, t1, t2, p, packed):
    applied = operator(v, u, sh, sl, stor, d1, d2, t1, t2)
    base = jnp.zeros((2 * RHS, 2 * RHS), F32)
    total = jnp.zeros((2 * RHS, RHS), F32)
    for x in range(FX):
        low, image = split(jnp.concatenate([p[part(x), :], v[part(x), :]], axis=0)), split(applied[x])
        base += dot3(low, low, NT)
        both = [jnp.concatenate([a[RHS:], b], axis=0) for a, b in zip(low, image)]
        total += dot3(both, image, NT)
    m0 = symmetric(base[:RHS, :RHS])
    m1 = 0.5 * (base[:RHS, RHS:] + base[RHS:, :RHS])
    m2 = symmetric(base[RHS:, RHS:])
    m3 = symmetric(total[:RHS])
    m4 = symmetric(total[RHS:])
    row, column = square_index()
    upper = row <= column
    packed[:RHS, :] = jnp.concatenate([jnp.where(upper, m0, m2), jnp.where(upper, m1, m3)], axis=1)
    ends = jnp.where(row == 0, diagonal(m2), jnp.where(row == 1, diagonal(m3), 0.0))
    packed[RHS:, :] = jnp.concatenate([m4, ends], axis=1)


def square_index():
    return [lax.broadcasted_iota(jnp.int32, (RHS, RHS), d) for d in (0, 1)]


def diagonal(matrix):
    row, column = square_index()
    return jnp.sum(jnp.where(row == column, matrix, 0.0), axis=0, keepdims=True)


def unpack_pair(matrix, ends):
    row, column = square_index()
    turned = jnp.transpose(matrix)
    first = jnp.where(row <= column, matrix, turned)
    second = jnp.where(row > column, matrix, jnp.where(row < column, turned, ends))
    return first, second


def eliminate(joined, panel=8):
    order, width = joined.shape
    parts = [joined[g : g + panel, :] for g in range(0, order, panel)]
    index = lax.broadcasted_iota(jnp.int32, (panel, width), 0)

    def wide(value):
        pieces = [value] * (width // LANE)
        if width % LANE:
            pieces.append(value[:, : width % LANE])
        return jnp.concatenate(pieces, axis=1) if len(pieces) > 1 else value

    def apply(rows, at, c0, c1, inverse, where):
        r0, r1 = rows[at : at + 1, :], rows[at + 1 : at + 2, :]
        s0 = inverse[0] * r0 + inverse[1] * r1
        s1 = inverse[2] * r0 + inverse[3] * r1
        rest = rows - (c0 * s0 + c1 * s1)
        return jnp.where(where == at, s0, jnp.where(where == at + 1, s1, rest))

    for g in range(len(parts)):
        rows = parts[g]
        first = g * panel
        columns = [
            jnp.broadcast_to(rows[:, first + q : first + q + 1], (panel, LANE)) for q in range(panel)
        ]
        for at in range(0, panel, 2):
            c0, c1 = columns[at], columns[at + 1]
            a, c = c0[at : at + 1, :], c0[at + 1 : at + 2, :]
            b, d = c1[at : at + 1, :], c1[at + 1 : at + 2, :]
            scale = 1.0 / (a * d - b * c)
            inverse = (d * scale, -b * scale, -c * scale, a * scale)
            for q in range(at + 2, panel):
                columns[q] = apply(columns[q], at, c0, c1, inverse, index[:, :LANE])
            rows = apply(rows, at, wide(c0), wide(c1), [wide(v) for v in inverse], index)
        parts[g] = rows
        for h in range(len(parts)):
            if h != g:
                taken = None
                for q in range(panel):
                    column = jnp.broadcast_to(parts[h][:, first + q : first + q + 1], (panel, width))
                    term = column * rows[q : q + 1, :]
                    taken = term if taken is None else taken + term
                parts[h] = parts[h] - taken
    return jnp.concatenate(parts, axis=0)[:, order:]


def symmetric(matrix):
    return 0.5 * (matrix + jnp.transpose(matrix))


def solve_kernel(packed, cells, heads, weights, later):
    m0, m2 = unpack_pair(packed[:RHS, :RHS], packed[RHS : RHS + 1, RHS:])
    m1, m3 = unpack_pair(packed[:RHS, RHS:], packed[RHS + 1 : RHS + 2, RHS:])
    first = eliminate(jnp.concatenate([m1, m0, m2], axis=1))
    alpha, shift = first[:, :RHS], first[:, RHS:]
    curved = symmetric(m3 - exact(m2, shift))
    target = m1 - exact(m2, alpha)
    gamma = eliminate(jnp.concatenate([curved, target], axis=1))
    mixed = alpha - exact(shift, gamma)
    both = jnp.concatenate([mixed, gamma], axis=0)
    high, rest = split(jnp.concatenate([both, both], axis=1))
    value = dot3((cells[:, :LANE], cells[:, LANE:]), (high, rest), NN)
    high = value.astype(BF16).astype(F32)
    heads[...] = jnp.where(low_lanes(FX * LANE), high, value - high).astype(BF16)
    weights[...] = both
    later[...] = jnp.concatenate([m2, m3], axis=1)


def gram_kernel(cell_total, packed, weights, later, gram):
    mixed, gamma = weights[:RHS, :], weights[RHS:, :]
    rest = exact(packed[RHS:, :RHS], gamma) + exact(later[:, RHS:], mixed) - later[:, :RHS]
    gram[...] = symmetric(exact(jnp.transpose(gamma), rest)) * (1.0 / cell_total)


def product_kernel(kriging, arrived, sens):
    product = dot(kriging[...], arrived[...], NN)
    sens[...] = product[:, :RHS] + product[:, RHS:]


def call(kernel, shapes, *operands, scratch=(), flops=1000000, place=pltpu.VMEM):
    return pl.pallas_call(
        kernel,
        out_shape=[jax.ShapeDtypeStruct(shape, kind) for shape, kind in shapes],
        in_specs=[pl.BlockSpec(memory_space=place)] * len(operands),
        out_specs=[pl.BlockSpec(memory_space=pltpu.VMEM)] * len(shapes),
        scratch_shapes=list(scratch),
        compiler_params=PARAMS,
        cost_estimate=pl.CostEstimate(flops=flops, bytes_accessed=1 << 20, transcendentals=0),
    )(*operands)


EDGES = (((RHS, LANE), BF16), ((RHS, LANE), BF16), ((ROWS // 2, LANE), BF16), ((ROWS // 2, LANE), BF16))
FIELD = ((ROWS, LANE), F32)


def exchange(d1, d2, t1, t2):
    def along(axis, one, two):
        devices = lax.axis_size(axis)
        first = [(i, i ^ 1) for i in range(devices)]
        second = [(i, ((i + 1) ^ 1) - 1) for i in range(1, devices - 1)]
        return lax.ppermute(one, axis, first), lax.ppermute(two, axis, second)

    return along("dom", d1, d2) + along("tile", t1, t2)


def member_groups(sizes, together):
    strides, total = [], 1
    for size in reversed(sizes):
        strides.insert(0, total)
        total *= size

    def numbers(axes):
        values = [0]
        for axis in axes:
            values = [v + i * strides[axis] for v in values for i in range(sizes[axis])]
        return values

    apart = [axis for axis in range(len(sizes)) if axis not in together]
    return [[base + v for v in numbers(together)] for base in numbers(apart)]


def reduce_all(packed):
    axes = ("dom", "tile")
    sizes = (4, 16, 2, 4)
    near = member_groups(sizes, (0, 2, 3))
    far = member_groups(sizes, (1,))

    def trade(array, groups):
        return lax.all_to_all(array, axes, 0, 0, axis_index_groups=groups, tiled=True)

    n, m = len(near[0]), len(far[0])
    mine = jnp.sum(trade(packed.reshape(n, -1, LANE), near), axis=0)
    mine = jnp.sum(trade(jnp.broadcast_to(mine[None], (m,) + mine.shape), far), axis=0)
    return trade(jnp.broadcast_to(mine[None], (n,) + mine.shape), near).reshape(packed.shape)


def shards(pumping, coupling, storage, tile_order, kriging):
    groups = lax.axis_size("dom")
    cell_total = storage.shape[0] * CB * groups * lax.axis_size("tile")
    scratch = lambda rows: pltpu.VMEM((rows, LANE), F32)
    p, sh, sl, u, *edges = call(
        first_kernel,
        (FIELD, ((FX * LANE, LANE), BF16), ((FX * LANE, LANE), BF16), FIELD) + EDGES,
        pltpu.with_memory_space_constraint(pumping, pltpu.HBM),
        pltpu.with_memory_space_constraint(coupling, pltpu.HBM),
        scratch=(
            pltpu.VMEM((16, RHS * CB), F32),
            pltpu.VMEM((16, CB * CB), F32),
            scratch(ROWS),
            scratch(ROWS),
            scratch(FX * LANE),
            pltpu.SemaphoreType.DMA((2, PIECES)),
        ),
        place=pltpu.HBM,
    )
    halo = exchange(*edges)
    ap, u, *edges = call(second_kernel, (FIELD, FIELD) + EDGES, p, u, sh, sl, storage, *halo)
    halo = exchange(*edges)
    (packed,) = call(
        third_kernel, (((2 * RHS, LANE), F32),), ap, u, sh, sl, storage, *halo, p
    )
    (cells,) = call(
        deal_kernel,
        (((FX * LANE, 4 * RHS), BF16),),
        *(tile_order, p, ap),
        scratch=(pltpu.VMEM((4 * RHS, FX * LANE), BF16),),
        flops=LONG,
    )
    packed = reduce_all(packed)
    heads, weights, later = call(
        solve_kernel,
        (((FX * LANE, LANE), BF16), ((2 * RHS, RHS), F32), ((RHS, LANE), F32)),
        *(packed, cells),
    )
    heads = lax.all_to_all(heads.reshape(groups, -1, LANE), "dom", 0, 0, tiled=True)
    (gram,) = call(
        lambda *refs: gram_kernel(cell_total, *refs),
        (((RHS, RHS), F32),),
        *(packed, weights, later),
        flops=LONG,
    )
    (sens,) = call(
        product_kernel,
        (((kriging.shape[0], RHS), F32),),
        *(kriging, heads.reshape(-1, LANE)),
    )
    return sens, gram


def solution(mesh):
    spec = P(("dom", "tile"), None)
    return jax.shard_map(
        shards, mesh=mesh, in_specs=(spec,) * 5, out_specs=(spec, P()), check_vma=False
    )
```

```python
import jax
import jax.numpy as jnp
from jax import lax
from jax.experimental import pallas as pl
from jax.experimental.pallas import tpu as pltpu
from jax.sharding import PartitionSpec as P

RHS = 64
CB = 64
FX = 8
LANE = 128
ROWS = FX * RHS
F32 = jnp.float32
BF16 = jnp.bfloat16
HIGHEST = lax.Precision.HIGHEST
PARAMS = pltpu.CompilerParams(vmem_limit_bytes=40 * 1024 * 1024)
PIECES = 4
WIDTH = RHS * CB // PIECES
LONG = 10**11
NN = (((1,), (0,)), ((), ()))
NT = (((1,), (1,)), ((), ()))


def split(value):
    high = value.astype(BF16)
    return high, (value - high.astype(F32)).astype(BF16)


def dot(left, right, dims):
    return lax.dot_general(left, right, dims, preferred_element_type=F32)


def dot3(left, right, dims):
    (lh, ll), (rh, rl) = left, right
    return dot(lh, rh, dims) + (dot(ll, rh, dims) + dot(lh, rl, dims))


def exact(left, right, dims=NN):
    return lax.dot_general(left, right, dims, precision=HIGHEST, preferred_element_type=F32)


def low_lanes(rows):
    return lax.broadcasted_iota(jnp.int32, (rows, LANE), 1) < CB


def swap(value):
    return pltpu.roll(value, CB, 1)


def part(x):
    return pl.ds(x * RHS, RHS)


def is_even(axis):
    return lax.rem(lax.axis_index(axis), 2) == 0


def by_parity(axis, first, second):
    even = is_even(axis)
    return jnp.where(even, first, second), jnp.where(even, second, first)


def write_edges(spread, d1, d2, t1, t2):
    low = low_lanes(RHS)
    one, two = by_parity("dom", spread[FX - 1], spread[0])
    d1[...] = one.astype(BF16)
    d2[:RHS, :] = two.astype(BF16)
    d2[RHS:, :] = jnp.zeros((d2.shape[0] - RHS, LANE), BF16)
    for i in range(FX // 2):
        even, odd = spread[2 * i], spread[2 * i + 1]
        left = jnp.where(low, even, swap(odd))
        right = jnp.where(low, swap(even), odd)
        one, two = by_parity("tile", right, left)
        t1[part(i), :] = one.astype(BF16)
        t2[part(i), :] = two.astype(BF16)


def first_kernel(pump_hbm, coup_hbm, p_out, sh_out, sl_out, u_out, d1, d2, t1, t2, pump, coup, rows_p, rows_s, mats, arrived):
    copies = []
    for i in range(PIECES):
        columns = pl.ds(i * WIDTH, WIDTH)
        for j, (source, target) in enumerate(((coup_hbm, coup), (pump_hbm, pump))):
            copies.append(
                pltpu.make_async_copy(source.at[:, columns], target.at[:, columns], arrived.at[j, i])
            )
    for copy in copies:
        copy.start()
    for copy in copies:
        copy.wait()
    for k in range(RHS // 2):
        chunk = slice(k * LANE, (k + 1) * LANE)
        rows_p[pl.ds(k, 16, stride=32), :] = pump[:, chunk]
        rows_s[pl.ds(k, 16, stride=32), :] = coup[:, chunk]
    low = low_lanes(32)
    zero = jnp.zeros((32, LANE), F32)
    for x in range(FX):
        a0, a1 = rows_p[pl.ds(x * 64, 32), :], rows_p[pl.ds(x * 64 + 32, 32), :]
        p_out[pl.ds(x * 64, 32, stride=2), :] = jnp.where(low, a0, swap(a1))
        p_out[pl.ds(x * 64 + 1, 32, stride=2), :] = jnp.where(low, swap(a0), a1)
        s0, s1 = rows_s[pl.ds(x * 64, 32), :], rows_s[pl.ds(x * 64 + 32, 32), :]
        mats[pl.ds(x * 128, 32, stride=2), :] = jnp.where(low, s0, zero)
        mats[pl.ds(x * 128 + 1, 32, stride=2), :] = jnp.where(low, swap(s0), zero)
        mats[pl.ds(x * 128 + 64, 32, stride=2), :] = jnp.where(low, zero, swap(s1))
        mats[pl.ds(x * 128 + 65, 32, stride=2), :] = jnp.where(low, zero, s1)
    spread = []
    for x in range(FX):
        block = pl.ds(x * LANE, LANE)
        high, rest = split(mats[block, :])
        sh_out[block, :] = high
        sl_out[block, :] = rest
        u = dot3(split(p_out[part(x), :]), (high, rest), NN)
        u_out[part(x), :] = u
        spread.append(u)
    write_edges(spread, d1, d2, t1, t2)


def operator(v, u, sh, sl, stor, d1, d2, t1, t2):
    low = low_lanes(RHS)
    spread = [u[part(x), :] for x in range(FX)]
    after, before = by_parity("dom", d1[...].astype(F32), d2[:RHS, :].astype(F32))
    ends = [before] + spread + [after]
    right, left = [], []
    for i in range(FX // 2):
        one, two = by_parity("tile", t1[part(i), :].astype(F32), t2[part(i), :].astype(F32))
        right.append(one)
        left.append(two)
    applied = []
    for x in range(FX):
        from_left, from_right = left[x // 2], right[x // 2]
        if x % 2 == 0:
            outside = jnp.where(low, from_left, swap(from_right))
        else:
            outside = jnp.where(low, swap(from_left), from_right)
        pulled = 4.0 * spread[x] - (ends[x] + ends[x + 2] + swap(spread[x]) + outside)
        block = pl.ds(x * LANE, LANE)
        capacity = jnp.concatenate([stor[2 * x : 2 * x + 1, :], stor[2 * x + 1 : 2 * x + 2, :]], axis=1)
        applied.append(
            capacity * v[part(x), :] + dot3(split(pulled), (sh[block, :], sl[block, :]), NT)
        )
    return applied


def second_kernel(v, u, sh, sl, stor, d1, d2, t1, t2, ap_out, u_out, *edges):
    applied = operator(v, u, sh, sl, stor, d1, d2, t1, t2)
    spread = []
    for x in range(FX):
        ap_out[part(x), :] = applied[x]
        block = pl.ds(x * LANE, LANE)
        s = dot3(split(applied[x]), (sh[block, :], sl[block, :]), NN)
        u_out[part(x), :] = s
        spread.append(s)
    write_edges(spread, *edges)


def deal_kernel(order, v, ap, cells, table):
    for x in range(FX):
        high, rest = split(jnp.concatenate([v[part(x), :], ap[part(x), :]], axis=0))
        table[: 2 * RHS, x * LANE : (x + 1) * LANE] = high
        table[2 * RHS :, x * LANE : (x + 1) * LANE] = rest
    lane = lax.broadcasted_iota(jnp.int32, (LANE, LANE), 1)
    for g in range(FX):
        row = jnp.broadcast_to(order[:, g * LANE : (g + 1) * LANE], (LANE, LANE))
        wanted = jnp.transpose(row)
        picks = [
            jnp.where(wanted == lane + l * LANE, 1.0, 0.0).astype(BF16) for l in range(FX)
        ]
        cells[pl.ds(g * LANE, LANE), :] = dot(
            jnp.concatenate(picks, axis=1), table[...], NT
        ).astype(BF16)


def third_kernel(v, u, sh, sl, stor, d1, d2, t1, t2, p, packed):
    applied = operator(v, u, sh, sl, stor, d1, d2, t1, t2)
    base = jnp.zeros((2 * RHS, 2 * RHS), F32)
    total = jnp.zeros((2 * RHS, RHS), F32)
    for x in range(FX):
        low, image = split(jnp.concatenate([p[part(x), :], v[part(x), :]], axis=0)), split(applied[x])
        base += dot3(low, low, NT)
        both = [jnp.concatenate([a[RHS:], b], axis=0) for a, b in zip(low, image)]
        total += dot3(both, image, NT)
    m0 = symmetric(base[:RHS, :RHS])
    m1 = 0.5 * (base[:RHS, RHS:] + base[RHS:, :RHS])
    m2 = symmetric(base[RHS:, RHS:])
    m3 = symmetric(total[:RHS])
    m4 = symmetric(total[RHS:])
    row, column = square_index()
    upper = row <= column
    packed[:RHS, :] = jnp.concatenate([jnp.where(upper, m0, m2), jnp.where(upper, m1, m3)], axis=1)
    ends = jnp.where(row == 0, diagonal(m2), jnp.where(row == 1, diagonal(m3), 0.0))
    packed[RHS:, :] = jnp.concatenate([m4, ends], axis=1)


def square_index():
    return [lax.broadcasted_iota(jnp.int32, (RHS, RHS), d) for d in (0, 1)]


def diagonal(matrix):
    row, column = square_index()
    return jnp.sum(jnp.where(row == column, matrix, 0.0), axis=0, keepdims=True)


def unpack_pair(matrix, ends):
    row, column = square_index()
    turned = jnp.transpose(matrix)
    first = jnp.where(row <= column, matrix, turned)
    second = jnp.where(row > column, matrix, jnp.where(row < column, turned, ends))
    return first, second


def eliminate(joined, panel=8):
    order, width = joined.shape
    parts = [joined[g : g + panel, :] for g in range(0, order, panel)]
    index = lax.broadcasted_iota(jnp.int32, (panel, width), 0)

    def wide(value):
        pieces = [value] * (width // LANE)
        if width % LANE:
            pieces.append(value[:, : width % LANE])
        return jnp.concatenate(pieces, axis=1) if len(pieces) > 1 else value

    def apply(rows, at, c0, c1, inverse, where):
        r0, r1 = rows[at : at + 1, :], rows[at + 1 : at + 2, :]
        s0 = inverse[0] * r0 + inverse[1] * r1
        s1 = inverse[2] * r0 + inverse[3] * r1
        rest = rows - (c0 * s0 + c1 * s1)
        return jnp.where(where == at, s0, jnp.where(where == at + 1, s1, rest))

    for g in range(len(parts)):
        rows = parts[g]
        first = g * panel
        columns = [
            jnp.broadcast_to(rows[:, first + q : first + q + 1], (panel, LANE)) for q in range(panel)
        ]
        for at in range(0, panel, 2):
            c0, c1 = columns[at], columns[at + 1]
            a, c = c0[at : at + 1, :], c0[at + 1 : at + 2, :]
            b, d = c1[at : at + 1, :], c1[at + 1 : at + 2, :]
            scale = 1.0 / (a * d - b * c)
            inverse = (d * scale, -b * scale, -c * scale, a * scale)
            for q in range(at + 2, panel):
                columns[q] = apply(columns[q], at, c0, c1, inverse, index[:, :LANE])
            rows = apply(rows, at, wide(c0), wide(c1), [wide(v) for v in inverse], index)
        parts[g] = rows
        for h in range(len(parts)):
            if h != g:
                taken = None
                for q in range(panel):
                    column = jnp.broadcast_to(parts[h][:, first + q : first + q + 1], (panel, width))
                    term = column * rows[q : q + 1, :]
                    taken = term if taken is None else taken + term
                parts[h] = parts[h] - taken
    return jnp.concatenate(parts, axis=0)[:, order:]


def symmetric(matrix):
    return 0.5 * (matrix + jnp.transpose(matrix))


def solve_kernel(packed, cells, heads, weights, later):
    m0, m2 = unpack_pair(packed[:RHS, :RHS], packed[RHS : RHS + 1, RHS:])
    m1, m3 = unpack_pair(packed[:RHS, RHS:], packed[RHS + 1 : RHS + 2, RHS:])
    first = eliminate(jnp.concatenate([m1, m0, m2], axis=1))
    alpha, shift = first[:, :RHS], first[:, RHS:]
    curved = symmetric(m3 - exact(m2, shift))
    target = m1 - exact(m2, alpha)
    gamma = eliminate(jnp.concatenate([curved, target], axis=1))
    mixed = alpha - exact(shift, gamma)
    both = jnp.concatenate([mixed, gamma], axis=0)
    high, rest = split(jnp.concatenate([both, both], axis=1))
    value = dot3((cells[:, :LANE], cells[:, LANE:]), (high, rest), NN)
    high = value.astype(BF16).astype(F32)
    heads[...] = jnp.where(low_lanes(FX * LANE), high, value - high).astype(BF16)
    weights[...] = both
    later[...] = jnp.concatenate([m2, m3], axis=1)


def gram_kernel(cell_total, packed, weights, later, gram):
    mixed, gamma = weights[:RHS, :], weights[RHS:, :]
    rest = exact(packed[RHS:, :RHS], gamma) + exact(later[:, RHS:], mixed) - later[:, :RHS]
    gram[...] = symmetric(exact(jnp.transpose(gamma), rest)) * (1.0 / cell_total)


def product_kernel(kriging, arrived, sens):
    product = dot(kriging[...], arrived[...], NN)
    sens[...] = product[:, :RHS] + product[:, RHS:]


def call(kernel, shapes, *operands, scratch=(), flops=1000000, place=pltpu.VMEM):
    return pl.pallas_call(
        kernel,
        out_shape=[jax.ShapeDtypeStruct(shape, kind) for shape, kind in shapes],
        in_specs=[pl.BlockSpec(memory_space=place)] * len(operands),
        out_specs=[pl.BlockSpec(memory_space=pltpu.VMEM)] * len(shapes),
        scratch_shapes=list(scratch),
        compiler_params=PARAMS,
        cost_estimate=pl.CostEstimate(flops=flops, bytes_accessed=1 << 20, transcendentals=0),
    )(*operands)


EDGES = (((RHS, LANE), BF16), ((ROWS // 2 + 16, LANE), BF16), ((ROWS // 2, LANE), BF16), ((ROWS // 2, LANE), BF16))
FIELD = ((ROWS, LANE), F32)


def exchange(d1, d2, t1, t2):
    def along(axis, one, two):
        devices = lax.axis_size(axis)
        first = [(i, i ^ 1) for i in range(devices)]
        second = [(i, ((i + 1) ^ 1) - 1) for i in range(1, devices - 1)]
        two = lax.ppermute(two, axis, second)
        return lax.ppermute(one, axis, first), two

    t1, t2 = along("tile", t1, t2)
    d1, d2 = along("dom", d1, d2)
    return d1, d2, t1, t2


def member_groups(sizes, together):
    strides, total = [], 1
    for size in reversed(sizes):
        strides.insert(0, total)
        total *= size

    def numbers(axes):
        values = [0]
        for axis in axes:
            values = [v + i * strides[axis] for v in values for i in range(sizes[axis])]
        return values

    apart = [axis for axis in range(len(sizes)) if axis not in together]
    return [[base + v for v in numbers(together)] for base in numbers(apart)]


def reduce_all(packed):
    axes = ("dom", "tile")
    sizes = (4, 16, 2, 4)
    near = member_groups(sizes, (0, 2, 3))
    far = member_groups(sizes, (1,))

    def trade(array, groups):
        return lax.all_to_all(array, axes, 0, 0, axis_index_groups=groups, tiled=True)

    n, m = len(near[0]), len(far[0])
    mine = jnp.sum(trade(packed.reshape(n, -1, LANE), near), axis=0)
    mine = jnp.sum(trade(jnp.broadcast_to(mine[None], (m,) + mine.shape), far), axis=0)
    return trade(jnp.broadcast_to(mine[None], (n,) + mine.shape), near).reshape(packed.shape)


def shards(pumping, coupling, storage, tile_order, kriging):
    groups = lax.axis_size("dom")
    cell_total = storage.shape[0] * CB * groups * lax.axis_size("tile")
    scratch = lambda rows: pltpu.VMEM((rows, LANE), F32)
    p, sh, sl, u, *edges = call(
        first_kernel,
        (FIELD, ((FX * LANE, LANE), BF16), ((FX * LANE, LANE), BF16), FIELD) + EDGES,
        pltpu.with_memory_space_constraint(pumping, pltpu.HBM),
        pltpu.with_memory_space_constraint(coupling, pltpu.HBM),
        scratch=(
            pltpu.VMEM((16, RHS * CB), F32),
            pltpu.VMEM((16, CB * CB), F32),
            scratch(ROWS),
            scratch(ROWS),
            scratch(FX * LANE),
            pltpu.SemaphoreType.DMA((2, PIECES)),
        ),
        place=pltpu.HBM,
    )
    halo = exchange(*edges)
    ap, u, *edges = call(second_kernel, (FIELD, FIELD) + EDGES, p, u, sh, sl, storage, *halo)
    halo = exchange(*edges)
    (packed,) = call(
        third_kernel, (((2 * RHS, LANE), F32),), ap, u, sh, sl, storage, *halo, p
    )
    (cells,) = call(
        deal_kernel,
        (((FX * LANE, 4 * RHS), BF16),),
        *(tile_order, p, ap),
        scratch=(pltpu.VMEM((4 * RHS, FX * LANE), BF16),),
        flops=LONG,
    )
    packed = reduce_all(packed)
    heads, weights, later = call(
        solve_kernel,
        (((FX * LANE, LANE), BF16), ((2 * RHS, RHS), F32), ((RHS, LANE), F32)),
        *(packed, cells),
    )
    heads = lax.all_to_all(heads.reshape(groups, -1, LANE), "dom", 0, 0, tiled=True)
    (gram,) = call(
        lambda *refs: gram_kernel(cell_total, *refs),
        (((RHS, RHS), F32),),
        *(packed, weights, later),
        flops=LONG,
    )
    (sens,) = call(
        product_kernel,
        (((kriging.shape[0], RHS), F32),),
        *(kriging, heads.reshape(-1, LANE)),
    )
    return sens, gram


def solution(mesh):
    spec = P(("dom", "tile"), None)
    return jax.shard_map(
        shards, mesh=mesh, in_specs=(spec,) * 5, out_specs=(spec, P()), check_vma=False
    )
```

```python
import jax
import jax.numpy as jnp
from jax import lax
from jax.experimental import pallas as pl
from jax.experimental.pallas import tpu as pltpu
from jax.sharding import PartitionSpec as P

RHS = 64
CB = 64
FX = 8
LANE = 128
ROWS = FX * RHS
F32 = jnp.float32
BF16 = jnp.bfloat16
HIGHEST = lax.Precision.HIGHEST
PARAMS = pltpu.CompilerParams(vmem_limit_bytes=40 * 1024 * 1024)
PIECES = 4
WIDTH = RHS * CB // PIECES
LONG = 10**11
NN = (((1,), (0,)), ((), ()))
NT = (((1,), (1,)), ((), ()))


def split(value):
    high = value.astype(BF16)
    return high, (value - high.astype(F32)).astype(BF16)


def dot(left, right, dims):
    return lax.dot_general(left, right, dims, preferred_element_type=F32)


def dot3(left, right, dims):
    (lh, ll), (rh, rl) = left, right
    return dot(lh, rh, dims) + (dot(ll, rh, dims) + dot(lh, rl, dims))


def exact(left, right, dims=NN):
    return lax.dot_general(left, right, dims, precision=HIGHEST, preferred_element_type=F32)


def low_lanes(rows):
    return lax.broadcasted_iota(jnp.int32, (rows, LANE), 1) < CB


def swap(value):
    return pltpu.roll(value, CB, 1)


def part(x):
    return pl.ds(x * RHS, RHS)


def is_even(axis):
    return lax.rem(lax.axis_index(axis), 2) == 0


def by_parity(axis, first, second):
    even = is_even(axis)
    return jnp.where(even, first, second), jnp.where(even, second, first)


def write_edges(spread, d1, d2, t1, t2):
    low = low_lanes(RHS)
    one, two = by_parity("dom", spread[FX - 1], spread[0])
    d1[...] = one.astype(BF16)
    d2[:RHS, :] = two.astype(BF16)
    d2[RHS:, :] = jnp.zeros((d2.shape[0] - RHS, LANE), BF16)
    for i in range(FX // 2):
        even, odd = spread[2 * i], spread[2 * i + 1]
        left = jnp.where(low, even, swap(odd))
        right = jnp.where(low, swap(even), odd)
        one, two = by_parity("tile", right, left)
        t1[part(i), :] = one.astype(BF16)
        t2[part(i), :] = two.astype(BF16)


def first_kernel(pump_hbm, coup_hbm, p_out, sh_out, sl_out, u_out, d1, d2, t1, t2, pump, coup, rows_p, rows_s, mats, arrived):
    copies = []
    for i in range(PIECES):
        columns = pl.ds(i * WIDTH, WIDTH)
        for j, (source, target) in enumerate(((coup_hbm, coup), (pump_hbm, pump))):
            copies.append(
                pltpu.make_async_copy(source.at[:, columns], target.at[:, columns], arrived.at[j, i])
            )
    for copy in copies:
        copy.start()
    for copy in copies:
        copy.wait()
    for k in range(RHS // 2):
        chunk = slice(k * LANE, (k + 1) * LANE)
        rows_p[pl.ds(k, 16, stride=32), :] = pump[:, chunk]
        rows_s[pl.ds(k, 16, stride=32), :] = coup[:, chunk]
    low = low_lanes(32)
    zero = jnp.zeros((32, LANE), F32)
    for x in range(FX):
        a0, a1 = rows_p[pl.ds(x * 64, 32), :], rows_p[pl.ds(x * 64 + 32, 32), :]
        p_out[pl.ds(x * 64, 32, stride=2), :] = jnp.where(low, a0, swap(a1))
        p_out[pl.ds(x * 64 + 1, 32, stride=2), :] = jnp.where(low, swap(a0), a1)
        s0, s1 = rows_s[pl.ds(x * 64, 32), :], rows_s[pl.ds(x * 64 + 32, 32), :]
        mats[pl.ds(x * 128, 32, stride=2), :] = jnp.where(low, s0, zero)
        mats[pl.ds(x * 128 + 1, 32, stride=2), :] = jnp.where(low, swap(s0), zero)
        mats[pl.ds(x * 128 + 64, 32, stride=2), :] = jnp.where(low, zero, swap(s1))
        mats[pl.ds(x * 128 + 65, 32, stride=2), :] = jnp.where(low, zero, s1)
    spread = []
    for x in range(FX):
        block = pl.ds(x * LANE, LANE)
        high, rest = split(mats[block, :])
        sh_out[block, :] = high
        sl_out[block, :] = rest
        u = dot3(split(p_out[part(x), :]), (high, rest), NN)
        u_out[part(x), :] = u
        spread.append(u)
    write_edges(spread, d1, d2, t1, t2)


def operator(v, u, sh, sl, stor, d1, d2, t1, t2):
    low = low_lanes(RHS)
    spread = [u[part(x), :] for x in range(FX)]
    after, before = by_parity("dom", d1[...].astype(F32), d2[:RHS, :].astype(F32))
    ends = [before] + spread + [after]
    right, left = [], []
    for i in range(FX // 2):
        one, two = by_parity("tile", t1[part(i), :].astype(F32), t2[part(i), :].astype(F32))
        right.append(one)
        left.append(two)
    applied = []
    for x in range(FX):
        from_left, from_right = left[x // 2], right[x // 2]
        if x % 2 == 0:
            outside = jnp.where(low, from_left, swap(from_right))
        else:
            outside = jnp.where(low, swap(from_left), from_right)
        pulled = 4.0 * spread[x] - (ends[x] + ends[x + 2] + swap(spread[x]) + outside)
        block = pl.ds(x * LANE, LANE)
        capacity = jnp.concatenate([stor[2 * x : 2 * x + 1, :], stor[2 * x + 1 : 2 * x + 2, :]], axis=1)
        applied.append(
            capacity * v[part(x), :] + dot3(split(pulled), (sh[block, :], sl[block, :]), NT)
        )
    return applied


def second_kernel(v, u, sh, sl, stor, d1, d2, t1, t2, ap_out, u_out, *edges):
    applied = operator(v, u, sh, sl, stor, d1, d2, t1, t2)
    spread = []
    for x in range(FX):
        ap_out[part(x), :] = applied[x]
        block = pl.ds(x * LANE, LANE)
        s = dot3(split(applied[x]), (sh[block, :], sl[block, :]), NN)
        u_out[part(x), :] = s
        spread.append(s)
    write_edges(spread, *edges)


def deal_kernel(order, v, ap, cells, table):
    for x in range(FX):
        high, rest = split(jnp.concatenate([v[part(x), :], ap[part(x), :]], axis=0))
        table[: 2 * RHS, x * LANE : (x + 1) * LANE] = high
        table[2 * RHS :, x * LANE : (x + 1) * LANE] = rest
    lane = lax.broadcasted_iota(jnp.int32, (LANE, LANE), 1)
    for g in range(FX):
        row = jnp.broadcast_to(order[:, g * LANE : (g + 1) * LANE], (LANE, LANE))
        wanted = jnp.transpose(row)
        picks = [
            jnp.where(wanted == lane + l * LANE, 1.0, 0.0).astype(BF16) for l in range(FX)
        ]
        cells[pl.ds(g * LANE, LANE), :] = dot(
            jnp.concatenate(picks, axis=1), table[...], NT
        ).astype(BF16)


def third_kernel(v, u, sh, sl, stor, d1, d2, t1, t2, p, packed):
    applied = operator(v, u, sh, sl, stor, d1, d2, t1, t2)
    base = jnp.zeros((2 * RHS, 2 * RHS), F32)
    total = jnp.zeros((2 * RHS, RHS), F32)
    for x in range(FX):
        low, image = split(jnp.concatenate([p[part(x), :], v[part(x), :]], axis=0)), split(applied[x])
        base += dot3(low, low, NT)
        both = [jnp.concatenate([a[RHS:], b], axis=0) for a, b in zip(low, image)]
        total += dot3(both, image, NT)
    m0 = symmetric(base[:RHS, :RHS])
    m1 = 0.5 * (base[:RHS, RHS:] + base[RHS:, :RHS])
    m2 = symmetric(base[RHS:, RHS:])
    m3 = symmetric(total[:RHS])
    m4 = symmetric(total[RHS:])
    row, column = square_index()
    upper = row <= column
    packed[:RHS, :] = jnp.concatenate([jnp.where(upper, m0, m2), jnp.where(upper, m1, m3)], axis=1)
    ends = jnp.where(row == 0, diagonal(m2), jnp.where(row == 1, diagonal(m3), 0.0))
    packed[RHS:, :] = jnp.concatenate([m4, ends], axis=1)


def square_index():
    return [lax.broadcasted_iota(jnp.int32, (RHS, RHS), d) for d in (0, 1)]


def diagonal(matrix):
    row, column = square_index()
    return jnp.sum(jnp.where(row == column, matrix, 0.0), axis=0, keepdims=True)


def column_diagonal(matrix):
    row, column = square_index()
    return jnp.sum(jnp.where(row == column, matrix, 0.0), axis=1, keepdims=True)


def unpack_pair(matrix, ends):
    row, column = square_index()
    turned = jnp.transpose(matrix)
    first = jnp.where(row <= column, matrix, turned)
    second = jnp.where(row > column, matrix, jnp.where(row < column, turned, ends))
    return first, second


def eliminate(joined, panel=8):
    order, width = joined.shape
    parts = [joined[g : g + panel, :] for g in range(0, order, panel)]
    index = lax.broadcasted_iota(jnp.int32, (panel, width), 0)

    def wide(value):
        pieces = [value] * (width // LANE)
        if width % LANE:
            pieces.append(value[:, : width % LANE])
        return jnp.concatenate(pieces, axis=1) if len(pieces) > 1 else value

    def apply(rows, at, c0, c1, inverse, where):
        r0, r1 = rows[at : at + 1, :], rows[at + 1 : at + 2, :]
        s0 = inverse[0] * r0 + inverse[1] * r1
        s1 = inverse[2] * r0 + inverse[3] * r1
        rest = rows - (c0 * s0 + c1 * s1)
        return jnp.where(where == at, s0, jnp.where(where == at + 1, s1, rest))

    for g in range(len(parts)):
        rows = parts[g]
        first = g * panel
        columns = [
            jnp.broadcast_to(rows[:, first + q : first + q + 1], (panel, LANE)) for q in range(panel)
        ]
        for at in range(0, panel, 2):
            c0, c1 = columns[at], columns[at + 1]
            a, c = c0[at : at + 1, :], c0[at + 1 : at + 2, :]
            b, d = c1[at : at + 1, :], c1[at + 1 : at + 2, :]
            scale = 1.0 / (a * d - b * c)
            inverse = (d * scale, -b * scale, -c * scale, a * scale)
            for q in range(at + 2, panel):
                columns[q] = apply(columns[q], at, c0, c1, inverse, index[:, :LANE])
            rows = apply(rows, at, wide(c0), wide(c1), [wide(v) for v in inverse], index)
        parts[g] = rows
        for h in range(len(parts)):
            if h != g:
                taken = None
                for q in range(panel):
                    column = jnp.broadcast_to(parts[h][:, first + q : first + q + 1], (panel, width))
                    term = column * rows[q : q + 1, :]
                    taken = term if taken is None else taken + term
                parts[h] = parts[h] - taken
    return jnp.concatenate(parts, axis=0)[:, order:]


def symmetric(matrix):
    return 0.5 * (matrix + jnp.transpose(matrix))


def solve_kernel(cell_total, packed, cells, heads, scale, weights, later, rows):
    m0, m2 = unpack_pair(packed[:RHS, :RHS], packed[RHS : RHS + 1, RHS:])
    m1, m3 = unpack_pair(packed[:RHS, RHS:], packed[RHS + 1 : RHS + 2, RHS:])
    first = eliminate(jnp.concatenate([m1, m0, m2], axis=1))
    alpha, shift = first[:, :RHS], first[:, RHS:]
    curved = symmetric(m3 - exact(m2, shift))
    target = m1 - exact(m2, alpha)
    gamma = eliminate(jnp.concatenate([curved, target], axis=1))
    mixed = alpha - exact(shift, gamma)
    both = jnp.concatenate([mixed, gamma], axis=0)
    spread = jnp.concatenate([column_diagonal(m0), column_diagonal(m2)], axis=0)
    bound = jnp.sum(jnp.abs(both) * jnp.sqrt(spread * (1.0 / cell_total)), axis=0, keepdims=True)
    bound = jnp.where(bound > 0.0, bound, 1.0)
    scale[...] = bound
    high, rest = split(jnp.concatenate([both / bound, both / bound], axis=1))
    value = dot3((cells[:, :LANE], cells[:, LANE:]), (high, rest), NN)
    rows[...] = value
    half = FX * LANE // 2
    even, odd = rows[pl.ds(0, half, stride=2), :], rows[pl.ds(1, half, stride=2), :]
    heads[...] = jnp.where(low_lanes(half), even, odd)
    weights[...] = both
    later[...] = jnp.concatenate([m2, m3], axis=1)


def gram_kernel(cell_total, packed, weights, later, gram):
    mixed, gamma = weights[:RHS, :], weights[RHS:, :]
    rest = exact(packed[RHS:, :RHS], gamma) + exact(later[:, RHS:], mixed) - later[:, :RHS]
    gram[...] = symmetric(exact(jnp.transpose(gamma), rest)) * (1.0 / cell_total)


def product_kernel(kriging, arrived, scale, sens, rows):
    half = FX * LANE // 2
    value = arrived[...].astype(F32)
    rows[pl.ds(0, half, stride=2), :] = value
    rows[pl.ds(1, half, stride=2), :] = swap(value)
    high, rest = split(rows[...])
    sens[...] = (dot(kriging[...], high, NN) + dot(kriging[...], rest, NN))[:, :RHS] * scale[...]


def call(kernel, shapes, *operands, scratch=(), flops=1000000, place=pltpu.VMEM):
    return pl.pallas_call(
        kernel,
        out_shape=[jax.ShapeDtypeStruct(shape, kind) for shape, kind in shapes],
        in_specs=[pl.BlockSpec(memory_space=place)] * len(operands),
        out_specs=[pl.BlockSpec(memory_space=pltpu.VMEM)] * len(shapes),
        scratch_shapes=list(scratch),
        compiler_params=PARAMS,
        cost_estimate=pl.CostEstimate(flops=flops, bytes_accessed=1 << 20, transcendentals=0),
    )(*operands)


EDGES = (((RHS, LANE), BF16), ((ROWS // 2 + 16, LANE), BF16), ((ROWS // 2, LANE), BF16), ((ROWS // 2, LANE), BF16))
FIELD = ((ROWS, LANE), F32)


def exchange(d1, d2, t1, t2):
    def along(axis, one, two):
        devices = lax.axis_size(axis)
        first = [(i, i ^ 1) for i in range(devices)]
        second = [(i, ((i + 1) ^ 1) - 1) for i in range(1, devices - 1)]
        two = lax.ppermute(two, axis, second)
        return lax.ppermute(one, axis, first), two

    t1, t2 = along("tile", t1, t2)
    d1, d2 = along("dom", d1, d2)
    return d1, d2, t1, t2


def member_groups(sizes, together):
    strides, total = [], 1
    for size in reversed(sizes):
        strides.insert(0, total)
        total *= size

    def numbers(axes):
        values = [0]
        for axis in axes:
            values = [v + i * strides[axis] for v in values for i in range(sizes[axis])]
        return values

    apart = [axis for axis in range(len(sizes)) if axis not in together]
    return [[base + v for v in numbers(together)] for base in numbers(apart)]


def reduce_all(packed):
    axes = ("dom", "tile")
    sizes = (4, 16, 2, 4)
    near = member_groups(sizes, (0, 2, 3))
    far = member_groups(sizes, (1,))

    def trade(array, groups):
        return lax.all_to_all(array, axes, 0, 0, axis_index_groups=groups, tiled=True)

    n, m = len(near[0]), len(far[0])
    mine = jnp.sum(trade(packed.reshape(n, -1, LANE), near), axis=0)
    mine = jnp.sum(trade(jnp.broadcast_to(mine[None], (m,) + mine.shape), far), axis=0)
    return trade(jnp.broadcast_to(mine[None], (n,) + mine.shape), near).reshape(packed.shape)


def shards(pumping, coupling, storage, tile_order, kriging):
    groups = lax.axis_size("dom")
    cell_total = storage.shape[0] * CB * groups * lax.axis_size("tile")
    scratch = lambda rows: pltpu.VMEM((rows, LANE), F32)
    p, sh, sl, u, *edges = call(
        first_kernel,
        (FIELD, ((FX * LANE, LANE), BF16), ((FX * LANE, LANE), BF16), FIELD) + EDGES,
        pltpu.with_memory_space_constraint(pumping, pltpu.HBM),
        pltpu.with_memory_space_constraint(coupling, pltpu.HBM),
        scratch=(
            pltpu.VMEM((16, RHS * CB), F32),
            pltpu.VMEM((16, CB * CB), F32),
            scratch(ROWS),
            scratch(ROWS),
            scratch(FX * LANE),
            pltpu.SemaphoreType.DMA((2, PIECES)),
        ),
        place=pltpu.HBM,
    )
    halo = exchange(*edges)
    ap, u, *edges = call(second_kernel, (FIELD, FIELD) + EDGES, p, u, sh, sl, storage, *halo)
    halo = exchange(*edges)
    (packed,) = call(
        third_kernel, (((2 * RHS, LANE), F32),), ap, u, sh, sl, storage, *halo, p
    )
    (cells,) = call(
        deal_kernel,
        (((FX * LANE, 4 * RHS), BF16),),
        *(tile_order, p, ap),
        scratch=(pltpu.VMEM((4 * RHS, FX * LANE), BF16),),
        flops=LONG,
    )
    packed = reduce_all(packed)
    heads, scale, weights, later = call(
        lambda *refs: solve_kernel(cell_total, *refs),
        (((FX * LANE // 2, LANE), F32), ((1, RHS), F32), ((2 * RHS, RHS), F32), ((RHS, LANE), F32)),
        *(packed, cells),
        scratch=(scratch(FX * LANE),),
    )
    heads = heads.astype(jnp.float16).reshape(groups, -1, LANE)
    heads = lax.all_to_all(heads, "dom", 0, 0, tiled=True).reshape(-1, LANE).astype(F32)
    (gram,) = call(
        lambda *refs: gram_kernel(cell_total, *refs),
        (((RHS, RHS), F32),),
        *(packed, weights, later),
        flops=LONG,
    )
    (sens,) = call(
        product_kernel,
        (((kriging.shape[0], RHS), F32),),
        *(kriging, heads, scale),
        scratch=(scratch(FX * LANE),),
    )
    return sens, gram


def solution(mesh):
    spec = P(("dom", "tile"), None)
    return jax.shard_map(
        shards, mesh=mesh, in_specs=(spec,) * 5, out_specs=(spec, P()), check_vma=False
    )
```

```python
import jax
import jax.numpy as jnp
from jax import lax
from jax.experimental import pallas as pl
from jax.experimental.pallas import tpu as pltpu
from jax.sharding import PartitionSpec as P

RHS = 64
CB = 64
FX = 8
LANE = 128
ROWS = FX * RHS
F32 = jnp.float32
BF16 = jnp.bfloat16
HIGHEST = lax.Precision.HIGHEST
PARAMS = pltpu.CompilerParams(vmem_limit_bytes=40 * 1024 * 1024)
PIECES = 4
WIDTH = RHS * CB // PIECES
LONG = 10**11
NN = (((1,), (0,)), ((), ()))
NT = (((1,), (1,)), ((), ()))


def split(value):
    high = value.astype(BF16)
    return high, (value - high.astype(F32)).astype(BF16)


def dot(left, right, dims):
    return lax.dot_general(left, right, dims, preferred_element_type=F32)


def dot3(left, right, dims):
    (lh, ll), (rh, rl) = left, right
    return dot(lh, rh, dims) + (dot(ll, rh, dims) + dot(lh, rl, dims))


def exact(left, right, dims=NN):
    return lax.dot_general(left, right, dims, precision=HIGHEST, preferred_element_type=F32)


def low_lanes(rows):
    return lax.broadcasted_iota(jnp.int32, (rows, LANE), 1) < CB


def swap(value):
    return pltpu.roll(value, CB, 1)


def part(x):
    return pl.ds(x * RHS, RHS)


def is_even(axis):
    return lax.rem(lax.axis_index(axis), 2) == 0


def by_parity(axis, first, second):
    even = is_even(axis)
    return jnp.where(even, first, second), jnp.where(even, second, first)


def write_edges(spread, d1, d2, t1, t2):
    low = low_lanes(RHS)
    one, two = by_parity("dom", spread[FX - 1], spread[0])
    d1[...] = one.astype(BF16)
    d2[:RHS, :] = two.astype(BF16)
    d2[RHS:, :] = jnp.zeros((d2.shape[0] - RHS, LANE), BF16)
    for i in range(FX // 2):
        even, odd = spread[2 * i], spread[2 * i + 1]
        left = jnp.where(low, even, swap(odd))
        right = jnp.where(low, swap(even), odd)
        one, two = by_parity("tile", right, left)
        t1[part(i), :] = one.astype(BF16)
        t2[part(i), :] = two.astype(BF16)


def first_kernel(pump_hbm, coup_hbm, p_out, sh_out, sl_out, u_out, d1, d2, t1, t2, pump, coup, rows_p, rows_s, mats, arrived):
    copies = []
    for source, target, order in ((pump_hbm, pump, 0), (coup_hbm, coup, 1)):
        for i in range(PIECES):
            columns = pl.ds(i * WIDTH, WIDTH)
            copies.append(
                pltpu.make_async_copy(source.at[:, columns], target.at[:, columns], arrived.at[order, i])
            )
            copies[-1].start()
    for i, copy in enumerate(copies):
        source, target = (pump, rows_p) if i < PIECES else (coup, rows_s)
        copy.wait()
        chunks = WIDTH // LANE
        for k in range(i % PIECES * chunks, (i % PIECES + 1) * chunks):
            target[pl.ds(k, 16, stride=32), :] = source[:, k * LANE : (k + 1) * LANE]
    low = low_lanes(32)
    zero = jnp.zeros((32, LANE), F32)
    for x in range(FX):
        a0, a1 = rows_p[pl.ds(x * 64, 32), :], rows_p[pl.ds(x * 64 + 32, 32), :]
        p_out[pl.ds(x * 64, 32, stride=2), :] = jnp.where(low, a0, swap(a1))
        p_out[pl.ds(x * 64 + 1, 32, stride=2), :] = jnp.where(low, swap(a0), a1)
        s0, s1 = rows_s[pl.ds(x * 64, 32), :], rows_s[pl.ds(x * 64 + 32, 32), :]
        mats[pl.ds(x * 128, 32, stride=2), :] = jnp.where(low, s0, zero)
        mats[pl.ds(x * 128 + 1, 32, stride=2), :] = jnp.where(low, swap(s0), zero)
        mats[pl.ds(x * 128 + 64, 32, stride=2), :] = jnp.where(low, zero, swap(s1))
        mats[pl.ds(x * 128 + 65, 32, stride=2), :] = jnp.where(low, zero, s1)
    spread = []
    for x in range(FX):
        block = pl.ds(x * LANE, LANE)
        high, rest = split(mats[block, :])
        sh_out[block, :] = high
        sl_out[block, :] = rest
        u = dot3(split(p_out[part(x), :]), (high, rest), NN)
        u_out[part(x), :] = u
        spread.append(u)
    write_edges(spread, d1, d2, t1, t2)


def operator(v, u, sh, sl, stor, d1, d2, t1, t2):
    low = low_lanes(RHS)
    spread = [u[part(x), :] for x in range(FX)]
    after, before = by_parity("dom", d1[...].astype(F32), d2[:RHS, :].astype(F32))
    ends = [before] + spread + [after]
    right, left = [], []
    for i in range(FX // 2):
        one, two = by_parity("tile", t1[part(i), :].astype(F32), t2[part(i), :].astype(F32))
        right.append(one)
        left.append(two)
    applied = []
    for x in range(FX):
        from_left, from_right = left[x // 2], right[x // 2]
        if x % 2 == 0:
            outside = jnp.where(low, from_left, swap(from_right))
        else:
            outside = jnp.where(low, swap(from_left), from_right)
        pulled = 4.0 * spread[x] - (ends[x] + ends[x + 2] + swap(spread[x]) + outside)
        block = pl.ds(x * LANE, LANE)
        capacity = jnp.concatenate([stor[2 * x : 2 * x + 1, :], stor[2 * x + 1 : 2 * x + 2, :]], axis=1)
        applied.append(
            capacity * v[part(x), :] + dot3(split(pulled), (sh[block, :], sl[block, :]), NT)
        )
    return applied


def second_kernel(v, u, sh, sl, stor, d1, d2, t1, t2, ap_out, u_out, *edges):
    applied = operator(v, u, sh, sl, stor, d1, d2, t1, t2)
    spread = []
    for x in range(FX):
        ap_out[part(x), :] = applied[x]
        block = pl.ds(x * LANE, LANE)
        s = dot3(split(applied[x]), (sh[block, :], sl[block, :]), NN)
        u_out[part(x), :] = s
        spread.append(s)
    write_edges(spread, *edges)


def deal_kernel(order, v, ap, cells, table):
    for x in range(FX):
        high, rest = split(jnp.concatenate([v[part(x), :], ap[part(x), :]], axis=0))
        table[: 2 * RHS, x * LANE : (x + 1) * LANE] = high
        table[2 * RHS :, x * LANE : (x + 1) * LANE] = rest
    lane = lax.broadcasted_iota(jnp.int32, (LANE, LANE), 1)
    for g in range(FX):
        row = jnp.broadcast_to(order[:, g * LANE : (g + 1) * LANE], (LANE, LANE))
        wanted = jnp.transpose(row)
        picks = [
            jnp.where(wanted == lane + l * LANE, 1.0, 0.0).astype(BF16) for l in range(FX)
        ]
        cells[pl.ds(g * LANE, LANE), :] = dot(
            jnp.concatenate(picks, axis=1), table[...], NT
        ).astype(BF16)


def base_kernel(p, v, base):
    total = jnp.zeros((2 * RHS, 2 * RHS), F32)
    for x in range(FX):
        both = split(jnp.concatenate([p[part(x), :], v[part(x), :]], axis=0))
        total += dot3(both, both, NT)
    base[...] = total


def third_kernel(v, u, sh, sl, stor, d1, d2, t1, t2, base, packed):
    applied = operator(v, u, sh, sl, stor, d1, d2, t1, t2)
    total = jnp.zeros((2 * RHS, RHS), F32)
    for x in range(FX):
        image = split(applied[x])
        both = [jnp.concatenate([a, b], axis=0) for a, b in zip(split(v[part(x), :]), image)]
        total += dot3(both, image, NT)
    m0, m1, m2 = base[:RHS, :RHS], base[:RHS, RHS:], base[RHS:, RHS:]
    m1 = symmetric(m1)
    m3 = symmetric(total[:RHS])
    m4 = total[RHS:]
    row, column = square_index()
    upper = row <= column
    packed[:RHS, :] = jnp.concatenate([jnp.where(upper, m0, m2), jnp.where(upper, m1, m3)], axis=1)
    ends = jnp.where(row == 0, diagonal(m2), jnp.where(row == 1, diagonal(m3), 0.0))
    packed[RHS:, :] = jnp.concatenate([m4, ends], axis=1)


def square_index():
    return [lax.broadcasted_iota(jnp.int32, (RHS, RHS), d) for d in (0, 1)]


def diagonal(matrix):
    row, column = square_index()
    return jnp.sum(jnp.where(row == column, matrix, 0.0), axis=0, keepdims=True)


def column_diagonal(matrix):
    row, column = square_index()
    return jnp.sum(jnp.where(row == column, matrix, 0.0), axis=1, keepdims=True)


def unpack_pair(matrix, ends):
    row, column = square_index()
    turned = jnp.transpose(matrix)
    first = jnp.where(row <= column, matrix, turned)
    second = jnp.where(row > column, matrix, jnp.where(row < column, turned, ends))
    return first, second


def eliminate(joined, panel=8):
    order, width = joined.shape
    parts = [joined[g : g + panel, :] for g in range(0, order, panel)]
    index = lax.broadcasted_iota(jnp.int32, (panel, width), 0)

    def wide(value):
        pieces = [value] * (width // LANE)
        if width % LANE:
            pieces.append(value[:, : width % LANE])
        return jnp.concatenate(pieces, axis=1) if len(pieces) > 1 else value

    def apply(rows, at, c0, c1, inverse, where):
        r0, r1 = rows[at : at + 1, :], rows[at + 1 : at + 2, :]
        s0 = inverse[0] * r0 + inverse[1] * r1
        s1 = inverse[2] * r0 + inverse[3] * r1
        rest = rows - (c0 * s0 + c1 * s1)
        return jnp.where(where == at, s0, jnp.where(where == at + 1, s1, rest))

    for g in range(len(parts)):
        rows = parts[g]
        first = g * panel
        columns = [
            jnp.broadcast_to(rows[:, first + q : first + q + 1], (panel, LANE)) for q in range(panel)
        ]
        for at in range(0, panel, 2):
            c0, c1 = columns[at], columns[at + 1]
            a, c = c0[at : at + 1, :], c0[at + 1 : at + 2, :]
            b, d = c1[at : at + 1, :], c1[at + 1 : at + 2, :]
            scale = 1.0 / (a * d - b * c)
            inverse = (d * scale, -b * scale, -c * scale, a * scale)
            for q in range(at + 2, panel):
                columns[q] = apply(columns[q], at, c0, c1, inverse, index[:, :LANE])
            rows = apply(rows, at, wide(c0), wide(c1), [wide(v) for v in inverse], index)
        parts[g] = rows
        for h in range(len(parts)):
            if h != g:
                taken = None
                for q in range(panel):
                    column = jnp.broadcast_to(parts[h][:, first + q : first + q + 1], (panel, width))
                    term = column * rows[q : q + 1, :]
                    taken = term if taken is None else taken + term
                parts[h] = parts[h] - taken
    return jnp.concatenate(parts, axis=0)[:, order:]


def symmetric(matrix):
    return 0.5 * (matrix + jnp.transpose(matrix))


def solve_kernel(cell_total, packed, cells, heads, scale, weights, later, rows):
    m0, m2 = unpack_pair(packed[:RHS, :RHS], packed[RHS : RHS + 1, RHS:])
    m1, m3 = unpack_pair(packed[:RHS, RHS:], packed[RHS + 1 : RHS + 2, RHS:])
    first = eliminate(jnp.concatenate([m1, m0, m2], axis=1))
    alpha, shift = first[:, :RHS], first[:, RHS:]
    curved = symmetric(m3 - exact(m2, shift))
    target = m1 - exact(m2, alpha)
    gamma = eliminate(jnp.concatenate([curved, target], axis=1))
    mixed = alpha - exact(shift, gamma)
    both = jnp.concatenate([mixed, gamma], axis=0)
    spread = jnp.concatenate([column_diagonal(m0), column_diagonal(m2)], axis=0)
    bound = jnp.sum(jnp.abs(both) * jnp.sqrt(spread * (1.0 / cell_total)), axis=0, keepdims=True)
    bound = jnp.where(bound > 0.0, bound, 1.0)
    scale[...] = bound
    high, rest = split(jnp.concatenate([both / bound, both / bound], axis=1))
    value = dot3((cells[:, :LANE], cells[:, LANE:]), (high, rest), NN)
    rows[...] = value
    half = FX * LANE // 2
    even, odd = rows[pl.ds(0, half, stride=2), :], rows[pl.ds(1, half, stride=2), :]
    heads[...] = jnp.where(low_lanes(half), even, odd)
    weights[...] = both
    later[...] = jnp.concatenate([m2, m3], axis=1)


def gram_kernel(cell_total, packed, weights, later, kriging, gram, kept):
    kept[...] = kriging[...]
    mixed, gamma = weights[:RHS, :], weights[RHS:, :]
    rest = exact(packed[RHS:, :RHS], gamma) + exact(later[:, RHS:], mixed) - later[:, :RHS]
    gram[...] = symmetric(exact(jnp.transpose(gamma), rest)) * (1.0 / cell_total)


def product_kernel(kriging, arrived, scale, sens, rows):
    half = FX * LANE // 2
    value = arrived[...].astype(F32)
    rows[pl.ds(0, half, stride=2), :] = value
    rows[pl.ds(1, half, stride=2), :] = swap(value)
    high, rest = split(rows[...])
    sens[...] = (dot(kriging[...], high, NN) + dot(kriging[...], rest, NN))[:, :RHS] * scale[...]


def call(kernel, shapes, *operands, scratch=(), flops=1000000, place=pltpu.VMEM):
    return pl.pallas_call(
        kernel,
        out_shape=[jax.ShapeDtypeStruct(shape, kind) for shape, kind in shapes],
        in_specs=[pl.BlockSpec(memory_space=place)] * len(operands),
        out_specs=[pl.BlockSpec(memory_space=pltpu.VMEM)] * len(shapes),
        scratch_shapes=list(scratch),
        compiler_params=PARAMS,
        cost_estimate=pl.CostEstimate(flops=flops, bytes_accessed=1 << 20, transcendentals=0),
    )(*operands)


EDGES = (((RHS, LANE), BF16), ((ROWS // 2 + 16, LANE), BF16), ((ROWS // 2, LANE), BF16), ((ROWS // 2, LANE), BF16))
FIELD = ((ROWS, LANE), F32)


def exchange(d1, d2, t1, t2):
    def along(axis, one, two):
        devices = lax.axis_size(axis)
        first = [(i, i ^ 1) for i in range(devices)]
        second = [(i, ((i + 1) ^ 1) - 1) for i in range(1, devices - 1)]
        two = lax.ppermute(two, axis, second)
        return lax.ppermute(one, axis, first), two

    t1, t2 = along("tile", t1, t2)
    d1, d2 = along("dom", d1, d2)
    return d1, d2, t1, t2


def member_groups(sizes, together):
    strides, total = [], 1
    for size in reversed(sizes):
        strides.insert(0, total)
        total *= size

    def numbers(axes):
        values = [0]
        for axis in axes:
            values = [v + i * strides[axis] for v in values for i in range(sizes[axis])]
        return values

    apart = [axis for axis in range(len(sizes)) if axis not in together]
    return [[base + v for v in numbers(together)] for base in numbers(apart)]


def reduce_all(packed):
    axes = ("dom", "tile")
    sizes = (4, 16, 2, 4)
    near = member_groups(sizes, (0, 2, 3))
    far = member_groups(sizes, (1,))

    def trade(array, groups):
        return lax.all_to_all(array, axes, 0, 0, axis_index_groups=groups, tiled=True)

    n, m = len(near[0]), len(far[0])
    mine = jnp.sum(trade(packed.reshape(n, -1, LANE), near), axis=0)
    mine = jnp.sum(trade(jnp.broadcast_to(mine[None], (m,) + mine.shape), far), axis=0)
    return trade(jnp.broadcast_to(mine[None], (n,) + mine.shape), near).reshape(packed.shape)


def shards(pumping, coupling, storage, tile_order, kriging):
    groups = lax.axis_size("dom")
    cell_total = storage.shape[0] * CB * groups * lax.axis_size("tile")
    scratch = lambda rows: pltpu.VMEM((rows, LANE), F32)
    p, sh, sl, u, *edges = call(
        first_kernel,
        (FIELD, ((FX * LANE, LANE), BF16), ((FX * LANE, LANE), BF16), FIELD) + EDGES,
        pltpu.with_memory_space_constraint(pumping, pltpu.HBM),
        pltpu.with_memory_space_constraint(coupling, pltpu.HBM),
        scratch=(
            pltpu.VMEM((16, RHS * CB), F32),
            pltpu.VMEM((16, CB * CB), F32),
            scratch(ROWS),
            scratch(ROWS),
            scratch(FX * LANE),
            pltpu.SemaphoreType.DMA((2, PIECES)),
        ),
        place=pltpu.HBM,
    )
    halo = exchange(*edges)
    ap, u, *edges = call(second_kernel, (FIELD, FIELD) + EDGES, p, u, sh, sl, storage, *halo)
    halo = exchange(*edges)
    (base,) = call(base_kernel, (((2 * RHS, LANE), F32),), p, ap)
    (packed,) = call(
        third_kernel, (((2 * RHS, LANE), F32),), ap, u, sh, sl, storage, *halo, base
    )
    (cells,) = call(
        deal_kernel,
        (((FX * LANE, 4 * RHS), BF16),),
        *(tile_order, p, ap),
        scratch=(pltpu.VMEM((4 * RHS, FX * LANE), BF16),),
        flops=LONG,
    )
    packed = reduce_all(packed)
    heads, scale, weights, later = call(
        lambda *refs: solve_kernel(cell_total, *refs),
        (((FX * LANE // 2, LANE), F32), ((1, RHS), F32), ((2 * RHS, RHS), F32), ((RHS, LANE), F32)),
        *(packed, cells),
        scratch=(scratch(FX * LANE),),
    )
    heads = heads.astype(jnp.float16).reshape(groups, -1, LANE)
    heads = lax.all_to_all(heads, "dom", 0, 0, tiled=True).reshape(-1, LANE).astype(F32)
    gram, kriging = call(
        lambda *refs: gram_kernel(cell_total, *refs),
        (((RHS, RHS), F32), (kriging.shape, BF16)),
        *(packed, weights, later, kriging),
        flops=LONG,
    )
    (sens,) = call(
        product_kernel,
        (((kriging.shape[0], RHS), F32),),
        *(kriging, heads, scale),
        scratch=(scratch(FX * LANE),),
    )
    return sens, gram


def solution(mesh):
    spec = P(("dom", "tile"), None)
    return jax.shard_map(
        shards, mesh=mesh, in_specs=(spec,) * 5, out_specs=(spec, P()), check_vma=False
    )
```

```python
import jax
import jax.numpy as jnp
from jax import lax
from jax.experimental import pallas as pl
from jax.experimental.pallas import tpu as pltpu
from jax.sharding import PartitionSpec as P

RHS = 64
CB = 64
FX = 8
N_TILE = 4
LANE = 128
ROWS = FX * RHS
F32 = jnp.float32
BF16 = jnp.bfloat16
HIGHEST = lax.Precision.HIGHEST
PARAMS = pltpu.CompilerParams(vmem_limit_bytes=40 * 1024 * 1024)
PIECES = 4
WIDTH = RHS * CB // PIECES
LONG = 10**11
NN = (((1,), (0,)), ((), ()))
NT = (((1,), (1,)), ((), ()))


def split(value):
    high = value.astype(BF16)
    return high, (value - high.astype(F32)).astype(BF16)


def dot(left, right, dims):
    return lax.dot_general(left, right, dims, preferred_element_type=F32)


def dot3(left, right, dims):
    (lh, ll), (rh, rl) = left, right
    return dot(lh, rh, dims) + (dot(ll, rh, dims) + dot(lh, rl, dims))


def exact(left, right, dims=NN):
    return lax.dot_general(left, right, dims, precision=HIGHEST, preferred_element_type=F32)


def low_lanes(rows):
    return lax.broadcasted_iota(jnp.int32, (rows, LANE), 1) < CB


def swap(value):
    return pltpu.roll(value, CB, 1)


def part(x):
    return pl.ds(x * RHS, RHS)


def is_even(axis):
    return lax.rem(lax.axis_index(axis), 2) == 0


def by_parity(axis, first, second):
    even = is_even(axis)
    return jnp.where(even, first, second), jnp.where(even, second, first)


def slot(step):
    index = lax.rem(lax.axis_index("tile") + step, N_TILE)
    return pl.multiple_of(index * (ROWS // 2), ROWS // 2)


def write_edges(spread, d1, d2, t):
    low = low_lanes(RHS)
    one, two = by_parity("dom", spread[FX - 1], spread[0])
    d1[...] = one.astype(BF16)
    d2[:RHS, :] = two.astype(BF16)
    d2[RHS:, :] = jnp.zeros((d2.shape[0] - RHS, LANE), BF16)
    for step in (0, 2):
        t[pl.ds(slot(step), ROWS // 2), :] = jnp.zeros((ROWS // 2, LANE), BF16)
    for i in range(FX // 2):
        even, odd = spread[2 * i], spread[2 * i + 1]
        t[pl.ds(slot(1) + i * RHS, RHS), :] = jnp.where(low, swap(even), odd).astype(BF16)
        t[pl.ds(slot(3) + i * RHS, RHS), :] = jnp.where(low, even, swap(odd)).astype(BF16)


def first_kernel(pump_hbm, coup_hbm, p_out, sh_out, sl_out, u_out, d1, d2, t, pump, coup, rows_p, rows_s, mats, arrived):
    copies = []
    for source, target, order in ((pump_hbm, pump, 0), (coup_hbm, coup, 1)):
        for i in range(PIECES):
            columns = pl.ds(i * WIDTH, WIDTH)
            copies.append(
                pltpu.make_async_copy(source.at[:, columns], target.at[:, columns], arrived.at[order, i])
            )
            copies[-1].start()
    for i, copy in enumerate(copies):
        source, target = (pump, rows_p) if i < PIECES else (coup, rows_s)
        copy.wait()
        chunks = WIDTH // LANE
        for k in range(i % PIECES * chunks, (i % PIECES + 1) * chunks):
            target[pl.ds(k, 16, stride=32), :] = source[:, k * LANE : (k + 1) * LANE]
    low = low_lanes(32)
    zero = jnp.zeros((32, LANE), F32)
    for x in range(FX):
        a0, a1 = rows_p[pl.ds(x * 64, 32), :], rows_p[pl.ds(x * 64 + 32, 32), :]
        p_out[pl.ds(x * 64, 32, stride=2), :] = jnp.where(low, a0, swap(a1))
        p_out[pl.ds(x * 64 + 1, 32, stride=2), :] = jnp.where(low, swap(a0), a1)
        s0, s1 = rows_s[pl.ds(x * 64, 32), :], rows_s[pl.ds(x * 64 + 32, 32), :]
        mats[pl.ds(x * 128, 32, stride=2), :] = jnp.where(low, s0, zero)
        mats[pl.ds(x * 128 + 1, 32, stride=2), :] = jnp.where(low, swap(s0), zero)
        mats[pl.ds(x * 128 + 64, 32, stride=2), :] = jnp.where(low, zero, swap(s1))
        mats[pl.ds(x * 128 + 65, 32, stride=2), :] = jnp.where(low, zero, s1)
    spread = []
    for x in range(FX):
        block = pl.ds(x * LANE, LANE)
        high, rest = split(mats[block, :])
        sh_out[block, :] = high
        sl_out[block, :] = rest
        u = dot3(split(p_out[part(x), :]), (high, rest), NN)
        u_out[part(x), :] = u
        spread.append(u)
    write_edges(spread, d1, d2, t)


def operator(v, u, sh, sl, stor, d1, d2, t):
    low = low_lanes(RHS)
    spread = [u[part(x), :] for x in range(FX)]
    after, before = by_parity("dom", d1[...].astype(F32), d2[:RHS, :].astype(F32))
    ends = [before] + spread + [after]
    right, left = [], []
    for i in range(FX // 2):
        there = t[pl.ds(slot(1) + i * RHS, RHS), :].astype(F32)
        here = t[pl.ds(slot(3) + i * RHS, RHS), :].astype(F32)
        place = lax.axis_index("tile")
        right.append(jnp.where(place < N_TILE - 1, there, jnp.zeros_like(there)))
        left.append(jnp.where(place > 0, here, jnp.zeros_like(here)))
    applied = []
    for x in range(FX):
        from_left, from_right = left[x // 2], right[x // 2]
        if x % 2 == 0:
            outside = jnp.where(low, from_left, swap(from_right))
        else:
            outside = jnp.where(low, swap(from_left), from_right)
        pulled = 4.0 * spread[x] - (ends[x] + ends[x + 2] + swap(spread[x]) + outside)
        block = pl.ds(x * LANE, LANE)
        capacity = jnp.concatenate([stor[2 * x : 2 * x + 1, :], stor[2 * x + 1 : 2 * x + 2, :]], axis=1)
        applied.append(
            capacity * v[part(x), :] + dot3(split(pulled), (sh[block, :], sl[block, :]), NT)
        )
    return applied


def second_kernel(v, u, sh, sl, stor, d1, d2, t, ap_out, u_out, *edges):
    applied = operator(v, u, sh, sl, stor, d1, d2, t)
    spread = []
    for x in range(FX):
        ap_out[part(x), :] = applied[x]
        block = pl.ds(x * LANE, LANE)
        s = dot3(split(applied[x]), (sh[block, :], sl[block, :]), NN)
        u_out[part(x), :] = s
        spread.append(s)
    write_edges(spread, *edges)


def deal_kernel(order, v, ap, cells, table):
    for x in range(FX):
        high, rest = split(jnp.concatenate([v[part(x), :], ap[part(x), :]], axis=0))
        table[: 2 * RHS, x * LANE : (x + 1) * LANE] = high
        table[2 * RHS :, x * LANE : (x + 1) * LANE] = rest
    lane = lax.broadcasted_iota(jnp.int32, (LANE, LANE), 1)
    for g in range(FX):
        row = jnp.broadcast_to(order[:, g * LANE : (g + 1) * LANE], (LANE, LANE))
        wanted = jnp.transpose(row)
        picks = [
            jnp.where(wanted == lane + l * LANE, 1.0, 0.0).astype(BF16) for l in range(FX)
        ]
        cells[pl.ds(g * LANE, LANE), :] = dot(
            jnp.concatenate(picks, axis=1), table[...], NT
        ).astype(BF16)


def base_kernel(p, v, base):
    total = jnp.zeros((2 * RHS, 2 * RHS), F32)
    for x in range(FX):
        both = split(jnp.concatenate([p[part(x), :], v[part(x), :]], axis=0))
        total += dot3(both, both, NT)
    base[...] = total


def third_kernel(v, u, sh, sl, stor, d1, d2, t, base, packed):
    applied = operator(v, u, sh, sl, stor, d1, d2, t)
    total = jnp.zeros((2 * RHS, RHS), F32)
    for x in range(FX):
        image = split(applied[x])
        both = [jnp.concatenate([a, b], axis=0) for a, b in zip(split(v[part(x), :]), image)]
        total += dot3(both, image, NT)
    m0, m1, m2 = base[:RHS, :RHS], base[:RHS, RHS:], base[RHS:, RHS:]
    m1 = symmetric(m1)
    m3 = symmetric(total[:RHS])
    m4 = total[RHS:]
    row, column = square_index()
    upper = row <= column
    packed[:RHS, :] = jnp.concatenate([jnp.where(upper, m0, m2), jnp.where(upper, m1, m3)], axis=1)
    ends = jnp.where(row == 0, diagonal(m2), jnp.where(row == 1, diagonal(m3), 0.0))
    packed[RHS:, :] = jnp.concatenate([m4, ends], axis=1)


def square_index():
    return [lax.broadcasted_iota(jnp.int32, (RHS, RHS), d) for d in (0, 1)]


def diagonal(matrix):
    row, column = square_index()
    return jnp.sum(jnp.where(row == column, matrix, 0.0), axis=0, keepdims=True)


def column_diagonal(matrix):
    row, column = square_index()
    return jnp.sum(jnp.where(row == column, matrix, 0.0), axis=1, keepdims=True)


def unpack_pair(matrix, ends):
    row, column = square_index()
    turned = jnp.transpose(matrix)
    first = jnp.where(row <= column, matrix, turned)
    second = jnp.where(row > column, matrix, jnp.where(row < column, turned, ends))
    return first, second


def eliminate(joined, panel=8):
    order, width = joined.shape
    parts = [joined[g : g + panel, :] for g in range(0, order, panel)]
    index = lax.broadcasted_iota(jnp.int32, (panel, width), 0)

    def wide(value):
        pieces = [value] * (width // LANE)
        if width % LANE:
            pieces.append(value[:, : width % LANE])
        return jnp.concatenate(pieces, axis=1) if len(pieces) > 1 else value

    def apply(rows, at, c0, c1, inverse, where):
        r0, r1 = rows[at : at + 1, :], rows[at + 1 : at + 2, :]
        s0 = inverse[0] * r0 + inverse[1] * r1
        s1 = inverse[2] * r0 + inverse[3] * r1
        rest = rows - (c0 * s0 + c1 * s1)
        return jnp.where(where == at, s0, jnp.where(where == at + 1, s1, rest))

    for g in range(len(parts)):
        rows = parts[g]
        first = g * panel
        columns = [
            jnp.broadcast_to(rows[:, first + q : first + q + 1], (panel, LANE)) for q in range(panel)
        ]
        for at in range(0, panel, 2):
            c0, c1 = columns[at], columns[at + 1]
            a, c = c0[at : at + 1, :], c0[at + 1 : at + 2, :]
            b, d = c1[at : at + 1, :], c1[at + 1 : at + 2, :]
            scale = 1.0 / (a * d - b * c)
            inverse = (d * scale, -b * scale, -c * scale, a * scale)
            for q in range(at + 2, panel):
                columns[q] = apply(columns[q], at, c0, c1, inverse, index[:, :LANE])
            rows = apply(rows, at, wide(c0), wide(c1), [wide(v) for v in inverse], index)
        parts[g] = rows
        for h in range(len(parts)):
            if h != g:
                taken = None
                for q in range(panel):
                    column = jnp.broadcast_to(parts[h][:, first + q : first + q + 1], (panel, width))
                    term = column * rows[q : q + 1, :]
                    taken = term if taken is None else taken + term
                parts[h] = parts[h] - taken
    return jnp.concatenate(parts, axis=0)[:, order:]


def symmetric(matrix):
    return 0.5 * (matrix + jnp.transpose(matrix))


def solve_kernel(cell_total, packed, cells, heads, scale, weights, later, rows):
    m0, m2 = unpack_pair(packed[:RHS, :RHS], packed[RHS : RHS + 1, RHS:])
    m1, m3 = unpack_pair(packed[:RHS, RHS:], packed[RHS + 1 : RHS + 2, RHS:])
    first = eliminate(jnp.concatenate([m1, m0, m2], axis=1))
    alpha, shift = first[:, :RHS], first[:, RHS:]
    curved = symmetric(m3 - exact(m2, shift))
    target = m1 - exact(m2, alpha)
    gamma = eliminate(jnp.concatenate([curved, target], axis=1))
    mixed = alpha - exact(shift, gamma)
    both = jnp.concatenate([mixed, gamma], axis=0)
    spread = jnp.concatenate([column_diagonal(m0), column_diagonal(m2)], axis=0)
    bound = jnp.sum(jnp.abs(both) * jnp.sqrt(spread * (1.0 / cell_total)), axis=0, keepdims=True)
    bound = jnp.where(bound > 0.0, bound, 1.0)
    scale[...] = bound
    high, rest = split(jnp.concatenate([both / bound, both / bound], axis=1))
    value = dot3((cells[:, :LANE], cells[:, LANE:]), (high, rest), NN)
    rows[...] = value
    half = FX * LANE // 2
    even, odd = rows[pl.ds(0, half, stride=2), :], rows[pl.ds(1, half, stride=2), :]
    heads[...] = jnp.where(low_lanes(half), even, odd)
    weights[...] = both
    later[...] = jnp.concatenate([m2, m3], axis=1)


def gram_kernel(cell_total, packed, weights, later, kriging, gram, kept):
    kept[...] = kriging[...]
    mixed, gamma = weights[:RHS, :], weights[RHS:, :]
    rest = exact(packed[RHS:, :RHS], gamma) + exact(later[:, RHS:], mixed) - later[:, :RHS]
    gram[...] = symmetric(exact(jnp.transpose(gamma), rest)) * (1.0 / cell_total)


def product_kernel(kriging, arrived, scale, sens, rows):
    half = FX * LANE // 2
    value = arrived[...].astype(F32)
    rows[pl.ds(0, half, stride=2), :] = value
    rows[pl.ds(1, half, stride=2), :] = swap(value)
    high, rest = split(rows[...])
    sens[...] = (dot(kriging[...], high, NN) + dot(kriging[...], rest, NN))[:, :RHS] * scale[...]


def call(kernel, shapes, *operands, scratch=(), flops=1000000, place=pltpu.VMEM):
    return pl.pallas_call(
        kernel,
        out_shape=[jax.ShapeDtypeStruct(shape, kind) for shape, kind in shapes],
        in_specs=[pl.BlockSpec(memory_space=place)] * len(operands),
        out_specs=[pl.BlockSpec(memory_space=pltpu.VMEM)] * len(shapes),
        scratch_shapes=list(scratch),
        compiler_params=PARAMS,
        cost_estimate=pl.CostEstimate(flops=flops, bytes_accessed=1 << 20, transcendentals=0),
    )(*operands)


EDGES = (((RHS, LANE), BF16), ((RHS + 16, LANE), BF16), ((N_TILE * ROWS // 2, LANE), BF16))
FIELD = ((ROWS, LANE), F32)


def exchange(d1, d2, t):
    devices = lax.axis_size("dom")
    first = [(i, i ^ 1) for i in range(devices)]
    second = [(i, ((i + 1) ^ 1) - 1) for i in range(1, devices - 1)]
    t = lax.all_to_all(t.reshape(N_TILE, -1, LANE), "tile", 0, 0, tiled=True)
    d2 = lax.ppermute(d2, "dom", second)
    return lax.ppermute(d1, "dom", first), d2, t.reshape(-1, LANE)


def member_groups(sizes, together):
    strides, total = [], 1
    for size in reversed(sizes):
        strides.insert(0, total)
        total *= size

    def numbers(axes):
        values = [0]
        for axis in axes:
            values = [v + i * strides[axis] for v in values for i in range(sizes[axis])]
        return values

    apart = [axis for axis in range(len(sizes)) if axis not in together]
    return [[base + v for v in numbers(together)] for base in numbers(apart)]


def reduce_all(packed):
    axes = ("dom", "tile")
    sizes = (4, 16, 2, 4)
    near = member_groups(sizes, (0, 2, 3))
    far = member_groups(sizes, (1,))

    def trade(array, groups):
        return lax.all_to_all(array, axes, 0, 0, axis_index_groups=groups, tiled=True)

    n, m = len(near[0]), len(far[0])
    mine = jnp.sum(trade(packed.reshape(n, -1, LANE), near), axis=0)
    mine = jnp.sum(trade(jnp.broadcast_to(mine[None], (m,) + mine.shape), far), axis=0)
    return trade(jnp.broadcast_to(mine[None], (n,) + mine.shape), near).reshape(packed.shape)


def shards(pumping, coupling, storage, tile_order, kriging):
    groups = lax.axis_size("dom")
    cell_total = storage.shape[0] * CB * groups * lax.axis_size("tile")
    scratch = lambda rows: pltpu.VMEM((rows, LANE), F32)
    p, sh, sl, u, *edges = call(
        first_kernel,
        (FIELD, ((FX * LANE, LANE), BF16), ((FX * LANE, LANE), BF16), FIELD) + EDGES,
        pltpu.with_memory_space_constraint(pumping, pltpu.HBM),
        pltpu.with_memory_space_constraint(coupling, pltpu.HBM),
        scratch=(
            pltpu.VMEM((16, RHS * CB), F32),
            pltpu.VMEM((16, CB * CB), F32),
            scratch(ROWS),
            scratch(ROWS),
            scratch(FX * LANE),
            pltpu.SemaphoreType.DMA((2, PIECES)),
        ),
        place=pltpu.HBM,
    )
    halo = exchange(*edges)
    ap, u, *edges = call(second_kernel, (FIELD, FIELD) + EDGES, p, u, sh, sl, storage, *halo)
    halo = exchange(*edges)
    (base,) = call(base_kernel, (((2 * RHS, LANE), F32),), p, ap)
    (packed,) = call(
        third_kernel, (((2 * RHS, LANE), F32),), ap, u, sh, sl, storage, *halo, base
    )
    (cells,) = call(
        deal_kernel,
        (((FX * LANE, 4 * RHS), BF16),),
        *(tile_order, p, ap),
        scratch=(pltpu.VMEM((4 * RHS, FX * LANE), BF16),),
        flops=LONG,
    )
    packed = reduce_all(packed)
    heads, scale, weights, later = call(
        lambda *refs: solve_kernel(cell_total, *refs),
        (((FX * LANE // 2, LANE), F32), ((1, RHS), F32), ((2 * RHS, RHS), F32), ((RHS, LANE), F32)),
        *(packed, cells),
        scratch=(scratch(FX * LANE),),
    )
    heads = heads.astype(jnp.float16).reshape(groups, -1, LANE)
    heads = lax.all_to_all(heads, "dom", 0, 0, tiled=True).reshape(-1, LANE).astype(F32)
    gram, kriging = call(
        lambda *refs: gram_kernel(cell_total, *refs),
        (((RHS, RHS), F32), (kriging.shape, BF16)),
        *(packed, weights, later, kriging),
        flops=LONG,
    )
    (sens,) = call(
        product_kernel,
        (((kriging.shape[0], RHS), F32),),
        *(kriging, heads, scale),
        scratch=(scratch(FX * LANE),),
    )
    return sens, gram


def solution(mesh):
    spec = P(("dom", "tile"), None)
    return jax.shard_map(
        shards, mesh=mesh, in_specs=(spec,) * 5, out_specs=(spec, P()), check_vma=False
    )
```

```python
import jax
import jax.numpy as jnp
from jax import lax
from jax.experimental import pallas as pl
from jax.experimental.pallas import tpu as pltpu
from jax.sharding import PartitionSpec as P

RHS = 64
CB = 64
FX = 8
PILOT = 16
N_TILE = 4
LANE = 128
ROWS = FX * RHS
F32 = jnp.float32
BF16 = jnp.bfloat16
HIGHEST = lax.Precision.HIGHEST
PARAMS = pltpu.CompilerParams(vmem_limit_bytes=40 * 1024 * 1024)
PIECES = 4
WIDTH = RHS * CB // PIECES
LONG = 10**11
NN = (((1,), (0,)), ((), ()))
NT = (((1,), (1,)), ((), ()))


def split(value):
    high = value.astype(BF16)
    return high, (value - high.astype(F32)).astype(BF16)


def dot(left, right, dims):
    return lax.dot_general(left, right, dims, preferred_element_type=F32)


def dot3(left, right, dims):
    (lh, ll), (rh, rl) = left, right
    return dot(lh, rh, dims) + (dot(ll, rh, dims) + dot(lh, rl, dims))


def exact(left, right, dims=NN):
    return lax.dot_general(left, right, dims, precision=HIGHEST, preferred_element_type=F32)


def low_lanes(rows):
    return lax.broadcasted_iota(jnp.int32, (rows, LANE), 1) < CB


def swap(value):
    return pltpu.roll(value, CB, 1)


def part(x):
    return pl.ds(x * RHS, RHS)


def is_even(axis):
    return lax.rem(lax.axis_index(axis), 2) == 0


def by_parity(axis, first, second):
    even = is_even(axis)
    return jnp.where(even, first, second), jnp.where(even, second, first)


def slot(step):
    return lax.rem(lax.axis_index("tile") + step, N_TILE)


def write_edges(spread, d1, d2, t):
    low = low_lanes(RHS)
    one, two = by_parity("dom", spread[FX - 1], spread[0])
    d1[...] = one.astype(BF16)
    d2[:RHS, :] = two.astype(BF16)
    d2[RHS:, :] = jnp.zeros((d2.shape[0] - RHS, LANE), BF16)
    for step in (0, 2):
        t[slot(step)] = jnp.zeros((ROWS // 2, LANE), BF16)
    for i in range(FX // 2):
        even, odd = spread[2 * i], spread[2 * i + 1]
        t[slot(1), part(i), :] = jnp.where(low, swap(even), odd).astype(BF16)
        t[slot(3), part(i), :] = jnp.where(low, even, swap(odd)).astype(BF16)


def first_kernel(pump_hbm, coup_hbm, p_out, sh_out, sl_out, u_out, d1, d2, t, pump, coup, rows_p, rows_s, mats, arrived):
    copies = []
    for source, target, order in ((pump_hbm, pump, 0), (coup_hbm, coup, 1)):
        for i in range(PIECES):
            columns = pl.ds(i * WIDTH, WIDTH)
            copies.append(
                pltpu.make_async_copy(source.at[:, columns], target.at[:, columns], arrived.at[order, i])
            )
            copies[-1].start()
    for i, copy in enumerate(copies):
        source, target = (pump, rows_p) if i < PIECES else (coup, rows_s)
        copy.wait()
        chunks = WIDTH // LANE
        for k in range(i % PIECES * chunks, (i % PIECES + 1) * chunks):
            target[pl.ds(k, 16, stride=32), :] = source[:, k * LANE : (k + 1) * LANE]
    low = low_lanes(32)
    zero = jnp.zeros((32, LANE), F32)
    for x in range(FX):
        a0, a1 = rows_p[pl.ds(x * 64, 32), :], rows_p[pl.ds(x * 64 + 32, 32), :]
        p_out[pl.ds(x * 64, 32, stride=2), :] = jnp.where(low, a0, swap(a1))
        p_out[pl.ds(x * 64 + 1, 32, stride=2), :] = jnp.where(low, swap(a0), a1)
        s0, s1 = rows_s[pl.ds(x * 64, 32), :], rows_s[pl.ds(x * 64 + 32, 32), :]
        mats[pl.ds(x * 128, 32, stride=2), :] = jnp.where(low, s0, zero)
        mats[pl.ds(x * 128 + 1, 32, stride=2), :] = jnp.where(low, swap(s0), zero)
        mats[pl.ds(x * 128 + 64, 32, stride=2), :] = jnp.where(low, zero, swap(s1))
        mats[pl.ds(x * 128 + 65, 32, stride=2), :] = jnp.where(low, zero, s1)
    spread = []
    for x in range(FX):
        block = pl.ds(x * LANE, LANE)
        high, rest = split(mats[block, :])
        sh_out[block, :] = high
        sl_out[block, :] = rest
        u = dot3(split(p_out[part(x), :]), (high, rest), NN)
        u_out[part(x), :] = u
        spread.append(u)
    write_edges(spread, d1, d2, t)


def operator(v, u, sh, sl, stor, d1, d2, t):
    low = low_lanes(RHS)
    spread = [u[part(x), :] for x in range(FX)]
    after, before = by_parity("dom", d1[...].astype(F32), d2[:RHS, :].astype(F32))
    ends = [before] + spread + [after]
    right, left = [], []
    for i in range(FX // 2):
        there = t[slot(1), part(i), :].astype(F32)
        here = t[slot(3), part(i), :].astype(F32)
        place = lax.axis_index("tile")
        right.append(jnp.where(place < N_TILE - 1, there, jnp.zeros_like(there)))
        left.append(jnp.where(place > 0, here, jnp.zeros_like(here)))
    applied = []
    for x in range(FX):
        from_left, from_right = left[x // 2], right[x // 2]
        if x % 2 == 0:
            outside = jnp.where(low, from_left, swap(from_right))
        else:
            outside = jnp.where(low, swap(from_left), from_right)
        pulled = 4.0 * spread[x] - (ends[x] + ends[x + 2] + swap(spread[x]) + outside)
        block = pl.ds(x * LANE, LANE)
        capacity = jnp.concatenate([stor[2 * x : 2 * x + 1, :], stor[2 * x + 1 : 2 * x + 2, :]], axis=1)
        applied.append(
            capacity * v[part(x), :] + dot3(split(pulled), (sh[block, :], sl[block, :]), NT)
        )
    return applied


def second_kernel(v, u, sh, sl, stor, d1, d2, t, ap_out, u_out, *edges):
    applied = operator(v, u, sh, sl, stor, d1, d2, t)
    spread = []
    for x in range(FX):
        ap_out[part(x), :] = applied[x]
        block = pl.ds(x * LANE, LANE)
        s = dot3(split(applied[x]), (sh[block, :], sl[block, :]), NN)
        u_out[part(x), :] = s
        spread.append(s)
    write_edges(spread, *edges)


def deal_kernel(order, v, ap, cells, table):
    for x in range(FX):
        high, rest = split(jnp.concatenate([v[part(x), :], ap[part(x), :]], axis=0))
        table[: 2 * RHS, x * LANE : (x + 1) * LANE] = high
        table[2 * RHS :, x * LANE : (x + 1) * LANE] = rest
    lane = lax.broadcasted_iota(jnp.int32, (LANE, LANE), 1)
    for g in range(FX):
        row = jnp.broadcast_to(order[:, g * LANE : (g + 1) * LANE], (LANE, LANE))
        wanted = jnp.transpose(row)
        picks = [
            jnp.where(wanted == lane + l * LANE, 1.0, 0.0).astype(BF16) for l in range(FX)
        ]
        cells[pl.ds(g * LANE, LANE), :] = dot(
            jnp.concatenate(picks, axis=1), table[...], NT
        ).astype(BF16)


def base_kernel(p, v, base):
    total = jnp.zeros((2 * RHS, 2 * RHS), F32)
    for x in range(FX):
        both = split(jnp.concatenate([p[part(x), :], v[part(x), :]], axis=0))
        total += dot3(both, both, NT)
    base[...] = total


def third_kernel(v, u, sh, sl, stor, d1, d2, t, base, packed):
    applied = operator(v, u, sh, sl, stor, d1, d2, t)
    total = jnp.zeros((2 * RHS, RHS), F32)
    for x in range(FX):
        image = split(applied[x])
        both = [jnp.concatenate([a, b], axis=0) for a, b in zip(split(v[part(x), :]), image)]
        total += dot3(both, image, NT)
    m0, m1, m2 = base[:RHS, :RHS], base[:RHS, RHS:], base[RHS:, RHS:]
    m1 = symmetric(m1)
    m3 = symmetric(total[:RHS])
    m4 = total[RHS:]
    row, column = square_index()
    upper = row <= column
    packed[:RHS, :] = jnp.concatenate([jnp.where(upper, m0, m2), jnp.where(upper, m1, m3)], axis=1)
    ends = jnp.where(row == 0, diagonal(m2), jnp.where(row == 1, diagonal(m3), 0.0))
    packed[RHS:, :] = jnp.concatenate([m4, ends], axis=1)


def square_index():
    return [lax.broadcasted_iota(jnp.int32, (RHS, RHS), d) for d in (0, 1)]


def diagonal(matrix):
    row, column = square_index()
    return jnp.sum(jnp.where(row == column, matrix, 0.0), axis=0, keepdims=True)


def column_diagonal(matrix):
    row, column = square_index()
    return jnp.sum(jnp.where(row == column, matrix, 0.0), axis=1, keepdims=True)


def unpack_pair(matrix, ends):
    row, column = square_index()
    turned = jnp.transpose(matrix)
    first = jnp.where(row <= column, matrix, turned)
    second = jnp.where(row > column, matrix, jnp.where(row < column, turned, ends))
    return first, second


def eliminate(joined, panel=8):
    order, width = joined.shape
    parts = [joined[g : g + panel, :] for g in range(0, order, panel)]
    index = lax.broadcasted_iota(jnp.int32, (panel, width), 0)

    def wide(value):
        pieces = [value] * (width // LANE)
        if width % LANE:
            pieces.append(value[:, : width % LANE])
        return jnp.concatenate(pieces, axis=1) if len(pieces) > 1 else value

    def apply(rows, at, c0, c1, inverse, where):
        r0, r1 = rows[at : at + 1, :], rows[at + 1 : at + 2, :]
        s0 = inverse[0] * r0 + inverse[1] * r1
        s1 = inverse[2] * r0 + inverse[3] * r1
        rest = rows - (c0 * s0 + c1 * s1)
        return jnp.where(where == at, s0, jnp.where(where == at + 1, s1, rest))

    for g in range(len(parts)):
        rows = parts[g]
        first = g * panel
        columns = [
            jnp.broadcast_to(rows[:, first + q : first + q + 1], (panel, LANE)) for q in range(panel)
        ]
        for at in range(0, panel, 2):
            c0, c1 = columns[at], columns[at + 1]
            a, c = c0[at : at + 1, :], c0[at + 1 : at + 2, :]
            b, d = c1[at : at + 1, :], c1[at + 1 : at + 2, :]
            scale = 1.0 / (a * d - b * c)
            inverse = (d * scale, -b * scale, -c * scale, a * scale)
            for q in range(at + 2, panel):
                columns[q] = apply(columns[q], at, c0, c1, inverse, index[:, :LANE])
            rows = apply(rows, at, wide(c0), wide(c1), [wide(v) for v in inverse], index)
        parts[g] = rows
        for h in range(len(parts)):
            if h != g:
                taken = None
                for q in range(panel):
                    column = jnp.broadcast_to(parts[h][:, first + q : first + q + 1], (panel, width))
                    term = column * rows[q : q + 1, :]
                    taken = term if taken is None else taken + term
                parts[h] = parts[h] - taken
    return jnp.concatenate(parts, axis=0)[:, order:]


def symmetric(matrix):
    return 0.5 * (matrix + jnp.transpose(matrix))


def solve_kernel(cell_total, packed, cells, heads, scale, weights, later, rows):
    m0, m2 = unpack_pair(packed[:RHS, :RHS], packed[RHS : RHS + 1, RHS:])
    m1, m3 = unpack_pair(packed[:RHS, RHS:], packed[RHS + 1 : RHS + 2, RHS:])
    first = eliminate(jnp.concatenate([m1, m0, m2], axis=1))
    alpha, shift = first[:, :RHS], first[:, RHS:]
    bent = exact(m2, first)
    curved = symmetric(m3 - bent[:, RHS:])
    target = m1 - bent[:, :RHS]
    gamma = eliminate(jnp.concatenate([curved, target], axis=1))
    mixed = alpha - exact(shift, gamma)
    both = jnp.concatenate([mixed, gamma], axis=0)
    spread = jnp.concatenate([column_diagonal(m0), column_diagonal(m2)], axis=0)
    bound = jnp.sum(jnp.abs(both) * jnp.sqrt(spread * (1.0 / cell_total)), axis=0, keepdims=True)
    bound = jnp.where(bound > 0.0, bound, 1.0)
    scale[...] = bound
    high, rest = split(jnp.concatenate([both / bound, both / bound], axis=1))
    value = dot3((cells[:, :LANE], cells[:, LANE:]), (high, rest), NN)
    rows[...] = value
    half = FX * LANE // 2
    even, odd = rows[pl.ds(0, half, stride=2), :], rows[pl.ds(1, half, stride=2), :]
    heads[...] = jnp.where(low_lanes(half), even, odd)
    weights[...] = both
    later[...] = jnp.concatenate([m2, m3], axis=1)


def gram_kernel(cell_total, packed, weights, later, kriging, gram, kept):
    cells = kriging.shape[1]
    source = lax.broadcasted_iota(jnp.int32, (cells, cells // 2), 0)
    target = lax.broadcasted_iota(jnp.int32, (cells, cells // 2), 1)
    for parity in range(2):
        pick = jnp.where(source == 2 * target + parity, 1.0, 0.0).astype(BF16)
        kept[pl.ds(parity * PILOT, PILOT), :] = dot(kriging[...], pick, NN).astype(BF16)
    mixed, gamma = weights[:RHS, :], weights[RHS:, :]
    rest = exact(packed[RHS:, :RHS], gamma) + exact(later[:, RHS:], mixed) - later[:, :RHS]
    gram[...] = symmetric(exact(jnp.transpose(gamma), rest)) * (1.0 / cell_total)


def product_kernel(kriging, arrived, scale, sens):
    high, rest = split(arrived[...])
    product = dot(kriging[...], high, NN) + dot(kriging[...], rest, NN)
    sens[...] = (product[:PILOT, :RHS] + product[PILOT:, RHS:]) * scale[...]


def call(kernel, shapes, *operands, scratch=(), flops=1000000, place=pltpu.VMEM):
    return pl.pallas_call(
        kernel,
        out_shape=[jax.ShapeDtypeStruct(shape, kind) for shape, kind in shapes],
        in_specs=[pl.BlockSpec(memory_space=place)] * len(operands),
        out_specs=[pl.BlockSpec(memory_space=pltpu.VMEM)] * len(shapes),
        scratch_shapes=list(scratch),
        compiler_params=PARAMS,
        cost_estimate=pl.CostEstimate(flops=flops, bytes_accessed=1 << 20, transcendentals=0),
    )(*operands)


EDGES = (((RHS, LANE), BF16), ((RHS + 16, LANE), BF16), ((N_TILE, ROWS // 2, LANE), BF16))
FIELD = ((ROWS, LANE), F32)


def exchange(d1, d2, t):
    devices = lax.axis_size("dom")
    first = [(i, i ^ 1) for i in range(devices)]
    second = [(i, ((i + 1) ^ 1) - 1) for i in range(1, devices - 1)]
    t = lax.all_to_all(t, "tile", 0, 0, tiled=True)
    d2 = lax.ppermute(d2, "dom", second)
    return lax.ppermute(d1, "dom", first), d2, t


def member_groups(sizes, together):
    strides, total = [], 1
    for size in reversed(sizes):
        strides.insert(0, total)
        total *= size

    def numbers(axes):
        values = [0]
        for axis in axes:
            values = [v + i * strides[axis] for v in values for i in range(sizes[axis])]
        return values

    apart = [axis for axis in range(len(sizes)) if axis not in together]
    return [[base + v for v in numbers(together)] for base in numbers(apart)]


def reduce_all(packed):
    axes = ("dom", "tile")
    sizes = (4, 16, 2, 4)
    near = member_groups(sizes, (0, 2, 3))
    far = member_groups(sizes, (1,))

    def trade(array, groups):
        return lax.all_to_all(array, axes, 0, 0, axis_index_groups=groups, tiled=True)

    n, m = len(near[0]), len(far[0])
    mine = jnp.sum(trade(packed.reshape(n, -1, LANE), near), axis=0)
    mine = jnp.sum(trade(jnp.broadcast_to(mine[None], (m,) + mine.shape), far), axis=0)
    return trade(jnp.broadcast_to(mine[None], (n,) + mine.shape), near).reshape(packed.shape)


def shards(pumping, coupling, storage, tile_order, kriging):
    groups = lax.axis_size("dom")
    cell_total = storage.shape[0] * CB * groups * lax.axis_size("tile")
    scratch = lambda rows: pltpu.VMEM((rows, LANE), F32)
    p, sh, sl, u, *edges = call(
        first_kernel,
        (FIELD, ((FX * LANE, LANE), BF16), ((FX * LANE, LANE), BF16), FIELD) + EDGES,
        pltpu.with_memory_space_constraint(pumping, pltpu.HBM),
        pltpu.with_memory_space_constraint(coupling, pltpu.HBM),
        scratch=(
            pltpu.VMEM((16, RHS * CB), F32),
            pltpu.VMEM((16, CB * CB), F32),
            scratch(ROWS),
            scratch(ROWS),
            scratch(FX * LANE),
            pltpu.SemaphoreType.DMA((2, PIECES)),
        ),
        place=pltpu.HBM,
    )
    halo = exchange(*edges)
    ap, u, *edges = call(second_kernel, (FIELD, FIELD) + EDGES, p, u, sh, sl, storage, *halo)
    halo = exchange(*edges)
    (base,) = call(base_kernel, (((2 * RHS, LANE), F32),), p, ap)
    (packed,) = call(
        third_kernel, (((2 * RHS, LANE), F32),), ap, u, sh, sl, storage, *halo, base
    )
    (cells,) = call(
        deal_kernel,
        (((FX * LANE, 4 * RHS), BF16),),
        *(tile_order, p, ap),
        scratch=(pltpu.VMEM((4 * RHS, FX * LANE), BF16),),
        flops=LONG,
    )
    packed = reduce_all(packed)
    heads, scale, weights, later = call(
        lambda *refs: solve_kernel(cell_total, *refs),
        (((FX * LANE // 2, LANE), F32), ((1, RHS), F32), ((2 * RHS, RHS), F32), ((RHS, LANE), F32)),
        *(packed, cells),
        scratch=(scratch(FX * LANE),),
    )
    heads = heads.astype(jnp.float16).reshape(groups, -1, LANE)
    heads = lax.all_to_all(heads, "dom", 0, 0, tiled=True).reshape(-1, LANE).astype(F32)
    gram, kriging = call(
        lambda *refs: gram_kernel(cell_total, *refs),
        (((RHS, RHS), F32), ((2 * PILOT, FX * LANE // 2), BF16)),
        *(packed, weights, later, kriging),
        flops=LONG,
    )
    (sens,) = call(
        product_kernel,
        (((PILOT, RHS), F32),),
        *(kriging, heads, scale),
    )
    return sens, gram


def solution(mesh):
    spec = P(("dom", "tile"), None)
    return jax.shard_map(
        shards, mesh=mesh, in_specs=(spec,) * 5, out_specs=(spec, P()), check_vma=False
    )
```

```python
import jax
import jax.numpy as jnp
from jax import lax
from jax.experimental import pallas as pl
from jax.experimental.pallas import tpu as pltpu
from jax.sharding import PartitionSpec as P

RHS = 64
CB = 64
FX = 8
PILOT = 16
LANE = 128
ROWS = FX * RHS
F32 = jnp.float32
BF16 = jnp.bfloat16
HIGHEST = lax.Precision.HIGHEST
PARAMS = pltpu.CompilerParams(vmem_limit_bytes=40 * 1024 * 1024)
PIECES = 4
WIDTH = RHS * CB // PIECES
LONG = 10**11
NN = (((1,), (0,)), ((), ()))
NT = (((1,), (1,)), ((), ()))


def split(value):
    high = value.astype(BF16)
    return high, (value - high.astype(F32)).astype(BF16)


def dot(left, right, dims):
    return lax.dot_general(left, right, dims, preferred_element_type=F32)


def dot3(left, right, dims):
    (lh, ll), (rh, rl) = left, right
    return dot(lh, rh, dims) + (dot(ll, rh, dims) + dot(lh, rl, dims))


def exact(left, right, dims=NN):
    return lax.dot_general(left, right, dims, precision=HIGHEST, preferred_element_type=F32)


def low_lanes(rows):
    return lax.broadcasted_iota(jnp.int32, (rows, LANE), 1) < CB


def swap(value):
    return pltpu.roll(value, CB, 1)


def part(x):
    return pl.ds(x * RHS, RHS)


def is_even(axis):
    return lax.rem(lax.axis_index(axis), 2) == 0


def by_parity(axis, first, second):
    even = is_even(axis)
    return jnp.where(even, first, second), jnp.where(even, second, first)


def write_edges(spread, d1, d2, t1, t2):
    low = low_lanes(RHS)
    one, two = by_parity("dom", spread[FX - 1], spread[0])
    d1[...] = one.astype(BF16)
    d2[:RHS, :] = two.astype(BF16)
    d2[RHS:, :] = jnp.zeros((d2.shape[0] - RHS, LANE), BF16)
    for i in range(FX // 2):
        even, odd = spread[2 * i], spread[2 * i + 1]
        left = jnp.where(low, even, swap(odd))
        right = jnp.where(low, swap(even), odd)
        one, two = by_parity("tile", right, left)
        t1[part(i), :] = one.astype(BF16)
        t2[part(i), :] = two.astype(BF16)


def first_kernel(pump_hbm, coup_hbm, p_out, sh_out, sl_out, u_out, d1, d2, t1, t2, pump, coup, rows_p, rows_s, mats, arrived):
    copies = []
    for source, target, order in ((pump_hbm, pump, 0), (coup_hbm, coup, 1)):
        for i in range(PIECES):
            columns = pl.ds(i * WIDTH, WIDTH)
            copies.append(
                pltpu.make_async_copy(source.at[:, columns], target.at[:, columns], arrived.at[order, i])
            )
            copies[-1].start()
    for i, copy in enumerate(copies):
        source, target = (pump, rows_p) if i < PIECES else (coup, rows_s)
        copy.wait()
        chunks = WIDTH // LANE
        for k in range(i % PIECES * chunks, (i % PIECES + 1) * chunks):
            target[pl.ds(k, 16, stride=32), :] = source[:, k * LANE : (k + 1) * LANE]
    low = low_lanes(32)
    zero = jnp.zeros((32, LANE), F32)
    for x in range(FX):
        a0, a1 = rows_p[pl.ds(x * 64, 32), :], rows_p[pl.ds(x * 64 + 32, 32), :]
        p_out[pl.ds(x * 64, 32, stride=2), :] = jnp.where(low, a0, swap(a1))
        p_out[pl.ds(x * 64 + 1, 32, stride=2), :] = jnp.where(low, swap(a0), a1)
        s0, s1 = rows_s[pl.ds(x * 64, 32), :], rows_s[pl.ds(x * 64 + 32, 32), :]
        mats[pl.ds(x * 128, 32, stride=2), :] = jnp.where(low, s0, zero)
        mats[pl.ds(x * 128 + 1, 32, stride=2), :] = jnp.where(low, swap(s0), zero)
        mats[pl.ds(x * 128 + 64, 32, stride=2), :] = jnp.where(low, zero, swap(s1))
        mats[pl.ds(x * 128 + 65, 32, stride=2), :] = jnp.where(low, zero, s1)
    spread = []
    for x in range(FX):
        block = pl.ds(x * LANE, LANE)
        high, rest = split(mats[block, :])
        sh_out[block, :] = high
        sl_out[block, :] = rest
        u = dot3(split(p_out[part(x), :]), (high, rest), NN)
        u_out[part(x), :] = u
        spread.append(u)
    write_edges(spread, d1, d2, t1, t2)


def operator(v, u, sh, sl, stor, d1, d2, t1, t2):
    low = low_lanes(RHS)
    spread = [u[part(x), :] for x in range(FX)]
    after, before = by_parity("dom", d1[...].astype(F32), d2[:RHS, :].astype(F32))
    ends = [before] + spread + [after]
    right, left = [], []
    for i in range(FX // 2):
        one, two = by_parity("tile", t1[part(i), :].astype(F32), t2[part(i), :].astype(F32))
        right.append(one)
        left.append(two)
    applied = []
    for x in range(FX):
        from_left, from_right = left[x // 2], right[x // 2]
        if x % 2 == 0:
            outside = jnp.where(low, from_left, swap(from_right))
        else:
            outside = jnp.where(low, swap(from_left), from_right)
        pulled = 4.0 * spread[x] - (ends[x] + ends[x + 2] + swap(spread[x]) + outside)
        block = pl.ds(x * LANE, LANE)
        capacity = jnp.concatenate([stor[2 * x : 2 * x + 1, :], stor[2 * x + 1 : 2 * x + 2, :]], axis=1)
        applied.append(
            capacity * v[part(x), :] + dot3(split(pulled), (sh[block, :], sl[block, :]), NT)
        )
    return applied


def second_kernel(v, u, sh, sl, stor, d1, d2, t1, t2, ap_out, u_out, *edges):
    applied = operator(v, u, sh, sl, stor, d1, d2, t1, t2)
    spread = []
    for x in range(FX):
        ap_out[part(x), :] = applied[x]
        block = pl.ds(x * LANE, LANE)
        s = dot3(split(applied[x]), (sh[block, :], sl[block, :]), NN)
        u_out[part(x), :] = s
        spread.append(s)
    write_edges(spread, *edges)


def deal_kernel(order, v, ap, cells, table):
    for x in range(FX):
        high, rest = split(jnp.concatenate([v[part(x), :], ap[part(x), :]], axis=0))
        table[: 2 * RHS, x * LANE : (x + 1) * LANE] = high
        table[2 * RHS :, x * LANE : (x + 1) * LANE] = rest
    lane = lax.broadcasted_iota(jnp.int32, (LANE, LANE), 1)
    for g in range(FX):
        row = jnp.broadcast_to(order[:, g * LANE : (g + 1) * LANE], (LANE, LANE))
        wanted = jnp.transpose(row)
        picks = [
            jnp.where(wanted == lane + l * LANE, 1.0, 0.0).astype(BF16) for l in range(FX)
        ]
        cells[pl.ds(g * LANE, LANE), :] = dot(
            jnp.concatenate(picks, axis=1), table[...], NT
        ).astype(BF16)


def base_kernel(p, v, base):
    total = jnp.zeros((2 * RHS, 2 * RHS), F32)
    for x in range(FX):
        both = split(jnp.concatenate([p[part(x), :], v[part(x), :]], axis=0))
        total += dot3(both, both, NT)
    base[...] = total


def third_kernel(v, u, sh, sl, stor, d1, d2, t1, t2, base, packed):
    applied = operator(v, u, sh, sl, stor, d1, d2, t1, t2)
    total = jnp.zeros((2 * RHS, RHS), F32)
    for x in range(FX):
        image = split(applied[x])
        both = [jnp.concatenate([a, b], axis=0) for a, b in zip(split(v[part(x), :]), image)]
        total += dot3(both, image, NT)
    m0, m1, m2 = base[:RHS, :RHS], base[:RHS, RHS:], base[RHS:, RHS:]
    m1 = symmetric(m1)
    m3 = symmetric(total[:RHS])
    m4 = total[RHS:]
    row, column = square_index()
    upper = row <= column
    packed[:RHS, :] = jnp.concatenate([jnp.where(upper, m0, m2), jnp.where(upper, m1, m3)], axis=1)
    ends = jnp.where(row == 0, diagonal(m2), jnp.where(row == 1, diagonal(m3), 0.0))
    packed[RHS:, :] = jnp.concatenate([m4, ends], axis=1)


def square_index():
    return [lax.broadcasted_iota(jnp.int32, (RHS, RHS), d) for d in (0, 1)]


def diagonal(matrix):
    row, column = square_index()
    return jnp.sum(jnp.where(row == column, matrix, 0.0), axis=0, keepdims=True)


def column_diagonal(matrix):
    row, column = square_index()
    return jnp.sum(jnp.where(row == column, matrix, 0.0), axis=1, keepdims=True)


def unpack_pair(matrix, ends):
    row, column = square_index()
    turned = jnp.transpose(matrix)
    first = jnp.where(row <= column, matrix, turned)
    second = jnp.where(row > column, matrix, jnp.where(row < column, turned, ends))
    return first, second


def eliminate(joined, panel=8):
    order, width = joined.shape
    parts = [joined[g : g + panel, :] for g in range(0, order, panel)]
    index = lax.broadcasted_iota(jnp.int32, (panel, width), 0)

    def wide(value):
        pieces = [value] * (width // LANE)
        if width % LANE:
            pieces.append(value[:, : width % LANE])
        return jnp.concatenate(pieces, axis=1) if len(pieces) > 1 else value

    def apply(rows, at, c0, c1, inverse, where):
        r0, r1 = rows[at : at + 1, :], rows[at + 1 : at + 2, :]
        s0 = inverse[0] * r0 + inverse[1] * r1
        s1 = inverse[2] * r0 + inverse[3] * r1
        rest = rows - (c0 * s0 + c1 * s1)
        return jnp.where(where == at, s0, jnp.where(where == at + 1, s1, rest))

    for g in range(len(parts)):
        rows = parts[g]
        first = g * panel
        columns = [
            jnp.broadcast_to(rows[:, first + q : first + q + 1], (panel, LANE)) for q in range(panel)
        ]
        for at in range(0, panel, 2):
            c0, c1 = columns[at], columns[at + 1]
            a, c = c0[at : at + 1, :], c0[at + 1 : at + 2, :]
            b, d = c1[at : at + 1, :], c1[at + 1 : at + 2, :]
            scale = 1.0 / (a * d - b * c)
            inverse = (d * scale, -b * scale, -c * scale, a * scale)
            for q in range(at + 2, panel):
                columns[q] = apply(columns[q], at, c0, c1, inverse, index[:, :LANE])
            rows = apply(rows, at, wide(c0), wide(c1), [wide(v) for v in inverse], index)
        parts[g] = rows
        for h in range(len(parts)):
            if h != g:
                terms = [
                    jnp.broadcast_to(parts[h][:, first + q : first + q + 1], (panel, width)) * rows[q : q + 1, :]
                    for q in range(panel)
                ]
                while len(terms) > 1:
                    terms = [a + b for a, b in zip(terms[::2], terms[1::2])]
                parts[h] = parts[h] - terms[0]
    return jnp.concatenate(parts, axis=0)[:, order:]


def symmetric(matrix):
    return 0.5 * (matrix + jnp.transpose(matrix))


def solve_kernel(cell_total, packed, cells, heads, scale, weights, later, rows):
    m0, m2 = unpack_pair(packed[:RHS, :RHS], packed[RHS : RHS + 1, RHS:])
    m1, m3 = unpack_pair(packed[:RHS, RHS:], packed[RHS + 1 : RHS + 2, RHS:])
    first = eliminate(jnp.concatenate([m1, m0, m2], axis=1))
    alpha, shift = first[:, :RHS], first[:, RHS:]
    bent = exact(m2, first)
    curved = symmetric(m3 - bent[:, RHS:])
    target = m1 - bent[:, :RHS]
    gamma = eliminate(jnp.concatenate([curved, target], axis=1))
    mixed = alpha - exact(shift, gamma)
    both = jnp.concatenate([mixed, gamma], axis=0)
    spread = jnp.concatenate([column_diagonal(m0), column_diagonal(m2)], axis=0)
    bound = jnp.sum(jnp.abs(both) * jnp.sqrt(spread * (1.0 / cell_total)), axis=0, keepdims=True)
    bound = jnp.where(bound > 0.0, bound, 1.0)
    scale[...] = bound
    high, rest = split(jnp.concatenate([both / bound, both / bound], axis=1))
    value = dot3((cells[:, :LANE], cells[:, LANE:]), (high, rest), NN)
    rows[...] = value
    half = FX * LANE // 2
    even, odd = rows[pl.ds(0, half, stride=2), :], rows[pl.ds(1, half, stride=2), :]
    heads[...] = jnp.where(low_lanes(half), even, odd)
    weights[...] = both
    later[...] = jnp.concatenate([m2, m3], axis=1)


def gram_kernel(cell_total, packed, weights, later, kriging, gram, kept):
    cells = kriging.shape[1]
    source = lax.broadcasted_iota(jnp.int32, (cells, cells // 2), 0)
    target = lax.broadcasted_iota(jnp.int32, (cells, cells // 2), 1)
    for parity in range(2):
        pick = jnp.where(source == 2 * target + parity, 1.0, 0.0).astype(BF16)
        kept[pl.ds(parity * PILOT, PILOT), :] = dot(kriging[...], pick, NN).astype(BF16)
    mixed, gamma = weights[:RHS, :], weights[RHS:, :]
    rest = exact(packed[RHS:, :RHS], gamma) + exact(later[:, RHS:], mixed) - later[:, :RHS]
    gram[...] = symmetric(exact(jnp.transpose(gamma), rest)) * (1.0 / cell_total)


def product_kernel(kriging, arrived, scale, sens):
    high, rest = split(arrived[...])
    product = dot(kriging[...], high, NN) + dot(kriging[...], rest, NN)
    sens[...] = (product[:PILOT, :RHS] + product[PILOT:, RHS:]) * scale[...]


def call(kernel, shapes, *operands, scratch=(), flops=1000000, place=pltpu.VMEM):
    return pl.pallas_call(
        kernel,
        out_shape=[jax.ShapeDtypeStruct(shape, kind) for shape, kind in shapes],
        in_specs=[pl.BlockSpec(memory_space=place)] * len(operands),
        out_specs=[pl.BlockSpec(memory_space=pltpu.VMEM)] * len(shapes),
        scratch_shapes=list(scratch),
        compiler_params=PARAMS,
        cost_estimate=pl.CostEstimate(flops=flops, bytes_accessed=1 << 20, transcendentals=0),
    )(*operands)


EDGES = (((RHS, LANE), BF16), ((RHS + 16, LANE), BF16), ((ROWS // 2, LANE), BF16), ((ROWS // 2, LANE), BF16))
FIELD = ((ROWS, LANE), F32)


def exchange(d1, d2, t1, t2):
    def along(axis, one, two):
        devices = lax.axis_size(axis)
        first = [(i, i ^ 1) for i in range(devices)]
        second = [(i, ((i + 1) ^ 1) - 1) for i in range(1, devices - 1)]
        two = lax.ppermute(two, axis, second)
        return lax.ppermute(one, axis, first), two

    t1, t2 = along("tile", t1, t2)
    d1, d2 = along("dom", d1, d2)
    return d1, d2, t1, t2


def member_groups(sizes, together):
    strides, total = [], 1
    for size in reversed(sizes):
        strides.insert(0, total)
        total *= size

    def numbers(axes):
        values = [0]
        for axis in axes:
            values = [v + i * strides[axis] for v in values for i in range(sizes[axis])]
        return values

    apart = [axis for axis in range(len(sizes)) if axis not in together]
    return [[base + v for v in numbers(together)] for base in numbers(apart)]


def reduce_all(packed):
    axes = ("dom", "tile")
    sizes = (4, 16, 2, 4)
    near = member_groups(sizes, (0, 2, 3))
    far = member_groups(sizes, (1,))

    def trade(array, groups):
        return lax.all_to_all(array, axes, 0, 0, axis_index_groups=groups, tiled=True)

    n, m = len(near[0]), len(far[0])
    mine = jnp.sum(trade(packed.reshape(n, -1, LANE), near), axis=0)
    mine = jnp.sum(trade(jnp.broadcast_to(mine[None], (m,) + mine.shape), far), axis=0)
    return trade(jnp.broadcast_to(mine[None], (n,) + mine.shape), near).reshape(packed.shape)


def shards(pumping, coupling, storage, tile_order, kriging):
    groups = lax.axis_size("dom")
    cell_total = storage.shape[0] * CB * groups * lax.axis_size("tile")
    scratch = lambda rows: pltpu.VMEM((rows, LANE), F32)
    p, sh, sl, u, *edges = call(
        first_kernel,
        (FIELD, ((FX * LANE, LANE), BF16), ((FX * LANE, LANE), BF16), FIELD) + EDGES,
        pltpu.with_memory_space_constraint(pumping, pltpu.HBM),
        pltpu.with_memory_space_constraint(coupling, pltpu.HBM),
        scratch=(
            pltpu.VMEM((16, RHS * CB), F32),
            pltpu.VMEM((16, CB * CB), F32),
            scratch(ROWS),
            scratch(ROWS),
            scratch(FX * LANE),
            pltpu.SemaphoreType.DMA((2, PIECES)),
        ),
        place=pltpu.HBM,
    )
    halo = exchange(*edges)
    ap, u, *edges = call(second_kernel, (FIELD, FIELD) + EDGES, p, u, sh, sl, storage, *halo)
    halo = exchange(*edges)
    (base,) = call(base_kernel, (((2 * RHS, LANE), F32),), p, ap)
    (packed,) = call(
        third_kernel, (((2 * RHS, LANE), F32),), ap, u, sh, sl, storage, *halo, base
    )
    (cells,) = call(
        deal_kernel,
        (((FX * LANE, 4 * RHS), BF16),),
        *(tile_order, p, ap),
        scratch=(pltpu.VMEM((4 * RHS, FX * LANE), BF16),),
        flops=LONG,
    )
    packed = reduce_all(packed)
    heads, scale, weights, later = call(
        lambda *refs: solve_kernel(cell_total, *refs),
        (((FX * LANE // 2, LANE), F32), ((1, RHS), F32), ((2 * RHS, RHS), F32), ((RHS, LANE), F32)),
        *(packed, cells),
        scratch=(scratch(FX * LANE),),
    )
    heads = heads.astype(jnp.float16).reshape(groups, -1, LANE)
    heads = lax.all_to_all(heads, "dom", 0, 0, tiled=True).reshape(-1, LANE).astype(F32)
    gram, kriging = call(
        lambda *refs: gram_kernel(cell_total, *refs),
        (((RHS, RHS), F32), ((2 * PILOT, FX * LANE // 2), BF16)),
        *(packed, weights, later, kriging),
        flops=LONG,
    )
    (sens,) = call(
        product_kernel,
        (((PILOT, RHS), F32),),
        *(kriging, heads, scale),
    )
    return sens, gram


def solution(mesh):
    spec = P(("dom", "tile"), None)
    return jax.shard_map(
        shards, mesh=mesh, in_specs=(spec,) * 5, out_specs=(spec, P()), check_vma=False
    )
```

```python
import jax
import jax.numpy as jnp
from jax import lax
from jax.experimental import pallas as pl
from jax.experimental.pallas import tpu as pltpu
from jax.sharding import PartitionSpec as P

RHS = 64
CB = 64
FX = 8
PILOT = 16
N_TILE = 4
LANE = 128
ROWS = FX * RHS
F32 = jnp.float32
BF16 = jnp.bfloat16
HIGHEST = lax.Precision.HIGHEST
PARAMS = pltpu.CompilerParams(vmem_limit_bytes=40 * 1024 * 1024)
PIECES = 4
WIDTH = RHS * CB // PIECES
LONG = 10**11
NN = (((1,), (0,)), ((), ()))
NT = (((1,), (1,)), ((), ()))


def split(value):
    high = value.astype(BF16)
    return high, (value - high.astype(F32)).astype(BF16)


def dot(left, right, dims):
    return lax.dot_general(left, right, dims, preferred_element_type=F32)


def dot3(left, right, dims):
    (lh, ll), (rh, rl) = left, right
    return dot(lh, rh, dims) + (dot(ll, rh, dims) + dot(lh, rl, dims))


def exact(left, right, dims=NN):
    return lax.dot_general(left, right, dims, precision=HIGHEST, preferred_element_type=F32)


def low_lanes(rows):
    return lax.broadcasted_iota(jnp.int32, (rows, LANE), 1) < CB


def swap(value):
    return pltpu.roll(value, CB, 1)


def part(x):
    return pl.ds(x * RHS, RHS)


def is_even(axis):
    return lax.rem(lax.axis_index(axis), 2) == 0


def by_parity(axis, first, second):
    even = is_even(axis)
    return jnp.where(even, first, second), jnp.where(even, second, first)


def slot(step):
    return lax.rem(lax.axis_index("tile") + step, N_TILE)


def write_edges(spread, d1, d2, t):
    low = low_lanes(RHS)
    one, two = by_parity("dom", spread[FX - 1], spread[0])
    d1[...] = one.astype(BF16)
    d2[:RHS, :] = two.astype(BF16)
    d2[RHS:, :] = jnp.zeros((d2.shape[0] - RHS, LANE), BF16)
    for step in (0, 2):
        t[slot(step)] = jnp.zeros((ROWS // 2, LANE), BF16)
    for i in range(FX // 2):
        even, odd = spread[2 * i], spread[2 * i + 1]
        t[slot(1), part(i), :] = jnp.where(low, swap(even), odd).astype(BF16)
        t[slot(3), part(i), :] = jnp.where(low, even, swap(odd)).astype(BF16)


def first_kernel(pump_hbm, coup_hbm, p_out, sh_out, sl_out, u_out, d1, d2, t, pump, coup, rows_p, rows_s, mats, arrived):
    copies = []
    for source, target, order in ((pump_hbm, pump, 0), (coup_hbm, coup, 1)):
        for i in range(PIECES):
            columns = pl.ds(i * WIDTH, WIDTH)
            copies.append(
                pltpu.make_async_copy(source.at[:, columns], target.at[:, columns], arrived.at[order, i])
            )
            copies[-1].start()
    for i, copy in enumerate(copies):
        source, target = (pump, rows_p) if i < PIECES else (coup, rows_s)
        copy.wait()
        chunks = WIDTH // LANE
        for k in range(i % PIECES * chunks, (i % PIECES + 1) * chunks):
            target[pl.ds(k, 16, stride=32), :] = source[:, k * LANE : (k + 1) * LANE]
    low = low_lanes(32)
    zero = jnp.zeros((32, LANE), F32)
    for x in range(FX):
        a0, a1 = rows_p[pl.ds(x * 64, 32), :], rows_p[pl.ds(x * 64 + 32, 32), :]
        p_out[pl.ds(x * 64, 32, stride=2), :] = jnp.where(low, a0, swap(a1))
        p_out[pl.ds(x * 64 + 1, 32, stride=2), :] = jnp.where(low, swap(a0), a1)
        s0, s1 = rows_s[pl.ds(x * 64, 32), :], rows_s[pl.ds(x * 64 + 32, 32), :]
        mats[pl.ds(x * 128, 32, stride=2), :] = jnp.where(low, s0, zero)
        mats[pl.ds(x * 128 + 1, 32, stride=2), :] = jnp.where(low, swap(s0), zero)
        mats[pl.ds(x * 128 + 64, 32, stride=2), :] = jnp.where(low, zero, swap(s1))
        mats[pl.ds(x * 128 + 65, 32, stride=2), :] = jnp.where(low, zero, s1)
    spread = []
    for x in range(FX):
        block = pl.ds(x * LANE, LANE)
        high, rest = split(mats[block, :])
        sh_out[block, :] = high
        sl_out[block, :] = rest
        u = dot3(split(p_out[part(x), :]), (high, rest), NN)
        u_out[part(x), :] = u
        spread.append(u)
    write_edges(spread, d1, d2, t)


def operator(v, u, sh, sl, stor, d1, d2, t):
    low = low_lanes(RHS)
    spread = [u[part(x), :] for x in range(FX)]
    after, before = by_parity("dom", d1[...].astype(F32), d2[:RHS, :].astype(F32))
    ends = [before] + spread + [after]
    right, left = [], []
    for i in range(FX // 2):
        there = t[slot(1), part(i), :].astype(F32)
        here = t[slot(3), part(i), :].astype(F32)
        place = lax.axis_index("tile")
        right.append(jnp.where(place < N_TILE - 1, there, jnp.zeros_like(there)))
        left.append(jnp.where(place > 0, here, jnp.zeros_like(here)))
    applied = []
    for x in range(FX):
        from_left, from_right = left[x // 2], right[x // 2]
        if x % 2 == 0:
            outside = jnp.where(low, from_left, swap(from_right))
        else:
            outside = jnp.where(low, swap(from_left), from_right)
        pulled = 4.0 * spread[x] - (ends[x] + ends[x + 2] + swap(spread[x]) + outside)
        block = pl.ds(x * LANE, LANE)
        capacity = jnp.concatenate([stor[2 * x : 2 * x + 1, :], stor[2 * x + 1 : 2 * x + 2, :]], axis=1)
        applied.append(
            capacity * v[part(x), :] + dot3(split(pulled), (sh[block, :], sl[block, :]), NT)
        )
    return applied


def second_kernel(v, u, sh, sl, stor, d1, d2, t, ap_out, u_out, *edges):
    applied = operator(v, u, sh, sl, stor, d1, d2, t)
    spread = []
    for x in range(FX):
        ap_out[part(x), :] = applied[x]
        block = pl.ds(x * LANE, LANE)
        s = dot3(split(applied[x]), (sh[block, :], sl[block, :]), NN)
        u_out[part(x), :] = s
        spread.append(s)
    write_edges(spread, *edges)


def deal_kernel(order, v, ap, kriging, cells, kept, table):
    count = kriging.shape[1]
    source = lax.broadcasted_iota(jnp.int32, (count, count // 2), 0)
    target = lax.broadcasted_iota(jnp.int32, (count, count // 2), 1)
    for parity in range(2):
        pick = jnp.where(source == 2 * target + parity, 1.0, 0.0).astype(BF16)
        kept[pl.ds(parity * PILOT, PILOT), :] = dot(kriging[...], pick, NN).astype(BF16)
    for x in range(FX):
        high, rest = split(jnp.concatenate([v[part(x), :], ap[part(x), :]], axis=0))
        table[: 2 * RHS, x * LANE : (x + 1) * LANE] = high
        table[2 * RHS :, x * LANE : (x + 1) * LANE] = rest
    lane = lax.broadcasted_iota(jnp.int32, (LANE, LANE), 1)
    for g in range(FX):
        row = jnp.broadcast_to(order[:, g * LANE : (g + 1) * LANE], (LANE, LANE))
        wanted = jnp.transpose(row)
        picks = [
            jnp.where(wanted == lane + l * LANE, 1.0, 0.0).astype(BF16) for l in range(FX)
        ]
        cells[pl.ds(g * LANE, LANE), :] = dot(
            jnp.concatenate(picks, axis=1), table[...], NT
        ).astype(BF16)


def base_kernel(p, v, base):
    total = jnp.zeros((2 * RHS, 2 * RHS), F32)
    for x in range(FX):
        both = split(jnp.concatenate([p[part(x), :], v[part(x), :]], axis=0))
        total += dot3(both, both, NT)
    base[...] = total


def third_kernel(v, u, sh, sl, stor, d1, d2, t, base, packed):
    applied = operator(v, u, sh, sl, stor, d1, d2, t)
    total = jnp.zeros((2 * RHS, RHS), F32)
    for x in range(FX):
        image = split(applied[x])
        both = [jnp.concatenate([a, b], axis=0) for a, b in zip(split(v[part(x), :]), image)]
        total += dot3(both, image, NT)
    m0, m1, m2 = base[:RHS, :RHS], base[:RHS, RHS:], base[RHS:, RHS:]
    m1 = symmetric(m1)
    m3 = symmetric(total[:RHS])
    m4 = total[RHS:]
    row, column = square_index()
    upper = row <= column
    packed[:RHS, :] = jnp.concatenate([jnp.where(upper, m0, m2), jnp.where(upper, m1, m3)], axis=1)
    ends = jnp.where(row == 0, diagonal(m2), jnp.where(row == 1, diagonal(m3), 0.0))
    packed[RHS:, :] = jnp.concatenate([m4, ends], axis=1)


def square_index():
    return [lax.broadcasted_iota(jnp.int32, (RHS, RHS), d) for d in (0, 1)]


def diagonal(matrix):
    row, column = square_index()
    return jnp.sum(jnp.where(row == column, matrix, 0.0), axis=0, keepdims=True)


def column_diagonal(matrix):
    row, column = square_index()
    return jnp.sum(jnp.where(row == column, matrix, 0.0), axis=1, keepdims=True)


def unpack_pair(matrix, ends):
    row, column = square_index()
    turned = jnp.transpose(matrix)
    first = jnp.where(row <= column, matrix, turned)
    second = jnp.where(row > column, matrix, jnp.where(row < column, turned, ends))
    return first, second


def eliminate(joined, panel=8):
    order, width = joined.shape
    parts = [joined[g : g + panel, :] for g in range(0, order, panel)]
    index = lax.broadcasted_iota(jnp.int32, (panel, width), 0)

    def wide(value):
        pieces = [value] * (width // LANE)
        if width % LANE:
            pieces.append(value[:, : width % LANE])
        return jnp.concatenate(pieces, axis=1) if len(pieces) > 1 else value

    def apply(rows, at, c0, c1, inverse, where):
        r0, r1 = rows[at : at + 1, :], rows[at + 1 : at + 2, :]
        s0 = inverse[0] * r0 + inverse[1] * r1
        s1 = inverse[2] * r0 + inverse[3] * r1
        rest = rows - (c0 * s0 + c1 * s1)
        return jnp.where(where == at, s0, jnp.where(where == at + 1, s1, rest))

    for g in range(len(parts)):
        rows = parts[g]
        first = g * panel
        columns = [
            jnp.broadcast_to(rows[:, first + q : first + q + 1], (panel, LANE)) for q in range(panel)
        ]
        for at in range(0, panel, 2):
            c0, c1 = columns[at], columns[at + 1]
            a, c = c0[at : at + 1, :], c0[at + 1 : at + 2, :]
            b, d = c1[at : at + 1, :], c1[at + 1 : at + 2, :]
            scale = 1.0 / (a * d - b * c)
            inverse = (d * scale, -b * scale, -c * scale, a * scale)
            for q in range(at + 2, panel):
                columns[q] = apply(columns[q], at, c0, c1, inverse, index[:, :LANE])
            rows = apply(rows, at, wide(c0), wide(c1), [wide(v) for v in inverse], index)
        parts[g] = rows
        for h in range(len(parts)):
            if h != g:
                taken = None
                for q in range(panel):
                    column = jnp.broadcast_to(parts[h][:, first + q : first + q + 1], (panel, width))
                    term = column * rows[q : q + 1, :]
                    taken = term if taken is None else taken + term
                parts[h] = parts[h] - taken
    return jnp.concatenate(parts, axis=0)[:, order:]


def symmetric(matrix):
    return 0.5 * (matrix + jnp.transpose(matrix))


def solve_kernel(cell_total, packed, cells, heads, scale, weights, later, rows):
    m0, m2 = unpack_pair(packed[:RHS, :RHS], packed[RHS : RHS + 1, RHS:])
    m1, m3 = unpack_pair(packed[:RHS, RHS:], packed[RHS + 1 : RHS + 2, RHS:])
    first = eliminate(jnp.concatenate([m1, m0, m2], axis=1))
    alpha, shift = first[:, :RHS], first[:, RHS:]
    bent = exact(m2, first)
    curved = symmetric(m3 - bent[:, RHS:])
    target = m1 - bent[:, :RHS]
    gamma = eliminate(jnp.concatenate([curved, target], axis=1))
    mixed = alpha - exact(shift, gamma)
    both = jnp.concatenate([mixed, gamma], axis=0)
    spread = jnp.concatenate([column_diagonal(m0), column_diagonal(m2)], axis=0)
    bound = jnp.sum(jnp.abs(both) * jnp.sqrt(spread * (1.0 / cell_total)), axis=0, keepdims=True)
    bound = jnp.where(bound > 0.0, bound, 1.0)
    scale[...] = bound
    high, rest = split(jnp.concatenate([both / bound, both / bound], axis=1))
    value = dot3((cells[:, :LANE], cells[:, LANE:]), (high, rest), NN)
    rows[...] = value
    half = FX * LANE // 2
    even, odd = rows[pl.ds(0, half, stride=2), :], rows[pl.ds(1, half, stride=2), :]
    heads[...] = jnp.where(low_lanes(half), even, odd)
    weights[...] = both
    later[...] = jnp.concatenate([m2, m3], axis=1)


def product_kernel(cell_total, kriging, arrived, scale, packed, weights, later, sens, gram):
    high, rest = split(arrived[...])
    product = dot(kriging[...], high, NN) + dot(kriging[...], rest, NN)
    sens[...] = (product[:PILOT, :RHS] + product[PILOT:, RHS:]) * scale[...]
    mixed, gamma = weights[:RHS, :], weights[RHS:, :]
    rest = exact(packed[RHS:, :RHS], gamma) + exact(later[:, RHS:], mixed) - later[:, :RHS]
    gram[...] = symmetric(exact(jnp.transpose(gamma), rest)) * (1.0 / cell_total)


def call(kernel, shapes, *operands, scratch=(), flops=1000000, place=pltpu.VMEM):
    return pl.pallas_call(
        kernel,
        out_shape=[jax.ShapeDtypeStruct(shape, kind) for shape, kind in shapes],
        in_specs=[pl.BlockSpec(memory_space=place)] * len(operands),
        out_specs=[pl.BlockSpec(memory_space=pltpu.VMEM)] * len(shapes),
        scratch_shapes=list(scratch),
        compiler_params=PARAMS,
        cost_estimate=pl.CostEstimate(flops=flops, bytes_accessed=1 << 20, transcendentals=0),
    )(*operands)


EDGES = (((RHS, LANE), BF16), ((RHS + 16, LANE), BF16), ((N_TILE, ROWS // 2, LANE), BF16))
FIELD = ((ROWS, LANE), F32)


def exchange(d1, d2, t):
    devices = lax.axis_size("dom")
    first = [(i, i ^ 1) for i in range(devices)]
    second = [(i, ((i + 1) ^ 1) - 1) for i in range(1, devices - 1)]
    t = lax.all_to_all(t, "tile", 0, 0, tiled=True)
    d2 = lax.ppermute(d2, "dom", second)
    return lax.ppermute(d1, "dom", first), d2, t


def member_groups(sizes, together):
    strides, total = [], 1
    for size in reversed(sizes):
        strides.insert(0, total)
        total *= size

    def numbers(axes):
        values = [0]
        for axis in axes:
            values = [v + i * strides[axis] for v in values for i in range(sizes[axis])]
        return values

    apart = [axis for axis in range(len(sizes)) if axis not in together]
    return [[base + v for v in numbers(together)] for base in numbers(apart)]


def reduce_all(packed):
    axes = ("dom", "tile")
    sizes = (4, 16, 2, 4)
    near = member_groups(sizes, (0, 2, 3))
    far = member_groups(sizes, (1,))

    def trade(array, groups):
        return lax.all_to_all(array, axes, 0, 0, axis_index_groups=groups, tiled=True)

    n, m = len(near[0]), len(far[0])
    mine = jnp.sum(trade(packed.reshape(n, -1, LANE), near), axis=0)
    mine = jnp.sum(trade(jnp.broadcast_to(mine[None], (m,) + mine.shape), far), axis=0)
    return trade(jnp.broadcast_to(mine[None], (n,) + mine.shape), near).reshape(packed.shape)


def shards(pumping, coupling, storage, tile_order, kriging):
    groups = lax.axis_size("dom")
    cell_total = storage.shape[0] * CB * groups * lax.axis_size("tile")
    scratch = lambda rows: pltpu.VMEM((rows, LANE), F32)
    p, sh, sl, u, *edges = call(
        first_kernel,
        (FIELD, ((FX * LANE, LANE), BF16), ((FX * LANE, LANE), BF16), FIELD) + EDGES,
        pltpu.with_memory_space_constraint(pumping, pltpu.HBM),
        pltpu.with_memory_space_constraint(coupling, pltpu.HBM),
        scratch=(
            pltpu.VMEM((16, RHS * CB), F32),
            pltpu.VMEM((16, CB * CB), F32),
            scratch(ROWS),
            scratch(ROWS),
            scratch(FX * LANE),
            pltpu.SemaphoreType.DMA((2, PIECES)),
        ),
        place=pltpu.HBM,
    )
    halo = exchange(*edges)
    ap, u, *edges = call(second_kernel, (FIELD, FIELD) + EDGES, p, u, sh, sl, storage, *halo)
    halo = exchange(*edges)
    (base,) = call(base_kernel, (((2 * RHS, LANE), F32),), p, ap)
    (packed,) = call(
        third_kernel, (((2 * RHS, LANE), F32),), ap, u, sh, sl, storage, *halo, base
    )
    cells, kriging = call(
        deal_kernel,
        (((FX * LANE, 4 * RHS), BF16), ((2 * PILOT, FX * LANE // 2), BF16)),
        *(tile_order, p, ap, kriging),
        scratch=(pltpu.VMEM((4 * RHS, FX * LANE), BF16),),
        flops=LONG,
    )
    packed = reduce_all(packed)
    heads, scale, weights, later = call(
        lambda *refs: solve_kernel(cell_total, *refs),
        (((FX * LANE // 2, LANE), F32), ((1, RHS), F32), ((2 * RHS, RHS), F32), ((RHS, LANE), F32)),
        *(packed, cells),
        scratch=(scratch(FX * LANE),),
    )
    heads = heads.astype(jnp.float16).reshape(groups, -1, LANE)
    heads = lax.all_to_all(heads, "dom", 0, 0, tiled=True).reshape(-1, LANE).astype(F32)
    sens, gram = call(
        lambda *refs: product_kernel(cell_total, *refs),
        (((PILOT, RHS), F32), ((RHS, RHS), F32)),
        *(kriging, heads, scale, packed, weights, later),
    )
    return sens, gram


def solution(mesh):
    spec = P(("dom", "tile"), None)
    return jax.shard_map(
        shards, mesh=mesh, in_specs=(spec,) * 5, out_specs=(spec, P()), check_vma=False
    )
```

```python
import jax
import jax.numpy as jnp
from jax import lax
from jax.experimental import pallas as pl
from jax.experimental.pallas import tpu as pltpu
from jax.sharding import PartitionSpec as P

RHS = 64
CB = 64
FX = 8
PILOT = 16
LANE = 128
ROWS = FX * RHS
F32 = jnp.float32
BF16 = jnp.bfloat16
HIGHEST = lax.Precision.HIGHEST
PARAMS = pltpu.CompilerParams(vmem_limit_bytes=40 * 1024 * 1024)
PIECES = 4
WIDTH = RHS * CB // PIECES
LONG = 10**11
NN = (((1,), (0,)), ((), ()))
NT = (((1,), (1,)), ((), ()))


def split(value):
    high = value.astype(BF16)
    return high, (value - high.astype(F32)).astype(BF16)


def dot(left, right, dims):
    return lax.dot_general(left, right, dims, preferred_element_type=F32)


def dot3(left, right, dims):
    (lh, ll), (rh, rl) = left, right
    return dot(lh, rh, dims) + (dot(ll, rh, dims) + dot(lh, rl, dims))


def exact(left, right, dims=NN):
    return lax.dot_general(left, right, dims, precision=HIGHEST, preferred_element_type=F32)


def low_lanes(rows):
    return lax.broadcasted_iota(jnp.int32, (rows, LANE), 1) < CB


def swap(value):
    return pltpu.roll(value, CB, 1)


def part(x):
    return pl.ds(x * RHS, RHS)


def is_even(axis):
    return lax.rem(lax.axis_index(axis), 2) == 0


def by_parity(axis, first, second):
    even = is_even(axis)
    return jnp.where(even, first, second), jnp.where(even, second, first)


def write_edges(spread, d1, d2, t1, t2):
    low = low_lanes(RHS)
    one, two = by_parity("dom", spread[FX - 1], spread[0])
    d1[...] = one.astype(BF16)
    d2[:RHS, :] = two.astype(BF16)
    d2[RHS:, :] = jnp.zeros((d2.shape[0] - RHS, LANE), BF16)
    for i in range(FX // 2):
        even, odd = spread[2 * i], spread[2 * i + 1]
        left = jnp.where(low, even, swap(odd))
        right = jnp.where(low, swap(even), odd)
        one, two = by_parity("tile", right, left)
        t1[part(i), :] = one.astype(BF16)
        t2[part(i), :] = two.astype(BF16)


def first_kernel(pump_hbm, coup_hbm, p_out, sh_out, sl_out, u_out, d1, d2, t1, t2, pump, coup, rows_p, rows_s, mats, arrived):
    copies = []
    for source, target, order in ((pump_hbm, pump, 0), (coup_hbm, coup, 1)):
        for i in range(PIECES):
            columns = pl.ds(i * WIDTH, WIDTH)
            copies.append(
                pltpu.make_async_copy(source.at[:, columns], target.at[:, columns], arrived.at[order, i])
            )
            copies[-1].start()
    for i, copy in enumerate(copies):
        source, target = (pump, rows_p) if i < PIECES else (coup, rows_s)
        copy.wait()
        chunks = WIDTH // LANE
        for k in range(i % PIECES * chunks, (i % PIECES + 1) * chunks):
            target[pl.ds(k, 16, stride=32), :] = source[:, k * LANE : (k + 1) * LANE]
    low = low_lanes(32)
    zero = jnp.zeros((32, LANE), F32)
    for x in range(FX):
        a0, a1 = rows_p[pl.ds(x * 64, 32), :], rows_p[pl.ds(x * 64 + 32, 32), :]
        p_out[pl.ds(x * 64, 32, stride=2), :] = jnp.where(low, a0, swap(a1))
        p_out[pl.ds(x * 64 + 1, 32, stride=2), :] = jnp.where(low, swap(a0), a1)
        s0, s1 = rows_s[pl.ds(x * 64, 32), :], rows_s[pl.ds(x * 64 + 32, 32), :]
        mats[pl.ds(x * 128, 32, stride=2), :] = jnp.where(low, s0, zero)
        mats[pl.ds(x * 128 + 1, 32, stride=2), :] = jnp.where(low, swap(s0), zero)
        mats[pl.ds(x * 128 + 64, 32, stride=2), :] = jnp.where(low, zero, swap(s1))
        mats[pl.ds(x * 128 + 65, 32, stride=2), :] = jnp.where(low, zero, s1)
    spread = []
    for x in range(FX):
        block = pl.ds(x * LANE, LANE)
        high, rest = split(mats[block, :])
        sh_out[block, :] = high
        sl_out[block, :] = rest
        u = dot3(split(p_out[part(x), :]), (high, rest), NN)
        u_out[part(x), :] = u
        spread.append(u)
    write_edges(spread, d1, d2, t1, t2)


def operator(v, u, sh, sl, stor, d1, d2, t1, t2):
    low = low_lanes(RHS)
    spread = [u[part(x), :] for x in range(FX)]
    after, before = by_parity("dom", d1[...].astype(F32), d2[:RHS, :].astype(F32))
    ends = [before] + spread + [after]
    right, left = [], []
    for i in range(FX // 2):
        one, two = by_parity("tile", t1[part(i), :].astype(F32), t2[part(i), :].astype(F32))
        right.append(one)
        left.append(two)
    applied = []
    for x in range(FX):
        from_left, from_right = left[x // 2], right[x // 2]
        if x % 2 == 0:
            outside = jnp.where(low, from_left, swap(from_right))
        else:
            outside = jnp.where(low, swap(from_left), from_right)
        pulled = 4.0 * spread[x] - (ends[x] + ends[x + 2] + swap(spread[x]) + outside)
        block = pl.ds(x * LANE, LANE)
        capacity = jnp.concatenate([stor[2 * x : 2 * x + 1, :], stor[2 * x + 1 : 2 * x + 2, :]], axis=1)
        applied.append(
            capacity * v[part(x), :] + dot3(split(pulled), (sh[block, :], sl[block, :]), NT)
        )
    return applied


def second_kernel(v, u, sh, sl, stor, d1, d2, t1, t2, ap_out, u_out, *edges):
    applied = operator(v, u, sh, sl, stor, d1, d2, t1, t2)
    spread = []
    for x in range(FX):
        ap_out[part(x), :] = applied[x]
        block = pl.ds(x * LANE, LANE)
        s = dot3(split(applied[x]), (sh[block, :], sl[block, :]), NN)
        u_out[part(x), :] = s
        spread.append(s)
    write_edges(spread, *edges)


def deal_kernel(order, v, ap, kriging, cells, kept, table):
    count = kriging.shape[1]
    source = lax.broadcasted_iota(jnp.int32, (count, count // 2), 0)
    target = lax.broadcasted_iota(jnp.int32, (count, count // 2), 1)
    for parity in range(2):
        pick = jnp.where(source == 2 * target + parity, 1.0, 0.0).astype(BF16)
        kept[pl.ds(parity * PILOT, PILOT), :] = dot(kriging[...], pick, NN).astype(BF16)
    for x in range(FX):
        high, rest = split(jnp.concatenate([v[part(x), :], ap[part(x), :]], axis=0))
        table[: 2 * RHS, x * LANE : (x + 1) * LANE] = high
        table[2 * RHS :, x * LANE : (x + 1) * LANE] = rest
    lane = lax.broadcasted_iota(jnp.int32, (LANE, LANE), 1)
    for g in range(FX):
        row = jnp.broadcast_to(order[:, g * LANE : (g + 1) * LANE], (LANE, LANE))
        wanted = jnp.transpose(row)
        picks = [
            jnp.where(wanted == lane + l * LANE, 1.0, 0.0).astype(BF16) for l in range(FX)
        ]
        cells[pl.ds(g * LANE, LANE), :] = dot(
            jnp.concatenate(picks, axis=1), table[...], NT
        ).astype(BF16)


def base_kernel(p, v, base):
    total = jnp.zeros((2 * RHS, 2 * RHS), F32)
    for x in range(FX):
        both = split(jnp.concatenate([p[part(x), :], v[part(x), :]], axis=0))
        total += dot3(both, both, NT)
    base[...] = total


def third_kernel(v, u, sh, sl, stor, d1, d2, t1, t2, base, packed):
    applied = operator(v, u, sh, sl, stor, d1, d2, t1, t2)
    total = jnp.zeros((2 * RHS, RHS), F32)
    for x in range(FX):
        image = split(applied[x])
        both = [jnp.concatenate([a, b], axis=0) for a, b in zip(split(v[part(x), :]), image)]
        total += dot3(both, image, NT)
    m0, m1, m2 = base[:RHS, :RHS], base[:RHS, RHS:], base[RHS:, RHS:]
    m1 = symmetric(m1)
    m3 = symmetric(total[:RHS])
    m4 = total[RHS:]
    row, column = square_index()
    upper = row <= column
    packed[:RHS, :] = jnp.concatenate([jnp.where(upper, m0, m2), jnp.where(upper, m1, m3)], axis=1)
    ends = jnp.where(row == 0, diagonal(m2), jnp.where(row == 1, diagonal(m3), 0.0))
    packed[RHS:, :] = jnp.concatenate([m4, ends], axis=1)


def square_index():
    return [lax.broadcasted_iota(jnp.int32, (RHS, RHS), d) for d in (0, 1)]


def diagonal(matrix):
    row, column = square_index()
    return jnp.sum(jnp.where(row == column, matrix, 0.0), axis=0, keepdims=True)


def column_diagonal(matrix):
    row, column = square_index()
    return jnp.sum(jnp.where(row == column, matrix, 0.0), axis=1, keepdims=True)


def unpack_pair(matrix, ends):
    row, column = square_index()
    turned = jnp.transpose(matrix)
    first = jnp.where(row <= column, matrix, turned)
    second = jnp.where(row > column, matrix, jnp.where(row < column, turned, ends))
    return first, second


def eliminate(joined, panel=8):
    order, width = joined.shape
    parts = [joined[g : g + panel, :] for g in range(0, order, panel)]
    index = lax.broadcasted_iota(jnp.int32, (panel, width), 0)

    def wide(value):
        pieces = [value] * (width // LANE)
        if width % LANE:
            pieces.append(value[:, : width % LANE])
        return jnp.concatenate(pieces, axis=1) if len(pieces) > 1 else value

    def apply(rows, at, c0, c1, inverse, where):
        r0, r1 = rows[at : at + 1, :], rows[at + 1 : at + 2, :]
        s0 = inverse[0] * r0 + inverse[1] * r1
        s1 = inverse[2] * r0 + inverse[3] * r1
        rest = rows - (c0 * s0 + c1 * s1)
        return jnp.where(where == at, s0, jnp.where(where == at + 1, s1, rest))

    for g in range(len(parts)):
        rows = parts[g]
        first = g * panel
        columns = [
            jnp.broadcast_to(rows[:, first + q : first + q + 1], (panel, LANE)) for q in range(panel)
        ]
        for at in range(0, panel, 2):
            c0, c1 = columns[at], columns[at + 1]
            a, c = c0[at : at + 1, :], c0[at + 1 : at + 2, :]
            b, d = c1[at : at + 1, :], c1[at + 1 : at + 2, :]
            scale = 1.0 / (a * d - b * c)
            inverse = (d * scale, -b * scale, -c * scale, a * scale)
            for q in range(at + 2, panel):
                columns[q] = apply(columns[q], at, c0, c1, inverse, index[:, :LANE])
            rows = apply(rows, at, wide(c0), wide(c1), [wide(v) for v in inverse], index)
        parts[g] = rows
        for h in range(len(parts)):
            if h != g:
                taken = None
                for q in range(panel):
                    column = jnp.broadcast_to(parts[h][:, first + q : first + q + 1], (panel, width))
                    term = column * rows[q : q + 1, :]
                    taken = term if taken is None else taken + term
                parts[h] = parts[h] - taken
    return jnp.concatenate(parts, axis=0)[:, order:]


def symmetric(matrix):
    return 0.5 * (matrix + jnp.transpose(matrix))


def solve_kernel(cell_total, packed, cells, heads, scale, weights, later, rows):
    m0, m2 = unpack_pair(packed[:RHS, :RHS], packed[RHS : RHS + 1, RHS:])
    m1, m3 = unpack_pair(packed[:RHS, RHS:], packed[RHS + 1 : RHS + 2, RHS:])
    first = eliminate(jnp.concatenate([m1, m0, m2], axis=1))
    alpha, shift = first[:, :RHS], first[:, RHS:]
    bent = exact(m2, first)
    curved = symmetric(m3 - bent[:, RHS:])
    target = m1 - bent[:, :RHS]
    gamma = eliminate(jnp.concatenate([curved, target], axis=1))
    mixed = alpha - exact(shift, gamma)
    both = jnp.concatenate([mixed, gamma], axis=0)
    spread = jnp.concatenate([column_diagonal(m0), column_diagonal(m2)], axis=0)
    bound = jnp.sum(jnp.abs(both) * jnp.sqrt(spread * (1.0 / cell_total)), axis=0, keepdims=True)
    bound = jnp.where(bound > 0.0, bound, 1.0)
    scale[...] = bound
    high, rest = split(jnp.concatenate([both / bound, both / bound], axis=1))
    value = dot3((cells[:, :LANE], cells[:, LANE:]), (high, rest), NN)
    rows[...] = value
    half = FX * LANE // 2
    even, odd = rows[pl.ds(0, half, stride=2), :], rows[pl.ds(1, half, stride=2), :]
    heads[...] = jnp.where(low_lanes(half), even, odd)
    weights[...] = both
    later[...] = jnp.concatenate([m2, m3], axis=1)


def product_kernel(cell_total, kriging, arrived, scale, packed, weights, later, sens, gram):
    high, rest = split(arrived[...])
    product = dot(kriging[...], high, NN) + dot(kriging[...], rest, NN)
    sens[...] = (product[:PILOT, :RHS] + product[PILOT:, RHS:]) * scale[...]
    mixed, gamma = weights[:RHS, :], weights[RHS:, :]
    rest = exact(packed[RHS:, :RHS], gamma) + exact(later[:, RHS:], mixed) - later[:, :RHS]
    gram[...] = symmetric(exact(jnp.transpose(gamma), rest)) * (1.0 / cell_total)


def call(kernel, shapes, *operands, scratch=(), flops=1000000, place=pltpu.VMEM):
    return pl.pallas_call(
        kernel,
        out_shape=[jax.ShapeDtypeStruct(shape, kind) for shape, kind in shapes],
        in_specs=[pl.BlockSpec(memory_space=place)] * len(operands),
        out_specs=[pl.BlockSpec(memory_space=pltpu.VMEM)] * len(shapes),
        scratch_shapes=list(scratch),
        compiler_params=PARAMS,
        cost_estimate=pl.CostEstimate(flops=flops, bytes_accessed=1 << 20, transcendentals=0),
    )(*operands)


EDGES = (((RHS, LANE), BF16), ((ROWS // 2 + 16, LANE), BF16), ((ROWS // 2, LANE), BF16), ((ROWS // 2, LANE), BF16))
FIELD = ((ROWS, LANE), F32)


def exchange(d1, d2, t1, t2):
    def along(axis, one, two):
        devices = lax.axis_size(axis)
        first = [(i, i ^ 1) for i in range(devices)]
        second = [(i, ((i + 1) ^ 1) - 1) for i in range(1, devices - 1)]
        two = lax.ppermute(two, axis, second)
        return lax.ppermute(one, axis, first), two

    t1, t2 = along("tile", t1, t2)
    d1, d2 = along("dom", d1, d2)
    return d1, d2, t1, t2


def member_groups(sizes, together):
    strides, total = [], 1
    for size in reversed(sizes):
        strides.insert(0, total)
        total *= size

    def numbers(axes):
        values = [0]
        for axis in axes:
            values = [v + i * strides[axis] for v in values for i in range(sizes[axis])]
        return values

    apart = [axis for axis in range(len(sizes)) if axis not in together]
    return [[base + v for v in numbers(together)] for base in numbers(apart)]


def reduce_all(packed):
    axes = ("dom", "tile")
    sizes = (4, 16, 2, 4)
    near = member_groups(sizes, (0, 2, 3))
    far = member_groups(sizes, (1,))

    def trade(array, groups):
        return lax.all_to_all(array, axes, 0, 0, axis_index_groups=groups, tiled=True)

    n, m = len(near[0]), len(far[0])
    mine = jnp.sum(trade(packed.reshape(n, -1, LANE), near), axis=0)
    mine = jnp.sum(trade(jnp.broadcast_to(mine[None], (m,) + mine.shape), far), axis=0)
    return trade(jnp.broadcast_to(mine[None], (n,) + mine.shape), near).reshape(packed.shape)


def shards(pumping, coupling, storage, tile_order, kriging):
    groups = lax.axis_size("dom")
    cell_total = storage.shape[0] * CB * groups * lax.axis_size("tile")
    scratch = lambda rows: pltpu.VMEM((rows, LANE), F32)
    p, sh, sl, u, *edges = call(
        first_kernel,
        (FIELD, ((FX * LANE, LANE), BF16), ((FX * LANE, LANE), BF16), FIELD) + EDGES,
        pltpu.with_memory_space_constraint(pumping, pltpu.HBM),
        pltpu.with_memory_space_constraint(coupling, pltpu.HBM),
        scratch=(
            pltpu.VMEM((16, RHS * CB), F32),
            pltpu.VMEM((16, CB * CB), F32),
            scratch(ROWS),
            scratch(ROWS),
            scratch(FX * LANE),
            pltpu.SemaphoreType.DMA((2, PIECES)),
        ),
        place=pltpu.HBM,
    )
    halo = exchange(*edges)
    ap, u, *edges = call(second_kernel, (FIELD, FIELD) + EDGES, p, u, sh, sl, storage, *halo)
    halo = exchange(*edges)
    (base,) = call(base_kernel, (((2 * RHS, LANE), F32),), p, ap)
    (packed,) = call(
        third_kernel, (((2 * RHS, LANE), F32),), ap, u, sh, sl, storage, *halo, base
    )
    cells, kriging = call(
        deal_kernel,
        (((FX * LANE, 4 * RHS), BF16), ((2 * PILOT, FX * LANE // 2), BF16)),
        *(tile_order, p, ap, kriging),
        scratch=(pltpu.VMEM((4 * RHS, FX * LANE), BF16),),
        flops=LONG,
    )
    packed = reduce_all(packed)
    heads, scale, weights, later = call(
        lambda *refs: solve_kernel(cell_total, *refs),
        (((FX * LANE // 2, LANE), F32), ((1, RHS), F32), ((2 * RHS, RHS), F32), ((RHS, LANE), F32)),
        *(packed, cells),
        scratch=(scratch(FX * LANE),),
    )
    heads = heads.astype(jnp.float16).reshape(groups, -1, LANE)
    heads = lax.all_to_all(heads, "dom", 0, 0, tiled=True).reshape(-1, LANE).astype(F32)
    sens, gram = call(
        lambda *refs: product_kernel(cell_total, *refs),
        (((PILOT, RHS), F32), ((RHS, RHS), F32)),
        *(kriging, heads, scale, packed, weights, later),
    )
    return sens, gram


def solution(mesh):
    spec = P(("dom", "tile"), None)
    return jax.shard_map(
        shards, mesh=mesh, in_specs=(spec,) * 5, out_specs=(spec, P()), check_vma=False
    )
```

```python
import jax
import jax.numpy as jnp
from jax import lax
from jax.experimental import pallas as pl
from jax.experimental.pallas import tpu as pltpu
from jax.sharding import PartitionSpec as P

RHS = 64
CB = 64
FX = 8
PILOT = 16
LANE = 128
ROWS = FX * RHS
F32 = jnp.float32
BF16 = jnp.bfloat16
HIGHEST = lax.Precision.HIGHEST
PARAMS = pltpu.CompilerParams(vmem_limit_bytes=40 * 1024 * 1024)
PIECES = 4
WIDTH = RHS * CB // PIECES
LONG = 10**11
NN = (((1,), (0,)), ((), ()))
NT = (((1,), (1,)), ((), ()))


def split(value):
    high = value.astype(BF16)
    return high, (value - high.astype(F32)).astype(BF16)


def dot(left, right, dims):
    return lax.dot_general(left, right, dims, preferred_element_type=F32)


def dot3(left, right, dims):
    (lh, ll), (rh, rl) = left, right
    return dot(lh, rh, dims) + (dot(ll, rh, dims) + dot(lh, rl, dims))


def exact(left, right, dims=NN):
    return lax.dot_general(left, right, dims, precision=HIGHEST, preferred_element_type=F32)


def low_lanes(rows):
    return lax.broadcasted_iota(jnp.int32, (rows, LANE), 1) < CB


def swap(value):
    return pltpu.roll(value, CB, 1)


def part(x):
    return pl.ds(x * RHS, RHS)


def is_even(axis):
    return lax.rem(lax.axis_index(axis), 2) == 0


def by_parity(axis, first, second):
    even = is_even(axis)
    return jnp.where(even, first, second), jnp.where(even, second, first)


def write_edges(spread, d1, d2, t1, t2):
    low = low_lanes(RHS)
    one, two = by_parity("dom", spread[FX - 1], spread[0])
    d1[...] = one.astype(BF16)
    d2[:RHS, :] = two.astype(BF16)
    d2[RHS:, :] = jnp.zeros((d2.shape[0] - RHS, LANE), BF16)
    for i in range(FX // 2):
        even, odd = spread[2 * i], spread[2 * i + 1]
        left = jnp.where(low, even, swap(odd))
        right = jnp.where(low, swap(even), odd)
        one, two = by_parity("tile", right, left)
        t1[part(i), :] = one.astype(BF16)
        t2[part(i), :] = two.astype(BF16)


def first_kernel(pump_hbm, coup_hbm, p_out, sh_out, sl_out, u_out, d1, d2, t1, t2, pump, coup, rows_p, rows_s, mats, arrived):
    copies = []
    for source, target, order in ((pump_hbm, pump, 0), (coup_hbm, coup, 1)):
        for i in range(PIECES):
            columns = pl.ds(i * WIDTH, WIDTH)
            copies.append(
                pltpu.make_async_copy(source.at[:, columns], target.at[:, columns], arrived.at[order, i])
            )
            copies[-1].start()
    for i, copy in enumerate(copies):
        source, target = (pump, rows_p) if i < PIECES else (coup, rows_s)
        copy.wait()
        chunks = WIDTH // LANE
        for k in range(i % PIECES * chunks, (i % PIECES + 1) * chunks):
            target[pl.ds(k, 16, stride=32), :] = source[:, k * LANE : (k + 1) * LANE]
    low = low_lanes(32)
    zero = jnp.zeros((32, LANE), F32)
    for x in range(FX):
        a0, a1 = rows_p[pl.ds(x * 64, 32), :], rows_p[pl.ds(x * 64 + 32, 32), :]
        p_out[pl.ds(x * 64, 32, stride=2), :] = jnp.where(low, a0, swap(a1))
        p_out[pl.ds(x * 64 + 1, 32, stride=2), :] = jnp.where(low, swap(a0), a1)
        s0, s1 = rows_s[pl.ds(x * 64, 32), :], rows_s[pl.ds(x * 64 + 32, 32), :]
        mats[pl.ds(x * 128, 32, stride=2), :] = jnp.where(low, s0, zero)
        mats[pl.ds(x * 128 + 1, 32, stride=2), :] = jnp.where(low, swap(s0), zero)
        mats[pl.ds(x * 128 + 64, 32, stride=2), :] = jnp.where(low, zero, swap(s1))
        mats[pl.ds(x * 128 + 65, 32, stride=2), :] = jnp.where(low, zero, s1)
    spread = []
    for x in range(FX):
        block = pl.ds(x * LANE, LANE)
        high, rest = split(mats[block, :])
        sh_out[block, :] = high
        sl_out[block, :] = rest
        u = dot3(split(p_out[part(x), :]), (high, rest), NN)
        u_out[part(x), :] = u
        spread.append(u)
    write_edges(spread, d1, d2, t1, t2)


def operator(v, u, sh, sl, stor, d1, d2, t1, t2):
    low = low_lanes(RHS)
    spread = [u[part(x), :] for x in range(FX)]
    after, before = by_parity("dom", d1[...].astype(F32), d2[:RHS, :].astype(F32))
    ends = [before] + spread + [after]
    right, left = [], []
    for i in range(FX // 2):
        one, two = by_parity("tile", t1[part(i), :].astype(F32), t2[part(i), :].astype(F32))
        right.append(one)
        left.append(two)
    applied = []
    for x in range(FX):
        from_left, from_right = left[x // 2], right[x // 2]
        if x % 2 == 0:
            outside = jnp.where(low, from_left, swap(from_right))
        else:
            outside = jnp.where(low, swap(from_left), from_right)
        pulled = 4.0 * spread[x] - (ends[x] + ends[x + 2] + swap(spread[x]) + outside)
        block = pl.ds(x * LANE, LANE)
        capacity = jnp.concatenate([stor[2 * x : 2 * x + 1, :], stor[2 * x + 1 : 2 * x + 2, :]], axis=1)
        applied.append(
            capacity * v[part(x), :] + dot3(split(pulled), (sh[block, :], sl[block, :]), NT)
        )
    return applied


def second_kernel(v, u, sh, sl, stor, d1, d2, t1, t2, ap_out, u_out, *edges):
    applied = operator(v, u, sh, sl, stor, d1, d2, t1, t2)
    spread = []
    for x in range(FX):
        ap_out[part(x), :] = applied[x]
        block = pl.ds(x * LANE, LANE)
        s = dot3(split(applied[x]), (sh[block, :], sl[block, :]), NN)
        u_out[part(x), :] = s
        spread.append(s)
    write_edges(spread, *edges)


def deal_kernel(order, v, ap, kriging, cells, kept, table):
    count = kriging.shape[1]
    source = lax.broadcasted_iota(jnp.int32, (count, count // 2), 0)
    target = lax.broadcasted_iota(jnp.int32, (count, count // 2), 1)
    for parity in range(2):
        pick = jnp.where(source == 2 * target + parity, 1.0, 0.0).astype(BF16)
        kept[pl.ds(parity * PILOT, PILOT), :] = dot(kriging[...], pick, NN).astype(BF16)
    for x in range(FX):
        high, rest = split(jnp.concatenate([v[part(x), :], ap[part(x), :]], axis=0))
        table[: 2 * RHS, x * LANE : (x + 1) * LANE] = high
        table[2 * RHS :, x * LANE : (x + 1) * LANE] = rest
    lane = lax.broadcasted_iota(jnp.int32, (LANE, LANE), 1)
    for g in range(FX):
        row = jnp.broadcast_to(order[:, g * LANE : (g + 1) * LANE], (LANE, LANE))
        wanted = jnp.transpose(row)
        picks = [
            jnp.where(wanted == lane + l * LANE, 1.0, 0.0).astype(BF16) for l in range(FX)
        ]
        cells[pl.ds(g * LANE, LANE), :] = dot(
            jnp.concatenate(picks, axis=1), table[...], NT
        ).astype(BF16)


def base_kernel(p, v, base):
    total = jnp.zeros((2 * RHS, 2 * RHS), F32)
    for x in range(FX):
        both = split(jnp.concatenate([p[part(x), :], v[part(x), :]], axis=0))
        total += dot3(both, both, NT)
    base[...] = total


def third_kernel(v, u, sh, sl, stor, d1, d2, t1, t2, base, packed):
    applied = operator(v, u, sh, sl, stor, d1, d2, t1, t2)
    total = jnp.zeros((2 * RHS, RHS), F32)
    for x in range(FX):
        image = split(applied[x])
        both = [jnp.concatenate([a, b], axis=0) for a, b in zip(split(v[part(x), :]), image)]
        total += dot3(both, image, NT)
    m0, m1, m2 = base[:RHS, :RHS], base[:RHS, RHS:], base[RHS:, RHS:]
    m1 = symmetric(m1)
    m3 = symmetric(total[:RHS])
    m4 = total[RHS:]
    row, column = square_index()
    upper = row <= column
    packed[:RHS, :] = jnp.concatenate([jnp.where(upper, m0, m2), jnp.where(upper, m1, m3)], axis=1)
    ends = jnp.where(row == 0, diagonal(m2), jnp.where(row == 1, diagonal(m3), 0.0))
    packed[RHS:, :] = jnp.concatenate([m4, ends], axis=1)


def square_index():
    return [lax.broadcasted_iota(jnp.int32, (RHS, RHS), d) for d in (0, 1)]


def diagonal(matrix):
    row, column = square_index()
    return jnp.sum(jnp.where(row == column, matrix, 0.0), axis=0, keepdims=True)


def column_diagonal(matrix):
    row, column = square_index()
    return jnp.sum(jnp.where(row == column, matrix, 0.0), axis=1, keepdims=True)


def unpack_pair(matrix, ends):
    row, column = square_index()
    turned = jnp.transpose(matrix)
    first = jnp.where(row <= column, matrix, turned)
    second = jnp.where(row > column, matrix, jnp.where(row < column, turned, ends))
    return first, second


def eliminate(joined, panel=8):
    order, width = joined.shape
    parts = [joined[g : g + panel, :] for g in range(0, order, panel)]
    index = lax.broadcasted_iota(jnp.int32, (panel, width), 0)

    def wide(value):
        pieces = [value] * (width // LANE)
        if width % LANE:
            pieces.append(value[:, : width % LANE])
        return jnp.concatenate(pieces, axis=1) if len(pieces) > 1 else value

    def apply(rows, at, c0, c1, inverse, where):
        r0, r1 = rows[at : at + 1, :], rows[at + 1 : at + 2, :]
        s0 = inverse[0] * r0 + inverse[1] * r1
        s1 = inverse[2] * r0 + inverse[3] * r1
        rest = rows - (c0 * s0 + c1 * s1)
        return jnp.where(where == at, s0, jnp.where(where == at + 1, s1, rest))

    for g in range(len(parts)):
        rows = parts[g]
        first = g * panel
        columns = [
            jnp.broadcast_to(rows[:, first + q : first + q + 1], (panel, LANE)) for q in range(panel)
        ]
        for at in range(0, panel, 2):
            c0, c1 = columns[at], columns[at + 1]
            a, c = c0[at : at + 1, :], c0[at + 1 : at + 2, :]
            b, d = c1[at : at + 1, :], c1[at + 1 : at + 2, :]
            scale = 1.0 / (a * d - b * c)
            inverse = (d * scale, -b * scale, -c * scale, a * scale)
            for q in range(at + 2, panel):
                columns[q] = apply(columns[q], at, c0, c1, inverse, index[:, :LANE])
            rows = apply(rows, at, wide(c0), wide(c1), [wide(v) for v in inverse], index)
        parts[g] = rows
        for h in range(len(parts)):
            if h != g:
                taken = None
                for q in range(panel):
                    column = jnp.broadcast_to(parts[h][:, first + q : first + q + 1], (panel, width))
                    term = column * rows[q : q + 1, :]
                    taken = term if taken is None else taken + term
                parts[h] = parts[h] - taken
    return jnp.concatenate(parts, axis=0)[:, order:]


def symmetric(matrix):
    return 0.5 * (matrix + jnp.transpose(matrix))


def solve_kernel(cell_total, packed, cells, heads, scale, weights, later, rows):
    m0, m2 = unpack_pair(packed[:RHS, :RHS], packed[RHS : RHS + 1, RHS:])
    m1, m3 = unpack_pair(packed[:RHS, RHS:], packed[RHS + 1 : RHS + 2, RHS:])
    first = eliminate(jnp.concatenate([m1, m0, m2], axis=1))
    alpha, shift = first[:, :RHS], first[:, RHS:]
    bent = exact(m2, first)
    curved = symmetric(m3 - bent[:, RHS:])
    target = m1 - bent[:, :RHS]
    gamma = eliminate(jnp.concatenate([curved, target], axis=1))
    mixed = alpha - exact(shift, gamma)
    both = jnp.concatenate([mixed, gamma], axis=0)
    spread = jnp.concatenate([column_diagonal(m0), column_diagonal(m2)], axis=0)
    bound = jnp.sum(jnp.abs(both) * jnp.sqrt(spread * (1.0 / cell_total)), axis=0, keepdims=True)
    bound = jnp.where(bound > 0.0, bound, 1.0)
    scale[...] = bound
    high, rest = split(jnp.concatenate([both / bound, both / bound], axis=1))
    value = dot3((cells[:, :LANE], cells[:, LANE:]), (high, rest), NN)
    rows[...] = value
    half = FX * LANE // 2
    even, odd = rows[pl.ds(0, half, stride=2), :], rows[pl.ds(1, half, stride=2), :]
    heads[...] = jnp.where(low_lanes(half), even, odd)
    weights[...] = both
    later[...] = jnp.concatenate([m2, m3], axis=1)


def product_kernel(cell_total, kriging, arrived, scale, packed, weights, later, sens, gram):
    high, rest = split(arrived[...])
    product = dot(kriging[...], high, NN) + dot(kriging[...], rest, NN)
    sens[...] = (product[:PILOT, :RHS] + product[PILOT:, RHS:]) * scale[...]
    mixed, gamma = weights[:RHS, :], weights[RHS:, :]
    rest = exact(packed[RHS:, :RHS], gamma) + exact(later[:, RHS:], mixed) - later[:, :RHS]
    gram[...] = symmetric(exact(jnp.transpose(gamma), rest)) * (1.0 / cell_total)


def call(kernel, shapes, *operands, scratch=(), flops=1000000, place=pltpu.VMEM):
    return pl.pallas_call(
        kernel,
        out_shape=[jax.ShapeDtypeStruct(shape, kind) for shape, kind in shapes],
        in_specs=[pl.BlockSpec(memory_space=place)] * len(operands),
        out_specs=[pl.BlockSpec(memory_space=pltpu.VMEM)] * len(shapes),
        scratch_shapes=list(scratch),
        compiler_params=PARAMS,
        cost_estimate=pl.CostEstimate(flops=flops, bytes_accessed=1 << 20, transcendentals=0),
    )(*operands)


EDGES = (((RHS, LANE), BF16), ((ROWS // 2 + 16, LANE), BF16), ((ROWS // 2, LANE), BF16), ((ROWS // 2, LANE), BF16))
FIELD = ((ROWS, LANE), F32)


def exchange(d1, d2, t1, t2):
    def along(axis, one, two):
        devices = lax.axis_size(axis)
        first = [(i, i ^ 1) for i in range(devices)]
        second = [(i, ((i + 1) ^ 1) - 1) for i in range(1, devices - 1)]
        two = lax.ppermute(two, axis, second)
        return lax.ppermute(one, axis, first), two

    t1, t2 = along("tile", t1, t2)
    d1, d2 = along("dom", d1, d2)
    return d1, d2, t1, t2


def member_groups(sizes, together):
    strides, total = [], 1
    for size in reversed(sizes):
        strides.insert(0, total)
        total *= size

    def numbers(axes):
        values = [0]
        for axis in axes:
            values = [v + i * strides[axis] for v in values for i in range(sizes[axis])]
        return values

    apart = [axis for axis in range(len(sizes)) if axis not in together]
    return [[base + v for v in numbers(together)] for base in numbers(apart)]


def reduce_all(packed):
    axes = ("dom", "tile")
    sizes = (4, 16, 2, 4)
    near = member_groups(sizes, (0, 2, 3))
    far = member_groups(sizes, (1,))

    def trade(array, groups):
        return lax.all_to_all(array, axes, 0, 0, axis_index_groups=groups, tiled=True)

    n, m = len(near[0]), len(far[0])
    mine = jnp.sum(trade(packed.reshape(n, -1, LANE), near), axis=0)
    mine = jnp.sum(trade(jnp.broadcast_to(mine[None], (m,) + mine.shape), far), axis=0)
    return trade(jnp.broadcast_to(mine[None], (n,) + mine.shape), near).reshape(packed.shape)


def shards(pumping, coupling, storage, tile_order, kriging):
    groups = lax.axis_size("dom")
    cell_total = storage.shape[0] * CB * groups * lax.axis_size("tile")
    scratch = lambda rows: pltpu.VMEM((rows, LANE), F32)
    p, sh, sl, u, *edges = call(
        first_kernel,
        (FIELD, ((FX * LANE, LANE), BF16), ((FX * LANE, LANE), BF16), FIELD) + EDGES,
        pltpu.with_memory_space_constraint(pumping, pltpu.HBM),
        pltpu.with_memory_space_constraint(coupling, pltpu.HBM),
        scratch=(
            pltpu.VMEM((16, RHS * CB), F32),
            pltpu.VMEM((16, CB * CB), F32),
            scratch(ROWS),
            scratch(ROWS),
            scratch(FX * LANE),
            pltpu.SemaphoreType.DMA((2, PIECES)),
        ),
        place=pltpu.HBM,
    )
    halo = exchange(*edges)
    ap, u, *edges = call(second_kernel, (FIELD, FIELD) + EDGES, p, u, sh, sl, storage, *halo)
    halo = exchange(*edges)
    (base,) = call(base_kernel, (((2 * RHS, LANE), F32),), p, ap)
    (packed,) = call(
        third_kernel, (((2 * RHS, LANE), F32),), ap, u, sh, sl, storage, *halo, base
    )
    cells, kriging = call(
        deal_kernel,
        (((FX * LANE, 4 * RHS), BF16), ((2 * PILOT, FX * LANE // 2), BF16)),
        *(tile_order, p, ap, kriging),
        scratch=(pltpu.VMEM((4 * RHS, FX * LANE), BF16),),
    )
    packed = reduce_all(packed)
    heads, scale, weights, later = call(
        lambda *refs: solve_kernel(cell_total, *refs),
        (((FX * LANE // 2, LANE), F32), ((1, RHS), F32), ((2 * RHS, RHS), F32), ((RHS, LANE), F32)),
        *(packed, cells),
        scratch=(scratch(FX * LANE),),
    )
    heads = heads.astype(jnp.float16).reshape(groups, -1, LANE)
    heads = lax.all_to_all(heads, "dom", 0, 0, tiled=True).reshape(-1, LANE).astype(F32)
    sens, gram = call(
        lambda *refs: product_kernel(cell_total, *refs),
        (((PILOT, RHS), F32), ((RHS, RHS), F32)),
        *(kriging, heads, scale, packed, weights, later),
    )
    return sens, gram


def solution(mesh):
    spec = P(("dom", "tile"), None)
    return jax.shard_map(
        shards, mesh=mesh, in_specs=(spec,) * 5, out_specs=(spec, P()), check_vma=False
    )
```
